128 devices in a mesh: section: 8 (over y_hi, z), dp: 16 (over y_lo, x, core).
Axes of the slice: x: 4, y: 4 (y_hi: 2, y_lo: 2; y = y_hi * 2 + y_lo), z: 4, core: 2. Of those that a mesh axis runs over, the one named last changes fastest.
Arguments:
- hidden_in: bfloat16 [12288, 1536], P('dp'), may hold values from -6 to 6
- segment_ids: int32 [48, 256], P('dp'), may hold values from 0 to 7, never falling along the last dimension, each value on 1 to 128 neighbouring positions
- cotangent: bfloat16 [12288, 1536], P('dp'), may hold values from -6 to 6
- in_proj: bfloat16 [8, 1536, 2304], P('section', 'dp'), may hold values from -1 to 1
- out_proj: bfloat16 [8, 768, 1536], P('section', 'dp'), may hold values from -0.21875 to 0.21875
- norm_gains: float32 [8, 1536], P('section'), may hold values from 0.5 to 1.5
Outputs:
- in_proj_grad: float32 [8, 1536, 2304], P('section', 'dp')
- out_proj_grad: float32 [8, 768, 1536], P('section', 'dp')
- gain_grad: float32 [8, 1536], P('section', 'dp')
- grad_rms: float32 [], replicated
The draws below stay inside these ranges and needn't reach their ends.
Inputs may be any that keep to these rules, and one draw needn't show every extreme that they name: `segment_ids`: ids never fall along a row; at most 128 positions of a row share one id.
All inputs are finite; a program needn't handle non-finite values.
Results may differ from the reference program's by a relative error of at most 0.035.
Values may be sent and summed in bfloat16 or wider, within the bound.
No kernel may reach another device: no remote copies, remote signals or barrier semaphores. Data moves between devices by JAX's collectives and lax.ppermute only.
A program may use at most 128 MiB of HBM per device.

```python
import math
import jax
import jax.numpy as jnp
import numpy as np
from jax import lax

D = 1536
HEADS = 6
HEAD_SIZE = 128
SEQ = 256
LAYERS = 8
INNER = 768
SEQS = 48
TOKENS = 12288
N_DP = 16


def draw_in_proj(key, part):
    key = jax.random.fold_in(key, 7)
    base = jax.random.normal(key, (LAYERS, D, 3 * HEADS * HEAD_SIZE), jnp.float32) * D ** (-0.5)
    base = jnp.clip(base, -1.0, 1.0)
    return base.astype(jnp.bfloat16)


def level_of(own_key, extent, shards, low, high):
    def one(axis_at, shards_of):
        steps = jax.random.uniform(jax.random.fold_in(jax.random.fold_in(own_key, 6), axis_at), (shards_of,), jnp.float32, low / len(shards), high / len(shards))
        return jnp.repeat(jnp.exp(steps), extent[axis_at] // shards_of).reshape((-1,) + (1,) * (len(extent) - axis_at - 1))

    level = one(*shards[0])
    for cut in shards[1:]:
        level = level * one(*cut)
    return level


def profile(count, total, bound, slope):
    loads = [(1 << 20) // math.isqrt(standing ** slope) + 1 for standing in range(2, count + 1)]
    spare, holding = total - bound - (count - 1), [1] * (count - 1)
    while spare > 0:
        candidates = [i for i in range(count - 1) if holding[i] < bound]
        mass, remaining = sum([loads[i] for i in candidates]), spare
        for i in candidates:
            extra = min(bound - holding[i], max(1, remaining * loads[i] // mass), spare)
            holding[i] = holding[i] + extra
            spare = spare - extra
    return np.array([bound] + holding)


def ragged_sizes(rng, number_of, total, bound, slope):
    if number_of == 2:
        one = jax.random.randint(rng, (), max(1, total - bound), min(bound, total - 1) + 1)
        return jnp.stack([one, total - one])
    tallies = jnp.asarray(profile(number_of, total, bound, slope), jnp.int32)
    twos = (number_of - 1) // 2
    giver, receiver = tallies[1:1 + 2 * twos:2], tallies[2:2 + 2 * twos:2]
    room = jnp.minimum(giver - 1, bound - receiver)
    moved = jax.random.randint(jax.random.fold_in(rng, 1), (twos,), 0, 1 << 20) % (room + 1)
    tallies = tallies.at[1:1 + 2 * twos:2].set(giver - moved).at[2:2 + 2 * twos:2].set(receiver + moved)
    return tallies[jax.random.permutation(jax.random.fold_in(rng, 2), number_of)]


def normal_values(stream_key, extent, scale, most, shards=(), kind=jnp.bfloat16):
    gain = level_of(stream_key, extent, shards, -0.22, 0.18) if shards else 1.0
    result = jax.random.normal(stream_key, extent, jnp.float32) * scale * gain
    return jnp.minimum(jnp.maximum(result, -most), most).astype(kind)


def setup_inputs(seed: int = 0) -> dict:
    arg_keys = jax.random.split(jax.random.key(seed), 7)
    hidden_in = normal_values(arg_keys[0], (TOKENS, D), 1.0, 6.0, ((0, 16),))
    segment_ids = jax.vmap(lambda own: jnp.searchsorted(jnp.cumsum(ragged_sizes(own, max(4, SEQ // 32), SEQ, SEQ // 2, 2)), jnp.arange(SEQ), side="right"))(jax.random.split(arg_keys[1], SEQS)).reshape((SEQS, SEQ)).astype(jnp.int32)
    cotangent = normal_values(arg_keys[2], (TOKENS, D), 1.0, 6.0, ((0, 16),))
    in_proj = draw_in_proj(jax.random.fold_in(arg_keys[6], 71), 0)
    out_proj = normal_values(arg_keys[4], (LAYERS, INNER, D), INNER ** -0.5, 0.21875, ((0, 8), (1, 16)))
    norm_gains = jnp.clip(1.0 + 0.1 * jax.random.normal(arg_keys[5], (LAYERS, D), jnp.float32), 0.5, 1.5)
    return dict(hidden_in=hidden_in, segment_ids=segment_ids, cotangent=cotangent, in_proj=in_proj, out_proj=out_proj, norm_gains=norm_gains)


epsilon = 1e-05
masked_score = -1e+30

def product(form, left, right):
    return jnp.einsum(form, left.astype(jnp.float32), right.astype(jnp.float32))

def attend_parts(hidden, segments, in_weight, gains_row):
    batch_count, seq_length, feature_count = hidden.shape
    inner_width = in_weight.shape[1] // 3
    head_count = inner_width // HEAD_SIZE
    residual = hidden.astype(jnp.float32)
    inverse_rms = lax.rsqrt(lax.optimization_barrier(jnp.mean(residual * residual, axis=-1, keepdims=True)) + epsilon)
    unit_rows = residual * inverse_rms
    normed = (unit_rows * gains_row).astype(jnp.bfloat16)
    joined = jnp.dot(normed.reshape(-1, feature_count), in_weight, preferred_element_type=jnp.float32)
    joined = joined.astype(jnp.bfloat16).reshape(batch_count, seq_length, 3, head_count, HEAD_SIZE)
    query_rows = joined[:, :, 0]
    key_rows = joined[:, :, 1]
    value_rows = joined[:, :, 2]
    row_ids = lax.broadcasted_iota(jnp.int32, (seq_length, seq_length), 0)
    col_ids = lax.broadcasted_iota(jnp.int32, (seq_length, seq_length), 1)
    allowed = (col_ids <= row_ids)[None] & (segments[:, :, None] == segments[:, None, :])
    scores = product('bqhe,bkhe->bhqk', query_rows, key_rows) * HEAD_SIZE ** (-0.5)
    scores = jnp.where(allowed[:, None], scores, masked_score)
    row_max = lax.optimization_barrier(jnp.max(scores, axis=-1, keepdims=True))
    exponentials = jnp.exp(scores - row_max)
    probabilities = exponentials / lax.optimization_barrier(jnp.sum(exponentials, axis=-1, keepdims=True))
    weights_low = probabilities.astype(jnp.bfloat16)
    attended = product('bhqk,bkhe->bqhe', weights_low, value_rows).astype(jnp.bfloat16)
    attended = attended.reshape(batch_count, seq_length, inner_width)
    return (residual, inverse_rms, unit_rows, normed, query_rows, key_rows, value_rows, probabilities, weights_low, attended)

def layer_forward(hidden, segments, in_weight, out_weight, gains_row):
    parts = attend_parts(hidden, segments, in_weight, gains_row)
    residual = parts[0]
    attended = parts[9]
    update = jnp.dot(attended.reshape(-1, attended.shape[-1]), out_weight, preferred_element_type=jnp.float32)
    return (residual + update.reshape(residual.shape)).astype(jnp.bfloat16)

def layer_backward(hidden, segments, grad_next, in_weight, out_weight, gains_row, groups):
    residual, inverse_rms, unit_rows, normed, query_rows, key_rows, value_rows, probabilities, weights_low, attended = attend_parts(hidden, segments, in_weight, gains_row)
    batch_count, seq_length, feature_count = hidden.shape
    inner_width = attended.shape[-1]
    head_count = inner_width // HEAD_SIZE
    grad_flat = grad_next.reshape(groups, -1, feature_count)
    out_grad = product('gtc,gtd->gcd', attended.reshape(groups, -1, inner_width), grad_flat)
    grad_attended = product('td,cd->tc', grad_next.reshape(-1, feature_count), out_weight)
    grad_attended = grad_attended.astype(jnp.bfloat16).reshape(batch_count, seq_length, head_count, HEAD_SIZE)
    grad_probs = product('bqhe,bkhe->bhqk', grad_attended, value_rows)
    grad_values = product('bhqk,bqhe->bkhe', weights_low, grad_attended)
    inner_sum = lax.optimization_barrier(jnp.sum(grad_probs * probabilities, axis=-1, keepdims=True))
    grad_scores = (probabilities * (grad_probs - inner_sum) * HEAD_SIZE ** (-0.5)).astype(jnp.bfloat16)
    grad_queries = product('bhqk,bkhe->bqhe', grad_scores, key_rows)
    grad_keys = product('bhqk,bqhe->bkhe', grad_scores, query_rows)
    grad_joined = jnp.stack([grad_queries, grad_keys, grad_values], axis=2).astype(jnp.bfloat16)
    grad_joined = grad_joined.reshape(-1, 3 * inner_width)
    in_grad = product('gtd,gtc->gdc', normed.reshape(groups, -1, feature_count), grad_joined.reshape(groups, -1, 3 * inner_width))
    grad_normed = product('tc,dc->td', grad_joined, in_weight).reshape(residual.shape)
    gain_grad = lax.optimization_barrier(jnp.sum((grad_normed * unit_rows).reshape(groups, -1, feature_count), axis=1))
    scaled = grad_normed * gains_row
    inner_mean = lax.optimization_barrier(jnp.mean(scaled * unit_rows, axis=-1, keepdims=True))
    grad_in = (grad_next.astype(jnp.float32) + inverse_rms * (scaled - unit_rows * inner_mean)).astype(jnp.bfloat16)
    return (grad_in, in_grad, out_grad, gain_grad)

def group_sum(partials):
    rounded = lax.optimization_barrier(partials.astype(jnp.bfloat16))
    return lax.optimization_barrier(jnp.sum(rounded.astype(jnp.float32), axis=0))

def reference(hidden_in, segment_ids, cotangent, in_proj, out_proj, norm_gains):
    current = hidden_in.reshape(SEQS, SEQ, D)
    stored = []
    for layer_index in range(LAYERS):
        stored.append(current)
        if layer_index + 1 < LAYERS:
            current = layer_forward(current, segment_ids, in_proj[layer_index], out_proj[layer_index], norm_gains[layer_index])
    grad_next = (cotangent.astype(jnp.float32) * (1.0 / math.sqrt(TOKENS))).astype(jnp.bfloat16)
    grad_next = grad_next.reshape(SEQS, SEQ, D)
    in_list = [None] * LAYERS
    out_list = [None] * LAYERS
    gain_list = [None] * LAYERS
    for layer_index in reversed(range(LAYERS)):
        grad_next, in_part, out_part, gain_part = layer_backward(stored[layer_index], segment_ids, grad_next, in_proj[layer_index], out_proj[layer_index], norm_gains[layer_index], N_DP)
        in_list[layer_index] = group_sum(in_part)
        out_list[layer_index] = group_sum(out_part)
        gain_list[layer_index] = group_sum(gain_part)
    in_proj_grad = jnp.stack(in_list)
    out_proj_grad = jnp.stack(out_list)
    gain_grad = jnp.stack(gain_list)
    grand_total = jnp.sum(in_proj_grad * in_proj_grad) + jnp.sum(out_proj_grad * out_proj_grad)
    grand_total = grand_total + jnp.sum(gain_grad * gain_grad)
    entry_count = float(in_proj_grad.size + out_proj_grad.size + gain_grad.size)
    grad_rms = jnp.sqrt(grand_total / entry_count)
    return (in_proj_grad, out_proj_grad, gain_grad, grad_rms)
```

```python
import functools
import math

import jax
import jax.numpy as jnp
from jax import lax
from jax.experimental import pallas as pl
from jax.experimental.pallas import tpu as pltpu
from jax.sharding import PartitionSpec as P

HEAD = 128
ROWS = 128
EPS = 1e-05
MASKED = -1e30
BF = jnp.bfloat16
F32 = jnp.float32


def mm(left, right, lc=1, rc=0):
    return lax.dot_general(left, right, (((lc,), (rc,)), ((), ())), preferred_element_type=F32)


def unit(h):
    r = lax.rsqrt(jnp.mean(h * h, axis=-1, keepdims=True) + EPS)
    return r, h * r


def weight_copies(pack, wi_s, wl_s, wr_s, sems, inner):
    half = wl_s.shape[1]
    third = 3 * inner
    wi = [
        pltpu.make_async_copy(
            pack.at[:, :, pl.ds(k * inner, inner)], wi_s.at[:, :, pl.ds(k * inner, inner)], sems.at[k]
        )
        for k in range(3)
    ]
    wo = [
        pltpu.make_async_copy(pack.at[:, pl.ds(0, half), pl.ds(third, inner)], wl_s, sems.at[3]),
        pltpu.make_async_copy(pack.at[:, pl.ds(half, half), pl.ds(third, inner)], wr_s, sems.at[4]),
    ]
    return wi, wo


def forward_kernel(cycle, micro, last, sec, recv, hid, bias, gains, pack, *refs):
    (sh, sa, sq, so, sl) = refs[5:10]
    out = refs[10]
    (h_s, wi_s, wl_s, wr_s, a_s, q_s, o_s, kv_s, b_s, l_s, n_s, sems) = refs[11:]
    inner = o_s.shape[1]
    feat = h_s.shape[1]
    heads = inner // HEAD
    odd = cycle % 2 == 1
    keys = 2 * ROWS if odd else ROWS
    section = sec[0]
    m = cycle - 2 * section

    @pl.when((m >= 0) & (m < micro))
    def _():
        from_in = pltpu.make_async_copy(hid.at[pl.ds(m * ROWS, ROWS)], h_s, sems.at[5])
        from_left = pltpu.make_async_copy(recv, h_s, sems.at[5])

        @pl.when(section == 0)
        def _():
            from_in.start()

        @pl.when(section != 0)
        def _():
            from_left.start()

        wi, wo = weight_copies(pack, wi_s, wl_s, wr_s, sems, inner)
        for copy in wi:
            copy.start()
        load_b = pltpu.make_async_copy(bias.at[pl.ds(m * ROWS, ROWS)], b_s, sems.at[6])
        load_b.start()
        if odd:
            load_kv = pltpu.make_async_copy(
                sq.at[m - 1, :, pl.ds(inner, 2 * inner)], kv_s, sems.at[7]
            )
            load_kv.start()
        for copy in wo:
            copy.start()
        from_left.wait()
        save_h = pltpu.make_async_copy(h_s, sh.at[m], sems.at[8])
        save_h.start()
        h = h_s[...].astype(F32)
        _, u = unit(h)
        a_s[...] = (u * gains[...]).astype(BF)
        save_a = pltpu.make_async_copy(a_s, sa.at[m], sems.at[9])
        save_a.start()
        a = a_s[...]
        for k in range(3):
            wi[k].wait()
            w = wi_s[:, :, k * inner:(k + 1) * inner].reshape(feat, inner)
            q_s[:, k * inner:(k + 1) * inner] = mm(a, w).astype(BF)
        save_q = pltpu.make_async_copy(q_s, sq.at[m], sems.at[10])
        save_q.start()
        load_b.wait()
        if odd:
            load_kv.wait()
        lane = lax.broadcasted_iota(jnp.int32, (ROWS, HEAD), 1)
        lse = jnp.zeros((ROWS, HEAD), F32)
        mask = b_s[:, :keys]
        for e in range(heads):
            lo, hi = e * HEAD, (e + 1) * HEAD
            q = q_s[:, lo:hi]
            k = q_s[:, inner + lo:inner + hi]
            v = q_s[:, 2 * inner + lo:2 * inner + hi]
            if odd:
                k = jnp.concatenate([kv_s[:, lo:hi], k], axis=0)
                v = jnp.concatenate([kv_s[:, inner + lo:inner + hi], v], axis=0)
            s = mm(q, k, 1, 1) * HEAD ** (-0.5) + mask
            top = jnp.max(s, axis=-1, keepdims=True)
            x = jnp.exp(s - top)
            total = jnp.sum(x, axis=-1, keepdims=True)
            p = x / total
            o_s[:, lo:hi] = mm(p.astype(BF), v).astype(BF)
            lse = jnp.where(lane == e, top + jnp.log(total), lse)
        l_s[...] = lse
        save_o = pltpu.make_async_copy(o_s, so.at[m], sems.at[11])
        save_o.start()
        save_l = pltpu.make_async_copy(l_s, sl.at[m], sems.at[12])
        save_l.start()
        for copy in wo:
            copy.wait()

        @pl.when(section != last)
        def _():
            o = o_s[...]
            for part, w in ((0, wl_s), (1, wr_s)):
                cols = slice(part * inner, (part + 1) * inner)
                n_s[:, cols] = (
                    h_s[:, cols].astype(F32) + mm(o, w[...].reshape(inner, inner))
                ).astype(BF)
            send = pltpu.make_async_copy(n_s, out, sems.at[13])
            send.start()
            send.wait()

        for copy in (save_h, save_a, save_q, save_o, save_l):
            copy.wait()


def backward_kernel(cycle, first, micro, last, sec, recv, seeds, bias, gains, pack, *refs):
    (sh, sa, sq, so, sl, sg, sd, sn, sp) = refs[9:18]
    out = refs[18]
    (h_s, wi_s, wl_s, wr_s, g_s, q_s, d_s, k_s, v_s, b_s, l_s, pd_s, gn_s, n_s, do_s, sems) = refs[19:]
    inner = k_s.shape[1]
    feat = h_s.shape[1]
    heads = inner // HEAD
    late = (cycle - first) % 2 == 0
    keys = 2 * ROWS if late else ROWS
    section = sec[0]
    n = cycle - first - 2 * (last - section)

    @pl.when((n >= 0) & (n < micro))
    def _():
        m = n + 1 if late else n - 1
        from_seed = pltpu.make_async_copy(seeds.at[pl.ds(m * ROWS, ROWS)], g_s, sems.at[5])
        from_right = pltpu.make_async_copy(recv, g_s, sems.at[5])

        @pl.when(section == last)
        def _():
            from_seed.start()

        @pl.when(section != last)
        def _():
            from_right.start()

        wi, wo = weight_copies(pack, wi_s, wl_s, wr_s, sems, inner)
        for copy in wo:
            copy.start()
        own = keys - ROWS
        loads = [
            pltpu.make_async_copy(sq.at[m, :, pl.ds(0, inner)], q_s, sems.at[6]),
            pltpu.make_async_copy(sq.at[m, :, pl.ds(inner, inner)], k_s.at[pl.ds(own, ROWS)], sems.at[7]),
            pltpu.make_async_copy(
                sq.at[m, :, pl.ds(2 * inner, inner)], v_s.at[pl.ds(own, ROWS)], sems.at[8]
            ),
            pltpu.make_async_copy(bias.at[pl.ds(m * ROWS, ROWS)], b_s, sems.at[9]),
            pltpu.make_async_copy(sl.at[m], l_s, sems.at[10]),
            pltpu.make_async_copy(sh.at[m], h_s, sems.at[11]),
        ]
        if late:
            loads.append(
                pltpu.make_async_copy(
                    sq.at[m - 1, :, pl.ds(inner, inner)], k_s.at[pl.ds(0, ROWS)], sems.at[12]
                )
            )
            loads.append(
                pltpu.make_async_copy(
                    sq.at[m - 1, :, pl.ds(2 * inner, inner)], v_s.at[pl.ds(0, ROWS)], sems.at[13]
                )
            )
        else:
            loads.append(pltpu.make_async_copy(sp, pd_s, sems.at[12]))
        for copy in loads:
            copy.start()
        for copy in wi:
            copy.start()
        from_right.wait()
        save_g = pltpu.make_async_copy(g_s, sg.at[m], sems.at[14])
        save_g.start()
        for copy in wo:
            copy.wait()
        do_s[...] = (
            mm(g_s[:, :inner], wl_s[...].reshape(inner, inner), 1, 1)
            + mm(g_s[:, inner:], wr_s[...].reshape(inner, inner), 1, 1)
        ).astype(BF)
        for copy in loads:
            copy.wait()
        mask = b_s[:, :keys]
        scale = HEAD ** (-0.5)
        for e in range(heads):
            lo, hi = e * HEAD, (e + 1) * HEAD
            q = q_s[:, lo:hi]
            k = k_s[:keys, lo:hi]
            v = v_s[:keys, lo:hi]
            do = do_s[:, lo:hi]
            s = mm(q, k, 1, 1) * scale + mask
            p = jnp.exp(s - l_s[:, e:e + 1])
            dp = mm(do, v, 1, 1)
            inside = jnp.sum(dp * p, axis=-1, keepdims=True)
            ds = (p * (dp - inside) * scale).astype(BF)
            d_s[:, lo:hi] = mm(ds, k).astype(BF)
            dk = mm(ds, q, 0, 0)
            dv = mm(p.astype(BF), do, 0, 0)
            if late:
                pd_s[:, lo:hi] = dk[:ROWS]
                pd_s[:, inner + lo:inner + hi] = dv[:ROWS]
                dk, dv = dk[ROWS:], dv[ROWS:]
            else:
                dk = dk + pd_s[:, lo:hi]
                dv = dv + pd_s[:, inner + lo:inner + hi]
            d_s[:, inner + lo:inner + hi] = dk.astype(BF)
            d_s[:, 2 * inner + lo:2 * inner + hi] = dv.astype(BF)
        saves = [save_g, pltpu.make_async_copy(d_s, sd.at[m], sems.at[15])]
        saves[-1].start()
        if late:
            saves.append(pltpu.make_async_copy(pd_s, sp, sems.at[16]))
            saves[-1].start()
        r, u = unit(h_s[...].astype(F32))
        da = None
        for k in range(3):
            wi[k].wait()
            cols = slice(k * inner, (k + 1) * inner)
            term = mm(d_s[:, cols], wi_s[:, :, cols].reshape(feat, inner), 1, 1)
            da = term if da is None else da + term
        gn_s[...] = jnp.sum((da * u).reshape(ROWS // 8, 8, feat), axis=0)
        saves.append(pltpu.make_async_copy(gn_s, sn.at[m], sems.at[17]))
        saves[-1].start()
        e = da * gains[...]
        mean = jnp.mean(e * u, axis=-1, keepdims=True)
        n_s[...] = (g_s[...].astype(F32) + r * (e - u * mean)).astype(BF)
        saves.append(pltpu.make_async_copy(n_s, out, sems.at[18]))
        saves[-1].start()
        for copy in saves:
            copy.wait()


ANY = pl.BlockSpec(memory_space=pl.ANY)
SMEM = pl.BlockSpec(memory_space=pltpu.SMEM)
VMEM = pl.BlockSpec(memory_space=pltpu.VMEM)


def call(body, ins, in_specs, states, out_shape, scratch, flops, name):
    count = len(ins)
    shapes = [jax.ShapeDtypeStruct(s.shape, s.dtype) for s in states]
    got = pl.pallas_call(
        body,
        out_shape=shapes + [out_shape],
        in_specs=in_specs + [ANY] * len(states),
        out_specs=[ANY] * (len(states) + 1),
        scratch_shapes=scratch,
        input_output_aliases={count + i: i for i in range(len(states))},
        compiler_params=pltpu.CompilerParams(vmem_limit_bytes=20 * 1024 * 1024),
        cost_estimate=pl.CostEstimate(flops=flops, bytes_accessed=12 * 1024 * 1024, transcendentals=0),
        name=name,
    )(*ins, *states)
    return got[-1], list(got[:-1])


def spread_sum(value, whole):
    rounds = [[1], [2, 4, 6], [8]]
    if whole:
        rounds = [[1], [2, 4, 6], [8, 64, 72], [16, 32, 48]]
    for masks in rounds:
        got = [
            lax.ppermute(value, ("section", "dp"), [(i, i ^ mask) for i in range(128)])
            for mask in masks
        ]
        for other in got:
            value = value + other
    return value


def local(hidden_in, segment_ids, cotangent, in_proj, out_proj, norm_gains):
    section = lax.axis_index("section")
    sections = lax.axis_size("section")
    width = lax.axis_size("dp")
    last = sections - 1
    seqs, length = segment_ids.shape
    feat = hidden_in.shape[1]
    shard = in_proj.shape[1]
    inner = out_proj.shape[1] * width
    micro = seqs * length // ROWS
    half = out_proj.shape[1]
    wo = jnp.concatenate([out_proj[0, :, :inner], out_proj[0, :, inner:]], axis=0)
    pack = lax.all_gather(jnp.concatenate([in_proj[0], wo], axis=1), "dp", axis=0)
    loss_scale = 1.0 / math.sqrt(width * hidden_in.shape[0])
    seeds = (cotangent.astype(F32) * loss_scale).astype(BF)
    rows = lax.broadcasted_iota(jnp.int32, (length, length), 0)
    cols = lax.broadcasted_iota(jnp.int32, (length, length), 1)
    allowed = (cols <= rows)[None] & (segment_ids[:, :, None] == segment_ids[:, None, :])
    bias = jnp.where(allowed, 0.0, MASKED).astype(F32).reshape(seqs * length, length)
    sec = jnp.full((1,), section, jnp.int32)

    def blank(*shape, dtype=BF):
        return jnp.zeros(shape, dtype)

    def vmem(*shape, dtype=BF):
        return pltpu.VMEM(shape, dtype)

    weights = [vmem(width, shard, 3 * inner), vmem(width, half, inner), vmem(width, half, inner)]
    f_scratch = (
        [vmem(ROWS, feat)] + weights
        + [vmem(ROWS, feat), vmem(ROWS, 3 * inner), vmem(ROWS, inner), vmem(ROWS, 2 * inner)]
        + [vmem(ROWS, length, dtype=F32), vmem(ROWS, HEAD, dtype=F32), vmem(ROWS, feat)]
        + [pltpu.SemaphoreType.DMA((14,))]
    )
    b_scratch = (
        [vmem(ROWS, feat)] + weights
        + [vmem(ROWS, feat), vmem(ROWS, inner), vmem(ROWS, 3 * inner)]
        + [vmem(2 * ROWS, inner), vmem(2 * ROWS, inner)]
        + [vmem(ROWS, length, dtype=F32), vmem(ROWS, HEAD, dtype=F32)]
        + [vmem(ROWS, 2 * inner, dtype=F32), vmem(8, feat, dtype=F32)]
        + [vmem(ROWS, feat), vmem(ROWS, inner)]
        + [pltpu.SemaphoreType.DMA((19,))]
    )
    states = [
        blank(micro, ROWS, feat),
        blank(micro, ROWS, feat),
        blank(micro, ROWS, 3 * inner),
        blank(micro, ROWS, inner),
        blank(micro, ROWS, HEAD, dtype=F32),
        blank(micro, ROWS, feat),
        blank(micro, ROWS, 3 * inner),
        blank(micro, 8, feat, dtype=F32),
        blank(ROWS, 2 * inner, dtype=F32),
    ]
    moved = jax.ShapeDtypeStruct((ROWS, feat), BF)
    per_row = 2 * feat * 4 * inner
    first = 2 * last + 1
    end = first + 2 * last + micro
    gains = norm_gains
    f_recv, b_recv = {}, {}
    for cycle in range(end):
        on = [s for s in range(sections) if 0 <= cycle - 2 * s < micro]
        if on:
            out, states[:5] = call(
                functools.partial(forward_kernel, cycle, micro, last),
                [sec, f_recv.get(cycle, hidden_in[:ROWS]), hidden_in, bias, gains, pack],
                [SMEM, ANY, ANY, ANY, VMEM, ANY],
                states[:5], moved, f_scratch, ROWS * per_row, "fwd_half",
            )
            pairs = [(s, s + 1) for s in on if s < last]
            if pairs:
                f_recv[cycle + 2] = lax.ppermute(out, "section", pairs)
        on = [s for s in range(sections) if 0 <= cycle - first - 2 * (last - s) < micro]
        if on:
            out, states = call(
                functools.partial(backward_kernel, cycle, first, micro, last),
                [sec, b_recv.get(cycle, seeds[:ROWS]), seeds, bias, gains, pack],
                [SMEM, ANY, ANY, ANY, VMEM, ANY],
                states, moved, b_scratch, 2 * ROWS * per_row, "bwd_half",
            )
            pairs = [(s, s - 1) for s in on if s > 0]
            if pairs:
                b_recv[cycle + 2] = lax.ppermute(out, "section", pairs)
    sa, so, sg, sd, sn = states[1], states[3], states[5], states[6], states[7]
    tokens = micro * ROWS
    out_part = mm(so.reshape(tokens, inner), sg.reshape(tokens, feat), 0, 0).astype(BF)
    in_part = mm(sa.reshape(tokens, feat), sd.reshape(tokens, 3 * inner), 0, 0).astype(BF)
    gain_part = jnp.sum(sn, axis=(0, 1)).astype(BF).astype(F32).reshape(feat // HEAD, HEAD)
    out_sum = lax.psum_scatter(out_part, "dp", scatter_dimension=0, tiled=True).astype(F32)
    in_sum = lax.psum_scatter(in_part, "dp", scatter_dimension=0, tiled=True).astype(F32)
    gain_all = spread_sum(gain_part, False).reshape(feat)
    own = feat // width
    gain_sum = lax.dynamic_slice_in_dim(gain_all, lax.axis_index("dp") * own, own)
    squares = jnp.sum(in_sum * in_sum) + jnp.sum(out_sum * out_sum) + jnp.sum(gain_sum * gain_sum)
    grand_total = spread_sum(jnp.full((8, HEAD), squares, F32), True)[0, 0]
    count = float(sections * width * (in_sum.size + out_sum.size + gain_sum.size))
    return (in_sum[None], out_sum[None], gain_sum[None], jnp.sqrt(grand_total / count))


def solution(mesh):
    placed = (
        P("dp", None),
        P("dp", None),
        P("dp", None),
        P("section", "dp", None),
        P("section", "dp", None),
        P("section", None),
    )
    return jax.shard_map(
        local,
        mesh=mesh,
        in_specs=placed,
        out_specs=(P("section", "dp", None), P("section", "dp", None), P("section", "dp"), P()),
        check_vma=False,
    )
```

```python
import functools
import math

import jax
import jax.numpy as jnp
from jax import lax
from jax.experimental import pallas as pl
from jax.experimental.pallas import tpu as pltpu
from jax.sharding import PartitionSpec as P

HEAD = 128
ROWS = 128
EPS = 1e-05
MASKED = -1e30
BF = jnp.bfloat16
F32 = jnp.float32


def mm(left, right, lc=1, rc=0):
    return lax.dot_general(left, right, (((lc,), (rc,)), ((), ())), preferred_element_type=F32)


def unit(h):
    r = lax.rsqrt(jnp.mean(h * h, axis=-1, keepdims=True) + EPS)
    return r, h * r


def weight_copies(pack, wi_s, wl_s, wr_s, sems, inner):
    half = wl_s.shape[1]
    third = 3 * inner
    wi = [
        pltpu.make_async_copy(
            pack.at[:, :, pl.ds(k * inner, inner)], wi_s.at[:, :, pl.ds(k * inner, inner)], sems.at[k]
        )
        for k in range(3)
    ]
    wo = [
        pltpu.make_async_copy(pack.at[:, pl.ds(0, half), pl.ds(third, inner)], wl_s, sems.at[3]),
        pltpu.make_async_copy(pack.at[:, pl.ds(half, half), pl.ds(third, inner)], wr_s, sems.at[4]),
    ]
    return wi, wo


def forward_kernel(cycle, micro, last, sec, recv, hid, bias, gains, pack, *refs):
    (sh, sa, sq, so, sl) = refs[5:10]
    out = refs[10]
    (h_s, wi_s, wl_s, wr_s, a_s, q_s, o_s, kv_s, b_s, l_s, n_s, sems) = refs[11:]
    inner = o_s.shape[1]
    feat = h_s.shape[1]
    heads = inner // HEAD
    odd = cycle % 2 == 1
    keys = 2 * ROWS if odd else ROWS
    section = sec[0]
    m = cycle - 2 * section

    @pl.when((m >= 0) & (m < micro))
    def _():
        from_in = pltpu.make_async_copy(hid.at[pl.ds(m * ROWS, ROWS)], h_s, sems.at[5])
        from_left = pltpu.make_async_copy(recv, h_s, sems.at[5])

        @pl.when(section == 0)
        def _():
            from_in.start()

        @pl.when(section != 0)
        def _():
            from_left.start()

        wi, wo = weight_copies(pack, wi_s, wl_s, wr_s, sems, inner)
        for copy in wi:
            copy.start()
        load_b = pltpu.make_async_copy(bias.at[pl.ds(m * ROWS, ROWS)], b_s, sems.at[6])
        load_b.start()
        if odd:
            load_kv = pltpu.make_async_copy(
                sq.at[m - 1, :, pl.ds(inner, 2 * inner)], kv_s, sems.at[7]
            )
            load_kv.start()
        for copy in wo:
            copy.start()
        from_left.wait()
        save_h = pltpu.make_async_copy(h_s, sh.at[m], sems.at[8])
        save_h.start()
        h = h_s[...].astype(F32)
        _, u = unit(h)
        a_s[...] = (u * gains[...]).astype(BF)
        save_a = pltpu.make_async_copy(a_s, sa.at[m], sems.at[9])
        save_a.start()
        a = a_s[...]
        for k in range(3):
            wi[k].wait()
            w = wi_s[:, :, k * inner:(k + 1) * inner].reshape(feat, inner)
            q_s[:, k * inner:(k + 1) * inner] = mm(a, w).astype(BF)
        save_q = pltpu.make_async_copy(q_s, sq.at[m], sems.at[10])
        save_q.start()
        load_b.wait()
        if odd:
            load_kv.wait()
        lane = lax.broadcasted_iota(jnp.int32, (ROWS, HEAD), 1)
        lse = jnp.zeros((ROWS, HEAD), F32)
        mask = b_s[:, :keys]
        for e in range(heads):
            lo, hi = e * HEAD, (e + 1) * HEAD
            q = q_s[:, lo:hi]
            k = q_s[:, inner + lo:inner + hi]
            v = q_s[:, 2 * inner + lo:2 * inner + hi]
            if odd:
                k = jnp.concatenate([kv_s[:, lo:hi], k], axis=0)
                v = jnp.concatenate([kv_s[:, inner + lo:inner + hi], v], axis=0)
            s = mm(q, k, 1, 1) * HEAD ** (-0.5) + mask
            top = jnp.max(s, axis=-1, keepdims=True)
            x = jnp.exp(s - top)
            total = jnp.sum(x, axis=-1, keepdims=True)
            p = x / total
            o_s[:, lo:hi] = mm(p.astype(BF), v).astype(BF)
            lse = jnp.where(lane == e, top + jnp.log(total), lse)
        l_s[...] = lse
        save_o = pltpu.make_async_copy(o_s, so.at[m], sems.at[11])
        save_o.start()
        save_l = pltpu.make_async_copy(l_s, sl.at[m], sems.at[12])
        save_l.start()
        for copy in wo:
            copy.wait()

        @pl.when(section != last)
        def _():
            o = o_s[...]
            for part, w in ((0, wl_s), (1, wr_s)):
                cols = slice(part * inner, (part + 1) * inner)
                n_s[:, cols] = (
                    h_s[:, cols].astype(F32) + mm(o, w[...].reshape(inner, inner))
                ).astype(BF)
            send = pltpu.make_async_copy(n_s, out, sems.at[13])
            send.start()
            send.wait()

        for copy in (save_h, save_a, save_q, save_o, save_l):
            copy.wait()


def backward_kernel(cycle, first, micro, last, sec, recv, seeds, bias, gains, pack, *refs):
    (sh, sa, sq, so, sl, sg, sd, sn, sp) = refs[9:18]
    out = refs[18]
    (h_s, wi_s, wl_s, wr_s, g_s, q_s, d_s, k_s, v_s, b_s, l_s, pd_s, gn_s, n_s, do_s, sems) = refs[19:]
    inner = k_s.shape[1]
    feat = h_s.shape[1]
    heads = inner // HEAD
    late = (cycle - first) % 2 == 0
    keys = 2 * ROWS if late else ROWS
    section = sec[0]
    n = cycle - first - 2 * (last - section)

    @pl.when((n >= 0) & (n < micro))
    def _():
        m = n + 1 if late else n - 1
        from_seed = pltpu.make_async_copy(seeds.at[pl.ds(m * ROWS, ROWS)], g_s, sems.at[5])
        from_right = pltpu.make_async_copy(recv, g_s, sems.at[5])

        @pl.when(section == last)
        def _():
            from_seed.start()

        @pl.when(section != last)
        def _():
            from_right.start()

        wi, wo = weight_copies(pack, wi_s, wl_s, wr_s, sems, inner)
        for copy in wo:
            copy.start()
        own = keys - ROWS
        loads = [
            pltpu.make_async_copy(sq.at[m, :, pl.ds(0, inner)], q_s, sems.at[6]),
            pltpu.make_async_copy(sq.at[m, :, pl.ds(inner, inner)], k_s.at[pl.ds(own, ROWS)], sems.at[7]),
            pltpu.make_async_copy(
                sq.at[m, :, pl.ds(2 * inner, inner)], v_s.at[pl.ds(own, ROWS)], sems.at[8]
            ),
            pltpu.make_async_copy(bias.at[pl.ds(m * ROWS, ROWS)], b_s, sems.at[9]),
            pltpu.make_async_copy(sl.at[m], l_s, sems.at[10]),
            pltpu.make_async_copy(sh.at[m], h_s, sems.at[11]),
        ]
        if late:
            loads.append(
                pltpu.make_async_copy(
                    sq.at[m - 1, :, pl.ds(inner, inner)], k_s.at[pl.ds(0, ROWS)], sems.at[12]
                )
            )
            loads.append(
                pltpu.make_async_copy(
                    sq.at[m - 1, :, pl.ds(2 * inner, inner)], v_s.at[pl.ds(0, ROWS)], sems.at[13]
                )
            )
        else:
            loads.append(pltpu.make_async_copy(sp, pd_s, sems.at[12]))
        for copy in loads:
            copy.start()
        for copy in wi:
            copy.start()
        from_right.wait()
        save_g = pltpu.make_async_copy(g_s, sg.at[m], sems.at[14])
        save_g.start()
        for copy in wo:
            copy.wait()
        do_s[...] = (
            mm(g_s[:, :inner], wl_s[...].reshape(inner, inner), 1, 1)
            + mm(g_s[:, inner:], wr_s[...].reshape(inner, inner), 1, 1)
        ).astype(BF)
        for copy in loads:
            copy.wait()
        mask = b_s[:, :keys]
        scale = HEAD ** (-0.5)
        for e in range(heads):
            lo, hi = e * HEAD, (e + 1) * HEAD
            q = q_s[:, lo:hi]
            k = k_s[:keys, lo:hi]
            v = v_s[:keys, lo:hi]
            do = do_s[:, lo:hi]
            s = mm(q, k, 1, 1) * scale + mask
            p = jnp.exp(s - l_s[:, e:e + 1])
            dp = mm(do, v, 1, 1)
            inside = jnp.sum(dp * p, axis=-1, keepdims=True)
            ds = (p * (dp - inside) * scale).astype(BF)
            d_s[:, lo:hi] = mm(ds, k).astype(BF)
            dk = mm(ds, q, 0, 0)
            dv = mm(p.astype(BF), do, 0, 0)
            if late:
                pd_s[:, lo:hi] = dk[:ROWS]
                pd_s[:, inner + lo:inner + hi] = dv[:ROWS]
                dk, dv = dk[ROWS:], dv[ROWS:]
            else:
                dk = dk + pd_s[:, lo:hi]
                dv = dv + pd_s[:, inner + lo:inner + hi]
            d_s[:, inner + lo:inner + hi] = dk.astype(BF)
            d_s[:, 2 * inner + lo:2 * inner + hi] = dv.astype(BF)
        saves = [save_g, pltpu.make_async_copy(d_s, sd.at[m], sems.at[15])]
        saves[-1].start()
        if late:
            saves.append(pltpu.make_async_copy(pd_s, sp, sems.at[16]))
            saves[-1].start()
        r, u = unit(h_s[...].astype(F32))
        da = None
        for k in range(3):
            wi[k].wait()
            cols = slice(k * inner, (k + 1) * inner)
            term = mm(d_s[:, cols], wi_s[:, :, cols].reshape(feat, inner), 1, 1)
            da = term if da is None else da + term
        gn_s[...] = jnp.sum((da * u).reshape(ROWS // 8, 8, feat), axis=0)
        saves.append(pltpu.make_async_copy(gn_s, sn.at[m], sems.at[17]))
        saves[-1].start()
        e = da * gains[...]
        mean = jnp.mean(e * u, axis=-1, keepdims=True)
        n_s[...] = (g_s[...].astype(F32) + r * (e - u * mean)).astype(BF)
        saves.append(pltpu.make_async_copy(n_s, out, sems.at[18]))
        saves[-1].start()
        for copy in saves:
            copy.wait()


ANY = pl.BlockSpec(memory_space=pl.ANY)
SMEM = pl.BlockSpec(memory_space=pltpu.SMEM)
VMEM = pl.BlockSpec(memory_space=pltpu.VMEM)


def call(body, ins, in_specs, states, out_shape, scratch, flops, name):
    count = len(ins)
    shapes = [jax.ShapeDtypeStruct(s.shape, s.dtype) for s in states]
    got = pl.pallas_call(
        body,
        out_shape=shapes + [out_shape],
        in_specs=in_specs + [ANY] * len(states),
        out_specs=[ANY] * (len(states) + 1),
        scratch_shapes=scratch,
        input_output_aliases={count + i: i for i in range(len(states))},
        compiler_params=pltpu.CompilerParams(vmem_limit_bytes=20 * 1024 * 1024),
        cost_estimate=pl.CostEstimate(flops=flops, bytes_accessed=12 * 1024 * 1024, transcendentals=0),
        name=name,
    )(*ins, *states)
    return got[-1], list(got[:-1])


def pair_set(on, low, high, size):
    hops = [s for s in on if low <= s < high]
    if not hops:
        return []
    start = min(max(hops[-1] - size + 1, low), high - size)
    return list(range(start, start + size))


def spread_sum(value, whole):
    rounds = [[1], [2, 4, 6], [8]]
    if whole:
        rounds = [[1], [2, 4, 6], [8], [64], [16, 32, 48]]
    for masks in rounds:
        got = [
            lax.ppermute(value, ("section", "dp"), [(i, i ^ mask) for i in range(128)])
            for mask in masks
        ]
        for other in got:
            value = value + other
    return value


def local(hidden_in, segment_ids, cotangent, in_proj, out_proj, norm_gains):
    section = lax.axis_index("section")
    sections = lax.axis_size("section")
    width = lax.axis_size("dp")
    last = sections - 1
    seqs, length = segment_ids.shape
    feat = hidden_in.shape[1]
    shard = in_proj.shape[1]
    inner = out_proj.shape[1] * width
    micro = seqs * length // ROWS
    half = out_proj.shape[1]
    wo = jnp.concatenate([out_proj[0, :, :inner], out_proj[0, :, inner:]], axis=0)
    pack = lax.all_gather(jnp.concatenate([in_proj[0], wo], axis=1), "dp", axis=0)
    loss_scale = 1.0 / math.sqrt(width * hidden_in.shape[0])
    seeds = (cotangent.astype(F32) * loss_scale).astype(BF)
    rows = lax.broadcasted_iota(jnp.int32, (length, length), 0)
    cols = lax.broadcasted_iota(jnp.int32, (length, length), 1)
    allowed = (cols <= rows)[None] & (segment_ids[:, :, None] == segment_ids[:, None, :])
    bias = jnp.where(allowed, 0.0, MASKED).astype(F32).reshape(seqs * length, length)
    sec = jnp.full((1,), section, jnp.int32)

    def blank(*shape, dtype=BF):
        return jnp.zeros(shape, dtype)

    def vmem(*shape, dtype=BF):
        return pltpu.VMEM(shape, dtype)

    weights = [vmem(width, shard, 3 * inner), vmem(width, half, inner), vmem(width, half, inner)]
    f_scratch = (
        [vmem(ROWS, feat)] + weights
        + [vmem(ROWS, feat), vmem(ROWS, 3 * inner), vmem(ROWS, inner), vmem(ROWS, 2 * inner)]
        + [vmem(ROWS, length, dtype=F32), vmem(ROWS, HEAD, dtype=F32), vmem(ROWS, feat)]
        + [pltpu.SemaphoreType.DMA((14,))]
    )
    b_scratch = (
        [vmem(ROWS, feat)] + weights
        + [vmem(ROWS, feat), vmem(ROWS, inner), vmem(ROWS, 3 * inner)]
        + [vmem(2 * ROWS, inner), vmem(2 * ROWS, inner)]
        + [vmem(ROWS, length, dtype=F32), vmem(ROWS, HEAD, dtype=F32)]
        + [vmem(ROWS, 2 * inner, dtype=F32), vmem(8, feat, dtype=F32)]
        + [vmem(ROWS, feat), vmem(ROWS, inner)]
        + [pltpu.SemaphoreType.DMA((19,))]
    )
    states = [
        blank(micro, ROWS, feat),
        blank(micro, ROWS, feat),
        blank(micro, ROWS, 3 * inner),
        blank(micro, ROWS, inner),
        blank(micro, ROWS, HEAD, dtype=F32),
        blank(micro, ROWS, feat),
        blank(micro, ROWS, 3 * inner),
        blank(micro, 8, feat, dtype=F32),
        blank(ROWS, 2 * inner, dtype=F32),
    ]
    moved = jax.ShapeDtypeStruct((ROWS, feat), BF)
    per_row = 2 * feat * 4 * inner
    first = 2 * last + 1
    end = first + 2 * last + micro
    gains = norm_gains
    f_recv, b_recv = {}, {}
    for cycle in range(end):
        on = [s for s in range(sections) if 0 <= cycle - 2 * s < micro]
        if on:
            out, states[:5] = call(
                functools.partial(forward_kernel, cycle, micro, last),
                [sec, f_recv.get(cycle, hidden_in[:ROWS]), hidden_in, bias, gains, pack],
                [SMEM, ANY, ANY, ANY, VMEM, ANY],
                states[:5], moved, f_scratch, ROWS * per_row, "fwd_half",
            )
            pairs = pair_set(on, 0, last, micro // 2)
            if pairs:
                pairs = [(s, s + 1) for s in pairs]
                f_recv[cycle + 2] = lax.ppermute(out, "section", pairs)
        on = [s for s in range(sections) if 0 <= cycle - first - 2 * (last - s) < micro]
        if on:
            out, states = call(
                functools.partial(backward_kernel, cycle, first, micro, last),
                [sec, b_recv.get(cycle, seeds[:ROWS]), seeds, bias, gains, pack],
                [SMEM, ANY, ANY, ANY, VMEM, ANY],
                states, moved, b_scratch, 2 * ROWS * per_row, "bwd_half",
            )
            pairs = pair_set([s - 1 for s in on], 0, last, micro // 2)
            if pairs:
                pairs = [(s + 1, s) for s in pairs]
                b_recv[cycle + 2] = lax.ppermute(out, "section", pairs)
    sa, so, sg, sd, sn = states[1], states[3], states[5], states[6], states[7]
    tokens = micro * ROWS
    out_part = mm(so.reshape(tokens, inner), sg.reshape(tokens, feat), 0, 0).astype(BF)
    in_part = mm(sa.reshape(tokens, feat), sd.reshape(tokens, 3 * inner), 0, 0).astype(BF)
    gain_part = jnp.sum(sn, axis=(0, 1)).astype(BF).astype(F32).reshape(feat // HEAD, HEAD)
    out_sum = lax.psum_scatter(out_part, "dp", scatter_dimension=0, tiled=True).astype(F32)
    in_sum = lax.psum_scatter(in_part, "dp", scatter_dimension=0, tiled=True).astype(F32)
    gain_all = spread_sum(gain_part, False).reshape(feat)
    own = feat // width
    gain_sum = lax.dynamic_slice_in_dim(gain_all, lax.axis_index("dp") * own, own)
    squares = jnp.sum(in_sum * in_sum) + jnp.sum(out_sum * out_sum) + jnp.sum(gain_sum * gain_sum)
    grand_total = spread_sum(jnp.full((8, HEAD), squares, F32), True)[0, 0]
    count = float(sections * width * (in_sum.size + out_sum.size + gain_sum.size))
    return (in_sum[None], out_sum[None], gain_sum[None], jnp.sqrt(grand_total / count))


def solution(mesh):
    placed = (
        P("dp", None),
        P("dp", None),
        P("dp", None),
        P("section", "dp", None),
        P("section", "dp", None),
        P("section", None),
    )
    return jax.shard_map(
        local,
        mesh=mesh,
        in_specs=placed,
        out_specs=(P("section", "dp", None), P("section", "dp", None), P("section", "dp"), P()),
        check_vma=False,
    )
```

```python
import functools
import math

import jax
import jax.numpy as jnp
from jax import lax
from jax.experimental import pallas as pl
from jax.experimental.pallas import tpu as pltpu
from jax.sharding import PartitionSpec as P

HEAD = 128
ROWS = 64
EPS = 1e-05
MASKED = -1e30
MOST = 128
LIMIT = 8 * 1024 * 1024
BF = jnp.bfloat16
F32 = jnp.float32


def mm(left, right, lc=1, rc=0):
    return lax.dot_general(left, right, (((lc,), (rc,)), ((), ())), preferred_element_type=F32)


def unit(h):
    r = lax.rsqrt(jnp.mean(h * h, axis=-1, keepdims=True) + EPS)
    return r, h * r


def w_in(pack, k, inner):
    return pack[:, :, k * inner:(k + 1) * inner].reshape(-1, inner)


def w_out(pack, part, inner):
    half = pack.shape[1] // 2
    return pack[:, part * half:(part + 1) * half, 3 * inner:].reshape(-1, inner)


def prepare_kernel(cotangent, scale, *refs):
    seeds, sq, acc = refs[-3:]
    seeds[...] = (cotangent[...].astype(F32) * scale[0]).astype(BF)
    sq[...] = jnp.zeros_like(sq)
    acc[...] = jnp.zeros_like(acc)


def forward_kernel(cycle, micro, last, sec, recv, hid, bias, gains, pack, *refs):
    (sh, sa, sq, so, sl, out) = refs[5:11]
    inner = so.shape[2]
    heads = inner // HEAD
    span = bias.shape[2]
    section = sec[0]
    m = cycle - 2 * section

    @pl.when((m >= 0) & (m < micro))
    def _():
        own = pl.multiple_of(m * ROWS, ROWS)
        base = pl.multiple_of(own + span - ROWS, ROWS)
        h = jnp.where(section == 0, hid[pl.ds(own, ROWS)], recv[...])
        sh[m] = h
        _, u = unit(h.astype(F32))
        a = (u * gains[...]).astype(BF)
        sa[m] = a
        for k in range(3):
            sq[pl.ds(base, ROWS), k * inner:(k + 1) * inner] = mm(a, w_in(pack, k, inner)).astype(BF)
        mask = bias[m]
        scores = []
        for e in range(heads):
            lo, hi = e * HEAD, (e + 1) * HEAD
            q = sq[pl.ds(base, ROWS), lo:hi]
            k = sq[pl.ds(own, span), inner + lo:inner + hi]
            scores.append(mm(q, k, 1, 1) * HEAD ** (-0.5) + mask)
        tops = [jnp.max(s, axis=-1, keepdims=True) for s in scores]
        xs = [jnp.exp(s - top) for s, top in zip(scores, tops)]
        totals = [jnp.sum(x, axis=-1, keepdims=True) for x in xs]
        lane = lax.broadcasted_iota(jnp.int32, (ROWS, HEAD), 1)
        lse = jnp.zeros((ROWS, HEAD), F32)
        for e in range(heads):
            lo, hi = e * HEAD, (e + 1) * HEAD
            v = sq[pl.ds(own, span), 2 * inner + lo:2 * inner + hi]
            so[m, :, lo:hi] = (mm(xs[e].astype(BF), v) * (1.0 / totals[e])).astype(BF)
            lse = jnp.where(lane == e, tops[e] + jnp.log(totals[e]), lse)
        sl[m] = lse

        @pl.when(section != last)
        def _():
            o = so[m]
            for part in range(2):
                cols = slice(part * inner, (part + 1) * inner)
                out[:, cols] = (
                    sh[m, :, cols].astype(F32) + mm(o, w_out(pack, part, inner))
                ).astype(BF)


def backward_kernel(cycle, first, micro, last, per, sec, recv, seeds, bias, gains, pack, *refs):
    (sh, sa, sq, so, sl, sg, sd, sn, acc, out) = refs[9:19]
    inner = so.shape[2]
    feat = sh.shape[2]
    heads = inner // HEAD
    span = bias.shape[2]
    section = sec[0]
    n = cycle - first - 2 * (last - section)

    @pl.when((n >= 0) & (n < micro))
    def _():
        m = (n // per) * per + (per - 1) - n % per
        own = pl.multiple_of(m * ROWS, ROWS)
        base = pl.multiple_of(own + span - ROWS, ROWS)
        g = jnp.where(section == last, seeds[pl.ds(own, ROWS)], recv[...])
        sg[m] = g
        do_all = (
            mm(g[:, :inner], w_out(pack, 0, inner), 1, 1)
            + mm(g[:, inner:], w_out(pack, 1, inner), 1, 1)
        ).astype(BF)
        mask = bias[m]
        lse = sl[m]
        scale = HEAD ** (-0.5)
        cut = [slice(e * HEAD, (e + 1) * HEAD) for e in range(heads)]
        qs = [sq[pl.ds(base, ROWS), e * HEAD:(e + 1) * HEAD] for e in range(heads)]
        ks = [sq[pl.ds(own, span), inner + e * HEAD:inner + (e + 1) * HEAD] for e in range(heads)]
        vs = [sq[pl.ds(own, span), 2 * inner + e * HEAD:2 * inner + (e + 1) * HEAD] for e in range(heads)]
        dos = [do_all[:, c] for c in cut]
        ps = [jnp.exp(mm(qs[e], ks[e], 1, 1) * scale + mask - lse[:, e:e + 1]) for e in range(heads)]
        dps = [mm(dos[e], vs[e], 1, 1) for e in range(heads)]
        insides = [jnp.sum(dp * p, axis=-1, keepdims=True) for dp, p in zip(dps, ps)]
        dss = [(p * (dp - i) * scale).astype(BF) for p, dp, i in zip(ps, dps, insides)]
        for e in range(heads):
            lo, hi = e * HEAD, (e + 1) * HEAD
            sd[m, :, lo:hi] = mm(dss[e], ks[e]).astype(BF)
            dk = mm(dss[e], qs[e], 0, 0)
            dv = mm(ps[e].astype(BF), dos[e], 0, 0)
            for at, value in ((0, dk), (inner, dv)):
                total = acc[pl.ds(own, span), at + lo:at + hi] + value
                acc[pl.ds(own, span - ROWS), at + lo:at + hi] = total[:span - ROWS]
                sd[m, :, inner + at + lo:inner + at + hi] = total[span - ROWS:].astype(BF)
        r, u = unit(sh[m].astype(F32))
        da = None
        for k in range(3):
            term = mm(sd[m, :, k * inner:(k + 1) * inner], w_in(pack, k, inner), 1, 1)
            da = term if da is None else da + term
        sn[m] = jnp.sum((da * u).reshape(ROWS // 8, 8, feat), axis=0)
        e = da * gains[...]
        mean = jnp.mean(e * u, axis=-1, keepdims=True)
        out[...] = (sg[m].astype(F32) + r * (e - u * mean)).astype(BF)


SMEM = pl.BlockSpec(memory_space=pltpu.SMEM)
VMEM = pl.BlockSpec(memory_space=pltpu.VMEM)


def call(body, ins, states, out_shape, flops, name):
    count = len(ins)
    shapes = [jax.ShapeDtypeStruct(s.shape, s.dtype) for s in states]
    got = pl.pallas_call(
        body,
        out_shape=shapes + [out_shape],
        in_specs=[SMEM] + [VMEM] * (count - 1 + len(states)),
        out_specs=[VMEM] * (len(states) + 1),
        input_output_aliases={count + i: i for i in range(len(states))},
        compiler_params=pltpu.CompilerParams(vmem_limit_bytes=LIMIT),
        cost_estimate=pl.CostEstimate(flops=flops, bytes_accessed=12 * 1024 * 1024, transcendentals=0),
        name=name,
    )(*ins, *states)
    return got[-1], list(got[:-1])


def pair_set(on, low, high, size):
    hops = [s for s in on if low <= s < high]
    if not hops:
        return []
    size = max(size, len(hops))
    start = min(max(hops[-1] - size + 1, low), high - size)
    return list(range(start, start + size))


def spread_sum(value, whole):
    rounds = [[1], [2, 4, 6], [8]]
    if whole:
        rounds = [[1], [2, 4, 6], [8], [64], [16, 32, 48]]
    for masks in rounds:
        got = [
            lax.ppermute(value, ("section", "dp"), [(i, i ^ mask) for i in range(128)])
            for mask in masks
        ]
        for other in got:
            value = value + other
    return value


def local(hidden_in, segment_ids, cotangent, in_proj, out_proj, norm_gains):
    section = lax.axis_index("section")
    sections = lax.axis_size("section")
    width = lax.axis_size("dp")
    last = sections - 1
    seqs, length = segment_ids.shape
    feat = hidden_in.shape[1]
    shard = in_proj.shape[1]
    inner = out_proj.shape[1] * width
    micro = seqs * length // ROWS
    wo = jnp.concatenate([out_proj[0, :, :inner], out_proj[0, :, inner:]], axis=0)
    pack = lax.all_gather(jnp.concatenate([in_proj[0], wo], axis=1), "dp", axis=0)
    loss_scale = 1.0 / math.sqrt(width * hidden_in.shape[0])
    per = length // ROWS
    window = min(per, MOST // ROWS + 1)
    span = window * ROWS
    ahead = span - ROWS
    tokens = seqs * length
    ident = segment_ids + 8 * lax.broadcasted_iota(jnp.int32, (seqs, length), 0)
    ident = ident.reshape(micro, ROWS)
    padded = jnp.concatenate([jnp.full((ahead,), -1, jnp.int32), ident.reshape(tokens)])
    keys = jnp.stack([padded[i * ROWS:i * ROWS + span] for i in range(micro)])
    rows = lax.broadcasted_iota(jnp.int32, (ROWS, span), 0) + ahead
    cols = lax.broadcasted_iota(jnp.int32, (ROWS, span), 1)
    allowed = (cols <= rows)[None] & (ident[:, :, None] == keys[:, None, :])
    bias = jnp.where(allowed, 0.0, MASKED).astype(F32)
    sec = jnp.full((1,), section, jnp.int32)

    def shaped(*shape, dtype=BF):
        return jax.ShapeDtypeStruct(shape, dtype)

    sh, sa, so, sl, sg, sd, sn, seeds, sq, acc = pl.pallas_call(
        prepare_kernel,
        out_shape=[
            shaped(micro, ROWS, feat),
            shaped(micro, ROWS, feat),
            shaped(micro, ROWS, inner),
            shaped(micro, ROWS, HEAD, dtype=F32),
            shaped(micro, ROWS, feat),
            shaped(micro, ROWS, 3 * inner),
            shaped(micro, 8, feat, dtype=F32),
            shaped(tokens, feat),
            shaped(tokens + ahead, 3 * inner),
            shaped(tokens + ahead, 2 * inner, dtype=F32),
        ],
        in_specs=[VMEM, SMEM],
        out_specs=[VMEM] * 10,
        compiler_params=pltpu.CompilerParams(vmem_limit_bytes=LIMIT),
        cost_estimate=pl.CostEstimate(flops=10**9, bytes_accessed=40 * 1024 * 1024, transcendentals=0),
        name="prepare",
    )(cotangent, jnp.full((1,), loss_scale, F32))
    states = [sh, sa, sq, so, sl, sg, sd, sn, acc]
    moved = jax.ShapeDtypeStruct((ROWS, feat), BF)
    per_row = 2 * feat * 4 * inner
    first = 2 * last + per - 1
    end = first + 2 * last + micro
    gains = norm_gains
    f_recv, b_recv = {}, {}
    for cycle in range(end):
        on = [s for s in range(sections) if 0 <= cycle - 2 * s < micro]
        if on:
            out, states[:5] = call(
                functools.partial(forward_kernel, cycle, micro, last),
                [sec, f_recv.get(cycle, hidden_in[:ROWS]), hidden_in, bias, gains, pack],
                states[:5], moved, ROWS * per_row, "fwd_half",
            )
            pairs = pair_set(on, 0, last, micro // 2)
            if pairs:
                pairs = [(s, s + 1) for s in pairs]
                f_recv[cycle + 2] = lax.ppermute(out, "section", pairs)
        on = [s for s in range(sections) if 0 <= cycle - first - 2 * (last - s) < micro]
        if on:
            out, states = call(
                functools.partial(backward_kernel, cycle, first, micro, last, per),
                [sec, b_recv.get(cycle, seeds[:ROWS]), seeds, bias, gains, pack],
                states, moved, 2 * ROWS * per_row, "bwd_half",
            )
            pairs = pair_set([s - 1 for s in on], 0, last, micro // 2 if cycle > first + 3 else 1)
            if pairs:
                pairs = [(s + 1, s) for s in pairs]
                b_recv[cycle + 2] = lax.ppermute(out, "section", pairs)
    sa, so, sg, sd, sn = states[1], states[3], states[5], states[6], states[7]
    out_part = mm(so.reshape(tokens, inner), sg.reshape(tokens, feat), 0, 0).astype(BF)
    in_part = mm(sa.reshape(tokens, feat), sd.reshape(tokens, 3 * inner), 0, 0).astype(BF)
    gain_part = jnp.sum(sn, axis=(0, 1)).astype(BF).astype(F32).reshape(feat // HEAD, HEAD)
    out_sum = lax.psum_scatter(out_part, "dp", scatter_dimension=0, tiled=True).astype(F32)
    in_sum = lax.psum_scatter(in_part, "dp", scatter_dimension=0, tiled=True).astype(F32)
    gain_all = spread_sum(gain_part, False).reshape(feat)
    own = feat // width
    gain_sum = lax.dynamic_slice_in_dim(gain_all, lax.axis_index("dp") * own, own)
    squares = jnp.sum(in_sum * in_sum) + jnp.sum(out_sum * out_sum) + jnp.sum(gain_sum * gain_sum)
    grand_total = spread_sum(jnp.full((8, HEAD), squares, F32), True)[0, 0]
    count = float(sections * width * (in_sum.size + out_sum.size + gain_sum.size))
    return (in_sum[None], out_sum[None], gain_sum[None], jnp.sqrt(grand_total / count))


def solution(mesh):
    placed = (
        P("dp", None),
        P("dp", None),
        P("dp", None),
        P("section", "dp", None),
        P("section", "dp", None),
        P("section", None),
    )
    return jax.shard_map(
        local,
        mesh=mesh,
        in_specs=placed,
        out_specs=(P("section", "dp", None), P("section", "dp", None), P("section", "dp"), P()),
        check_vma=False,
    )
```

```python
import functools
import math

import jax
import jax.numpy as jnp
from jax import lax
from jax.experimental import pallas as pl
from jax.experimental.pallas import tpu as pltpu
from jax.sharding import PartitionSpec as P

HEAD = 128
ROWS = 128
EPS = 1e-05
MASKED = -1e30
LIMIT = 8 * 1024 * 1024
BF = jnp.bfloat16
F32 = jnp.float32


def mm(left, right, lc=1, rc=0):
    return lax.dot_general(left, right, (((lc,), (rc,)), ((), ())), preferred_element_type=F32)


def unit(h):
    r = lax.rsqrt(jnp.mean(h * h, axis=-1, keepdims=True) + EPS)
    return r, h * r


def w_in(pack, k, inner):
    return pack[:, :, k * inner:(k + 1) * inner].reshape(-1, inner)


def w_out(pack, part, inner):
    half = pack.shape[1] // 2
    return pack[:, part * half:(part + 1) * half, 3 * inner:].reshape(-1, inner)


def forward_kernel(cycle, micro, last, sec, recv, hid, bias, gains, pack, *refs):
    (sh, sa, sq, so, sl, out) = refs[-6:]
    inner = so.shape[2]
    heads = inner // HEAD
    odd = cycle % 2
    span = (1 + odd) * ROWS
    section = sec[0]
    m = cycle - 2 * section

    @pl.when((m >= 0) & (m < micro))
    def _():
        own = pl.multiple_of(m * ROWS, ROWS)
        base = pl.multiple_of(own - odd * ROWS, ROWS)

        @pl.when(section == 0)
        def _():
            sh[m] = hid[pl.ds(own, ROWS)]

        @pl.when(section != 0)
        def _():
            sh[m] = recv[...]

        _, u = unit(sh[m].astype(F32))
        a = (u * gains[...]).astype(BF)
        sa[m] = a
        for k in range(3):
            sq[pl.ds(own, ROWS), k * inner:(k + 1) * inner] = mm(a, w_in(pack, k, inner)).astype(BF)
        mask = bias[m, :, :span]
        scores = []
        for e in range(heads):
            lo, hi = e * HEAD, (e + 1) * HEAD
            q = sq[pl.ds(own, ROWS), lo:hi]
            k = sq[pl.ds(base, span), inner + lo:inner + hi]
            scores.append(mm(q, k, 1, 1) * HEAD ** (-0.5) + mask)
        tops = [jnp.max(s, axis=-1, keepdims=True) for s in scores]
        xs = [jnp.exp(s - top) for s, top in zip(scores, tops)]
        totals = [jnp.sum(x, axis=-1, keepdims=True) for x in xs]
        lane = lax.broadcasted_iota(jnp.int32, (ROWS, HEAD), 1)
        lse = jnp.zeros((ROWS, HEAD), F32)
        for e in range(heads):
            lo, hi = e * HEAD, (e + 1) * HEAD
            v = sq[pl.ds(base, span), 2 * inner + lo:2 * inner + hi]
            so[m, :, lo:hi] = (mm(xs[e].astype(BF), v) * (1.0 / totals[e])).astype(BF)
            lse = jnp.where(lane == e, tops[e] + jnp.log(totals[e]), lse)
        sl[m] = lse

        @pl.when(section != last)
        def _():
            o = so[m]
            for part in range(2):
                cols = slice(part * inner, (part + 1) * inner)
                out[:, cols] = (
                    sh[m, :, cols].astype(F32) + mm(o, w_out(pack, part, inner))
                ).astype(BF)


def backward_kernel(cycle, first, micro, last, loss_scale, sec, recv, cot, bias, gains, pack, sh, sq, sl, *refs):
    (sg, sd, sn, sp, out) = refs[-5:]
    inner = sd.shape[2] // 3
    feat = sh.shape[2]
    heads = inner // HEAD
    late = (cycle - first) % 2 == 0
    span = 2 * ROWS if late else ROWS
    section = sec[0]
    n = cycle - first - 2 * (last - section)

    @pl.when((n >= 0) & (n < micro))
    def _():
        m = n + 1 if late else n - 1
        own = pl.multiple_of(m * ROWS, ROWS)
        base = pl.multiple_of(own + ROWS - span, ROWS)

        @pl.when(section == last)
        def _():
            sg[m] = (cot[pl.ds(own, ROWS)].astype(F32) * loss_scale).astype(BF)

        @pl.when(section != last)
        def _():
            sg[m] = recv[...]

        g = sg[m]
        do_all = (
            mm(g[:, :inner], w_out(pack, 0, inner), 1, 1)
            + mm(g[:, inner:], w_out(pack, 1, inner), 1, 1)
        ).astype(BF)
        mask = bias[m, :, :span]
        lse = sl[m]
        scale = HEAD ** (-0.5)
        cut = [slice(e * HEAD, (e + 1) * HEAD) for e in range(heads)]
        qs = [sq[pl.ds(own, ROWS), e * HEAD:(e + 1) * HEAD] for e in range(heads)]
        ks = [sq[pl.ds(base, span), inner + e * HEAD:inner + (e + 1) * HEAD] for e in range(heads)]
        vs = [sq[pl.ds(base, span), 2 * inner + e * HEAD:2 * inner + (e + 1) * HEAD] for e in range(heads)]
        dos = [do_all[:, c] for c in cut]
        ps = [jnp.exp(mm(qs[e], ks[e], 1, 1) * scale + mask - lse[:, e:e + 1]) for e in range(heads)]
        dps = [mm(dos[e], vs[e], 1, 1) for e in range(heads)]
        insides = [jnp.sum(dp * p, axis=-1, keepdims=True) for dp, p in zip(dps, ps)]
        dss = [(p * (dp - i) * scale).astype(BF) for p, dp, i in zip(ps, dps, insides)]
        for e in range(heads):
            lo, hi = e * HEAD, (e + 1) * HEAD
            sd[m, :, lo:hi] = mm(dss[e], ks[e]).astype(BF)
            dk = mm(dss[e], qs[e], 0, 0)
            dv = mm(ps[e].astype(BF), dos[e], 0, 0)
            for at, value in ((0, dk), (inner, dv)):
                if late:
                    sp[:, at + lo:at + hi] = value[:ROWS]
                    value = value[ROWS:]
                else:
                    value = value + sp[:, at + lo:at + hi]
                sd[m, :, inner + at + lo:inner + at + hi] = value.astype(BF)
        r, u = unit(sh[m].astype(F32))
        da = None
        for k in range(3):
            term = mm(sd[m, :, k * inner:(k + 1) * inner], w_in(pack, k, inner), 1, 1)
            da = term if da is None else da + term
        sn[m] = jnp.sum((da * u).reshape(ROWS // 8, 8, feat), axis=0)
        e = da * gains[...]
        mean = jnp.mean(e * u, axis=-1, keepdims=True)
        out[...] = (sg[m].astype(F32) + r * (e - u * mean)).astype(BF)


def place(order, rel):
    low, high, y = rel % 2, (rel // 2) % 2, rel // 4
    bit = {2: (low + high) % 2, 6: high, 8: y}
    return 4 * bit[order[0]] + 2 * bit[order[1]] + bit[order[2]]


def gradient_kernel(order, cut, outs, me, sa, sd, so, sg, gain, keep, send):
    micro, rows, feat = sa.shape
    tokens = micro * rows
    width, shard, lanes = gain.shape
    inner = so.shape[2]
    lo, hi = cut
    mine = me[0]

    def store(d, pieces):
        low = (d + mine) % 2
        x = (d // 2) % 4
        my_x = (mine // 2) % 4
        first = (x + my_x) % 2
        second = (x // 2 + my_x // 2) % 2
        y = (d // 8 + mine // 8) % 2
        slot = place(order, first + 2 * second + 4 * y)
        for ref, want in ((keep, 0), (send, 1)):
            @pl.when(low == want)
            def _():
                for where, value in pieces:
                    ref[slot, where[0], where[1]] = value

    group = 4
    for c in range(width // group):
        a = sa[:, :, c * group * shard:(c + 1) * group * shard].reshape(tokens, group * shard)
        res = mm(a, sd[:, :, lo:hi].reshape(tokens, hi - lo), 0, 0).astype(BF)
        for j in range(group):
            d = c * group + j
            pieces = [((slice(None), slice(0, hi - lo)), res[j * shard:(j + 1) * shard])]
            if outs:
                pieces.append(((slice(None), slice(hi - lo + inner, None)), gain[d]))
            store(d, pieces)
    if outs:
        half = inner // width
        group = 8
        at = slice(hi - lo, hi - lo + inner)
        g = sg[...].reshape(tokens, feat)
        for c in range(width // group):
            o = so[:, :, c * group * half:(c + 1) * group * half].reshape(tokens, group * half)
            res = mm(o, g, 0, 0).astype(BF)
            for j in range(group):
                rows_of = res[j * half:(j + 1) * half]
                store(c * group + j, [
                    ((slice(0, half), at), rows_of[:, :inner]),
                    ((slice(half, 2 * half), at), rows_of[:, inner:]),
                ])


SMEM = pl.BlockSpec(memory_space=pltpu.SMEM)
VMEM = pl.BlockSpec(memory_space=pltpu.VMEM)


def call(body, ins, states, shapes, out_shape, flops, name):
    count = len(ins)
    got = pl.pallas_call(
        body,
        out_shape=list(shapes) + [out_shape],
        in_specs=[SMEM] + [VMEM] * (count - 1 + len(states)),
        out_specs=[VMEM] * (len(shapes) + 1),
        input_output_aliases={count + i: i for i in range(len(states))},
        compiler_params=pltpu.CompilerParams(vmem_limit_bytes=LIMIT),
        cost_estimate=pl.CostEstimate(flops=flops, bytes_accessed=12 * 1024 * 1024, transcendentals=0),
        name=name,
    )(*ins, *states)
    return got[-1], list(got[:-1])


def pair_set(on, low, high, size):
    hops = [s for s in on if low <= s < high]
    if not hops:
        return []
    size = max(size, len(hops))
    start = min(max(hops[-1] - size + 1, low), high - size)
    return list(range(start, start + size))


def spread_sum(value):
    for masks in ([1], [2, 4, 6], [8], [64], [16, 32, 48]):
        got = [
            lax.ppermute(value, ("section", "dp"), [(i, i ^ mask) for i in range(128)])
            for mask in masks
        ]
        for other in got:
            value = value + other
    return value


def swap(value, mask):
    return lax.ppermute(value, "dp", [(i, i ^ mask) for i in range(16)])


def scatter_sum(keep, send, order):
    total = keep.astype(F32) + swap(send, 1).astype(F32)
    for mask in order:
        half = total.shape[0] // 2
        total = total[:half] + swap(total[half:].astype(BF), mask).astype(F32)
    return total[0]


def local(hidden_in, segment_ids, cotangent, in_proj, out_proj, norm_gains):
    section = lax.axis_index("section")
    sections = lax.axis_size("section")
    width = lax.axis_size("dp")
    last = sections - 1
    seqs, length = segment_ids.shape
    feat = hidden_in.shape[1]
    shard = in_proj.shape[1]
    inner = out_proj.shape[1] * width
    micro = seqs * length // ROWS
    wo = jnp.concatenate([out_proj[0, :, :inner], out_proj[0, :, inner:]], axis=0)
    pack = lax.all_gather(jnp.concatenate([in_proj[0], wo], axis=1), "dp", axis=0)
    loss_scale = 1.0 / math.sqrt(width * hidden_in.shape[0])
    tokens = seqs * length
    ident = segment_ids.reshape(seqs, 2, ROWS)
    rows = lax.broadcasted_iota(jnp.int32, (ROWS, 2 * ROWS), 0)
    cols = lax.broadcasted_iota(jnp.int32, (ROWS, 2 * ROWS), 1)
    same = ident[:, :, :, None] == segment_ids[:, None, None, :]
    causal = jnp.stack([cols <= rows, cols <= rows + ROWS])
    bias = jnp.where(same & causal, 0.0, MASKED).astype(F32).reshape(micro, ROWS, length)
    sec = jnp.full((1,), section, jnp.int32)

    def shaped(*shape, dtype=BF):
        return jax.ShapeDtypeStruct(shape, dtype)

    f_shapes = [
        shaped(micro, ROWS, feat),
        shaped(micro, ROWS, feat),
        shaped(tokens, 3 * inner),
        shaped(micro, ROWS, inner),
        shaped(micro, ROWS, HEAD, dtype=F32),
    ]
    b_shapes = [
        shaped(micro, ROWS, feat),
        shaped(micro, ROWS, 3 * inner),
        shaped(micro, 8, feat, dtype=F32),
        shaped(ROWS, 2 * inner, dtype=F32),
    ]
    moved = shaped(ROWS, feat)
    per_row = 2 * feat * 4 * inner
    first = 2 * last + 1
    end = first + 2 * last + micro
    f_state, b_state = [], []
    f_recv, b_recv = {}, {}
    for cycle in range(end):
        on = [s for s in range(sections) if 0 <= cycle - 2 * s < micro]
        if on:
            out, f_state = call(
                functools.partial(forward_kernel, cycle, micro, last),
                [sec, f_recv.get(cycle, hidden_in[:ROWS]), hidden_in, bias, norm_gains, pack],
                f_state, f_shapes, moved, ROWS * per_row, "fwd_half",
            )
            pairs = pair_set(on, 0, last, micro // 2)
            if pairs:
                pairs = [(s, s + 1) for s in pairs]
                f_recv[cycle + 2] = lax.ppermute(out, "section", pairs)
        on = [s for s in range(sections) if 0 <= cycle - first - 2 * (last - s) < micro]
        if on:
            sh, _, sq, _, sl = f_state
            out, b_state = call(
                functools.partial(backward_kernel, cycle, first, micro, last, loss_scale),
                [sec, b_recv.get(cycle, cotangent[:ROWS]), cotangent, bias, norm_gains, pack, sh, sq, sl],
                b_state, b_shapes, moved, 2 * ROWS * per_row, "bwd_half",
            )
            pairs = pair_set([s - 1 for s in on], 0, last, micro // 2 if cycle > first + 1 else 1)
            if pairs:
                pairs = [(s + 1, s) for s in pairs]
                b_recv[cycle + 2] = lax.ppermute(out, "section", pairs)
    _, sa, _, so, _ = f_state
    sg, sd, sn, _ = b_state
    gain_part = jnp.sum(sn, axis=(0, 1)).astype(BF).reshape(width, shard, 1)
    gain_part = jnp.broadcast_to(gain_part, (width, shard, HEAD))
    me = jnp.full((1,), lax.axis_index("dp"), jnp.int32)
    third = 4 * inner // 3
    parts = []
    for index, order in enumerate(((2, 6, 8), (6, 8, 2), (8, 2, 6))):
        outs = index == 2
        cut = (index * third, min((index + 1) * third, 3 * inner))
        block = shaped(width // 2, shard, third + (HEAD if outs else 0))
        keep, send = pl.pallas_call(
            functools.partial(gradient_kernel, order, cut, outs),
            out_shape=[block, block],
            in_specs=[SMEM] + [VMEM] * 5,
            out_specs=[VMEM] * 2,
            compiler_params=pltpu.CompilerParams(vmem_limit_bytes=LIMIT),
            cost_estimate=pl.CostEstimate(
                flops=2 * tokens * feat * third, bytes_accessed=12 * 1024 * 1024, transcendentals=0
            ),
            name="gradient",
        )(me, sa, sd, so, sg, gain_part)
        parts.append((keep, send, order))
    parts = [scatter_sum(*part) for part in parts]
    rest = parts[2]
    edge = 3 * inner - 2 * third
    half = out_proj.shape[1]
    in_sum = jnp.concatenate([parts[0], parts[1], rest[:, :edge]], axis=1)
    out_sum = jnp.concatenate([rest[:half, edge:third], rest[half:, edge:third]], axis=1)
    gain_sum = rest[:, third]
    squares = sum(jnp.sum(p * p) for p in (parts[0], parts[1], rest[:, :third], gain_sum))
    grand_total = spread_sum(jnp.full((8, HEAD), squares, F32))[0, 0]
    count = float(sections * width * (in_sum.size + out_sum.size + gain_sum.size))
    return (in_sum[None], out_sum[None], gain_sum[None], jnp.sqrt(grand_total / count))


def solution(mesh):
    placed = (
        P("dp", None),
        P("dp", None),
        P("dp", None),
        P("section", "dp", None),
        P("section", "dp", None),
        P("section", None),
    )
    return jax.shard_map(
        local,
        mesh=mesh,
        in_specs=placed,
        out_specs=(P("section", "dp", None), P("section", "dp", None), P("section", "dp"), P()),
        check_vma=False,
    )
```

```python
import functools
import math

import jax
import jax.numpy as jnp
import numpy as np
from jax import lax
from jax.experimental import pallas as pl
from jax.experimental.pallas import tpu as pltpu
from jax.sharding import PartitionSpec as P

HEAD = 128
ROWS = 128
EPS = 1e-05
MASKED = -1e30
LIMIT = 8 * 1024 * 1024
BF = jnp.bfloat16
F32 = jnp.float32


def mm(left, right, lc=1, rc=0):
    return lax.dot_general(left, right, (((lc,), (rc,)), ((), ())), preferred_element_type=F32)


def unit(h):
    r = lax.rsqrt(jnp.mean(h * h, axis=-1, keepdims=True) + EPS)
    return r, h * r


def w_in(pack, k, inner):
    return pack[:, :, k * inner:(k + 1) * inner].reshape(-1, inner)


def w_out(pack, part, inner):
    half = pack.shape[1] // 2
    return pack[:, part * half:(part + 1) * half, 3 * inner:].reshape(-1, inner)


def forward_kernel(odd, micro, last, received, sec, at, hid, bias, gains, pack, *refs):
    (sh, sa, sq, so, sl, out) = refs[-6:]
    inner = so.shape[2]
    heads = inner // HEAD
    cycle = at[0]
    span = (1 + odd) * ROWS
    section = sec[0]
    m = cycle - 2 * section

    @pl.when((m >= 0) & (m < micro))
    def _():
        own = pl.multiple_of(m * ROWS, ROWS)
        base = pl.multiple_of(own - odd * ROWS, ROWS)

        @pl.when(section == 0)
        def _():
            sh[m] = hid[pl.ds(own, ROWS)]

        if received:
            @pl.when(section != 0)
            def _():
                sh[m] = refs[0][...]

        _, u = unit(sh[m].astype(F32))
        a = (u * gains[...]).astype(BF)
        sa[m] = a
        for k in range(3):
            sq[pl.ds(own, ROWS), k * inner:(k + 1) * inner] = mm(a, w_in(pack, k, inner)).astype(BF)
        mask = bias[m, :, :span]
        scores = []
        for e in range(heads):
            lo, hi = e * HEAD, (e + 1) * HEAD
            q = sq[pl.ds(own, ROWS), lo:hi]
            k = sq[pl.ds(base, span), inner + lo:inner + hi]
            scores.append(mm(q, k, 1, 1) * HEAD ** (-0.5) + mask)
        tops = [jnp.max(s, axis=-1, keepdims=True) for s in scores]
        xs = [jnp.exp(s - top) for s, top in zip(scores, tops)]
        totals = [jnp.sum(x, axis=-1, keepdims=True) for x in xs]
        lane = lax.broadcasted_iota(jnp.int32, (ROWS, HEAD), 1)
        lse = jnp.zeros((ROWS, HEAD), F32)
        for e in range(heads):
            lo, hi = e * HEAD, (e + 1) * HEAD
            v = sq[pl.ds(base, span), 2 * inner + lo:2 * inner + hi]
            so[m, :, lo:hi] = (mm(xs[e].astype(BF), v) * (1.0 / totals[e])).astype(BF)
            lse = jnp.where(lane == e, tops[e] + jnp.log(totals[e]), lse)
        sl[m] = lse

        @pl.when(section != last)
        def _():
            o = so[m]
            for part in range(2):
                cols = slice(part * inner, (part + 1) * inner)
                out[:, cols] = (
                    sh[m, :, cols].astype(F32) + mm(o, w_out(pack, part, inner))
                ).astype(BF)


def backward_kernel(late, micro, last, loss_scale, received, sec, at, cot, bias, gains, pack, sh, sq, sl, *refs):
    (sg, sd, sn, sp, out) = refs[-5:]
    inner = sd.shape[2] // 3
    feat = sh.shape[2]
    heads = inner // HEAD
    cycle = at[0]
    span = 2 * ROWS if late else ROWS
    section = sec[0]
    n = cycle - 2 * (last - section)

    @pl.when((n >= 0) & (n < micro))
    def _():
        m = n + 1 if late else n - 1
        own = pl.multiple_of(m * ROWS, ROWS)
        base = pl.multiple_of(own + ROWS - span, ROWS)

        @pl.when(section == last)
        def _():
            sg[m] = (cot[pl.ds(own, ROWS)].astype(F32) * loss_scale).astype(BF)

        if received:
            @pl.when(section != last)
            def _():
                sg[m] = refs[0][...]

        g = sg[m]
        do_all = (
            mm(g[:, :inner], w_out(pack, 0, inner), 1, 1)
            + mm(g[:, inner:], w_out(pack, 1, inner), 1, 1)
        ).astype(BF)
        mask = bias[m, :, :span]
        lse = sl[m]
        scale = HEAD ** (-0.5)
        cut = [slice(e * HEAD, (e + 1) * HEAD) for e in range(heads)]
        qs = [sq[pl.ds(own, ROWS), e * HEAD:(e + 1) * HEAD] for e in range(heads)]
        ks = [sq[pl.ds(base, span), inner + e * HEAD:inner + (e + 1) * HEAD] for e in range(heads)]
        vs = [sq[pl.ds(base, span), 2 * inner + e * HEAD:2 * inner + (e + 1) * HEAD] for e in range(heads)]
        dos = [do_all[:, c] for c in cut]
        ps = [jnp.exp(mm(qs[e], ks[e], 1, 1) * scale + mask - lse[:, e:e + 1]) for e in range(heads)]
        dps = [mm(dos[e], vs[e], 1, 1) for e in range(heads)]
        insides = [jnp.sum(dp * p, axis=-1, keepdims=True) for dp, p in zip(dps, ps)]
        dss = [(p * (dp - i) * scale).astype(BF) for p, dp, i in zip(ps, dps, insides)]
        for e in range(heads):
            lo, hi = e * HEAD, (e + 1) * HEAD
            sd[m, :, lo:hi] = mm(dss[e], ks[e]).astype(BF)
            dk = mm(dss[e], qs[e], 0, 0)
            dv = mm(ps[e].astype(BF), dos[e], 0, 0)
            for at, value in ((0, dk), (inner, dv)):
                if late:
                    sp[:, at + lo:at + hi] = value[:ROWS]
                    value = value[ROWS:]
                else:
                    value = value + sp[:, at + lo:at + hi]
                sd[m, :, inner + at + lo:inner + at + hi] = value.astype(BF)
        r, u = unit(sh[m].astype(F32))
        da = None
        for k in range(3):
            term = mm(sd[m, :, k * inner:(k + 1) * inner], w_in(pack, k, inner), 1, 1)
            da = term if da is None else da + term
        sn[m] = jnp.sum((da * u).reshape(ROWS // 8, 8, feat), axis=0)
        e = da * gains[...]
        mean = jnp.mean(e * u, axis=-1, keepdims=True)
        out[...] = (sg[m].astype(F32) + r * (e - u * mean)).astype(BF)


def place(order, rel):
    low, high, y = rel % 2, (rel // 2) % 2, rel // 4
    bit = {2: (low + high) % 2, 6: high, 8: y}
    return 4 * bit[order[0]] + 2 * bit[order[1]] + bit[order[2]]


def gradient_kernel(order, cut, outs, me, sa, sd, so, sg, sn, keep, send):
    micro, rows, feat = sa.shape
    tokens = micro * rows
    inner = so.shape[2]
    width, shard = 2 * keep.shape[0], keep.shape[1]
    lo, hi = cut
    mine = me[1]

    def store(d, pieces):
        low = (d + mine) % 2
        x = (d // 2) % 4
        my_x = (mine // 2) % 4
        first = (x + my_x) % 2
        second = (x // 2 + my_x // 2) % 2
        y = (d // 8 + mine // 8) % 2
        slot = place(order, first + 2 * second + 4 * y)
        for ref, want in ((keep, 0), (send, 1)):
            @pl.when(low == want)
            def _():
                for where, value in pieces:
                    ref[slot, where[0], where[1]] = value

    if outs:
        total = jnp.sum(sn[...], axis=(0, 1)).reshape(1, feat)
        gain = jnp.concatenate(
            [
                jnp.broadcast_to(total[:, c * HEAD:(c + 1) * HEAD], (HEAD, HEAD)).T
                for c in range(feat // HEAD)
            ],
            axis=0,
        ).astype(BF)
    group = 4
    for c in range(width // group):
        a = sa[:, :, c * group * shard:(c + 1) * group * shard].reshape(tokens, group * shard)
        res = mm(a, sd[:, :, lo:hi].reshape(tokens, hi - lo), 0, 0).astype(BF)
        for j in range(group):
            d = c * group + j
            pieces = [((slice(None), slice(0, hi - lo)), res[j * shard:(j + 1) * shard])]
            if outs:
                pieces.append(
                    ((slice(None), slice(hi - lo + inner, None)), gain[d * shard:(d + 1) * shard])
                )
            store(d, pieces)
    if outs:
        half = inner // width
        group = 8
        at = slice(hi - lo, hi - lo + inner)
        g = sg[...].reshape(tokens, feat)
        for c in range(width // group):
            o = so[:, :, c * group * half:(c + 1) * group * half].reshape(tokens, group * half)
            res = mm(o, g, 0, 0).astype(BF)
            for j in range(group):
                rows_of = res[j * half:(j + 1) * half]
                store(c * group + j, [
                    ((slice(0, half), at), rows_of[:, :inner]),
                    ((slice(half, 2 * half), at), rows_of[:, inner:]),
                ])


SMEM = pl.BlockSpec(memory_space=pltpu.SMEM)
VMEM = pl.BlockSpec(memory_space=pltpu.VMEM)


def call(body, ins, states, shapes, out_shape, flops, name):
    count = len(ins)
    got = pl.pallas_call(
        body,
        out_shape=list(shapes) + [out_shape],
        in_specs=[SMEM] * 2 + [VMEM] * (count - 2 + len(states)),
        out_specs=[VMEM] * (len(shapes) + 1),
        input_output_aliases={count + i: i for i in range(len(states))},
        compiler_params=pltpu.CompilerParams(vmem_limit_bytes=LIMIT),
        cost_estimate=pl.CostEstimate(flops=flops, bytes_accessed=12 * 1024 * 1024, transcendentals=0),
        name=name,
    )(*ins, *states)
    return got[-1], list(got[:-1])


def hops(step, last):
    runs = [(0, 1), (0, 3), (0, 3), (1, 5), (1, 5), (3, 6)] + [(4, 7)] * 3
    low, high = runs[min(step // 2, len(runs) - 1)]
    return range(low, min(high, last))


def spread_sum(value):
    for masks in ([1], [2, 4, 6], [8], [64], [16, 32, 48]):
        got = [
            lax.ppermute(value, ("section", "dp"), [(i, i ^ mask) for i in range(128)])
            for mask in masks
        ]
        for other in got:
            value = value + other
    return value


def swap(value, mask):
    return lax.ppermute(value, "dp", [(i, i ^ mask) for i in range(16)])


def scatter_sum(keep, send, order):
    total = keep.astype(F32) + swap(send, 1).astype(F32)
    for mask in order:
        half = total.shape[0] // 2
        total = total[:half] + swap(total[half:].astype(BF), mask).astype(F32)
    return total[0]


def local(hidden_in, segment_ids, cotangent, in_proj, out_proj, norm_gains):
    section = lax.axis_index("section")
    sections = lax.axis_size("section")
    width = lax.axis_size("dp")
    last = sections - 1
    seqs, length = segment_ids.shape
    feat = hidden_in.shape[1]
    shard = in_proj.shape[1]
    inner = out_proj.shape[1] * width
    micro = seqs * length // ROWS
    wo = jnp.concatenate([out_proj[0, :, :inner], out_proj[0, :, inner:]], axis=0)
    pack = lax.all_gather(jnp.concatenate([in_proj[0], wo], axis=1), "dp", axis=0)
    loss_scale = 1.0 / math.sqrt(width * hidden_in.shape[0])
    tokens = seqs * length
    ident = segment_ids.reshape(seqs, 2, ROWS)
    rows = lax.broadcasted_iota(jnp.int32, (ROWS, 2 * ROWS), 0)
    cols = lax.broadcasted_iota(jnp.int32, (ROWS, 2 * ROWS), 1)
    same = ident[:, :, :, None] == segment_ids[:, None, None, :]
    causal = jnp.stack([cols <= rows, cols <= rows + ROWS])
    bias = jnp.where(same & causal, 0.0, MASKED).astype(F32).reshape(micro, ROWS, length)
    sec = jnp.stack([section, lax.axis_index("dp")]).astype(jnp.int32)

    def shaped(*shape, dtype=BF):
        return jax.ShapeDtypeStruct(shape, dtype)

    f_shapes = [
        shaped(micro, ROWS, feat),
        shaped(micro, ROWS, feat),
        shaped(tokens, 3 * inner),
        shaped(micro, ROWS, inner),
        shaped(micro, ROWS, HEAD, dtype=F32),
    ]
    b_shapes = [
        shaped(micro, ROWS, feat),
        shaped(micro, ROWS, 3 * inner),
        shaped(micro, 8, feat, dtype=F32),
        shaped(ROWS, 2 * inner, dtype=F32),
    ]
    moved = shaped(ROWS, feat)
    per_row = 2 * feat * 4 * inner
    first = 2 * last + 1
    end = first + 2 * last + micro
    f_state, b_state = [], []
    f_recv, b_recv = {}, {}
    for cycle in range(end):
        on = [s for s in range(sections) if 0 <= cycle - 2 * s < micro]
        if on:
            out, f_state = call(
                functools.partial(forward_kernel, cycle % 2, micro, last, cycle in f_recv),
                [sec, np.full((1,), cycle, np.int32), hidden_in, bias, norm_gains, pack]
                + ([f_recv[cycle]] if cycle in f_recv else []),
                f_state, f_shapes, moved, ROWS * per_row, "fwd_half",
            )
            if on != [last]:
                pairs = [(s, s + 1) for s in hops(cycle, last)]
                f_recv[cycle + 2] = lax.ppermute(out, "section", pairs)
        on = [s for s in range(sections) if 0 <= cycle - first - 2 * (last - s) < micro]
        if on:
            sh, _, sq, _, sl = f_state
            out, b_state = call(
                functools.partial(
                    backward_kernel, (cycle - first) % 2 == 0, micro, last, loss_scale, cycle in b_recv
                ),
                [sec, np.full((1,), cycle - first, np.int32), cotangent, bias, norm_gains, pack, sh, sq, sl]
                + ([b_recv[cycle]] if cycle in b_recv else []),
                b_state, b_shapes, moved, 2 * ROWS * per_row, "bwd_half",
            )
            if on != [0]:
                pairs = [(last - s, last - s - 1) for s in hops(cycle - first, last)]
                b_recv[cycle + 2] = lax.ppermute(out, "section", pairs)
    _, sa, _, so, _ = f_state
    sg, sd, sn, _ = b_state
    third = 4 * inner // 3
    parts = []
    for index, order in enumerate(((2, 6, 8), (6, 8, 2), (8, 2, 6))):
        outs = index == 2
        cut = (index * third, min((index + 1) * third, 3 * inner))
        block = shaped(width // 2, shard, third + (HEAD if outs else 0))
        keep, send = pl.pallas_call(
            functools.partial(gradient_kernel, order, cut, outs),
            out_shape=[block, block],
            in_specs=[SMEM] + [VMEM] * 5,
            out_specs=[VMEM] * 2,
            compiler_params=pltpu.CompilerParams(vmem_limit_bytes=LIMIT),
            cost_estimate=pl.CostEstimate(
                flops=2 * tokens * feat * third, bytes_accessed=12 * 1024 * 1024, transcendentals=0
            ),
            name="gradient",
        )(sec, sa, sd, so, sg, sn)
        parts.append((keep, send, order))
    parts = [scatter_sum(*part) for part in parts]
    rest = parts[2]
    edge = 3 * inner - 2 * third
    half = out_proj.shape[1]
    in_sum = jnp.concatenate([parts[0], parts[1], rest[:, :edge]], axis=1)
    out_sum = jnp.concatenate([rest[:half, edge:third], rest[half:, edge:third]], axis=1)
    gain_sum = rest[:, third]
    squares = sum(jnp.sum(p * p) for p in (parts[0], parts[1], rest[:, :third], gain_sum))
    grand_total = spread_sum(jnp.full((8, HEAD), squares, F32))[0, 0]
    count = float(sections * width * (in_sum.size + out_sum.size + gain_sum.size))
    return (in_sum[None], out_sum[None], gain_sum[None], jnp.sqrt(grand_total / count))


def solution(mesh):
    placed = (
        P("dp", None),
        P("dp", None),
        P("dp", None),
        P("section", "dp", None),
        P("section", "dp", None),
        P("section", None),
    )
    return jax.shard_map(
        local,
        mesh=mesh,
        in_specs=placed,
        out_specs=(P("section", "dp", None), P("section", "dp", None), P("section", "dp"), P()),
        check_vma=False,
    )
```

```python
import functools
import math

import jax
import jax.numpy as jnp
from jax import lax
from jax.experimental import pallas as pl
from jax.experimental.pallas import tpu as pltpu
from jax.sharding import PartitionSpec as P

HEAD = 128
ROWS = 128
EPS = 1e-05
MASKED = -1e30
LIMIT = 8 * 1024 * 1024
BF = jnp.bfloat16
F32 = jnp.float32


def mm(left, right, lc=1, rc=0):
    return lax.dot_general(left, right, (((lc,), (rc,)), ((), ())), preferred_element_type=F32)


def unit(h):
    r = lax.rsqrt(jnp.mean(h * h, axis=-1, keepdims=True) + EPS)
    return r, h * r


def w_in(pack, k, inner):
    return pack[:, :, k * inner:(k + 1) * inner].reshape(-1, inner)


def w_out(pack, part, inner):
    half = pack.shape[1] // 2
    return pack[:, part * half:(part + 1) * half, 3 * inner:].reshape(-1, inner)


def forward_kernel(cycle, micro, last, received, sec, hid, bias, gains, pack, *refs):
    (sh, sa, sq, so, sl, out) = refs[-6:]
    inner = so.shape[2]
    heads = inner // HEAD
    odd = cycle % 2
    span = (1 + odd) * ROWS
    section = sec[0]
    m = cycle - 2 * section

    @pl.when((m >= 0) & (m < micro))
    def _():
        own = pl.multiple_of(m * ROWS, ROWS)
        base = pl.multiple_of(own - odd * ROWS, ROWS)

        @pl.when(section == 0)
        def _():
            sh[m] = hid[pl.ds(own, ROWS)]

        if received:
            @pl.when(section != 0)
            def _():
                sh[m] = refs[0][...]

        _, u = unit(sh[m].astype(F32))
        a = (u * gains[...]).astype(BF)
        sa[m] = a
        for k in range(3):
            sq[pl.ds(own, ROWS), k * inner:(k + 1) * inner] = mm(a, w_in(pack, k, inner)).astype(BF)
        mask = bias[m, :, :span]
        scores = []
        for e in range(heads):
            lo, hi = e * HEAD, (e + 1) * HEAD
            q = sq[pl.ds(own, ROWS), lo:hi]
            k = sq[pl.ds(base, span), inner + lo:inner + hi]
            scores.append(mm(q, k, 1, 1) * HEAD ** (-0.5) + mask)
        tops = [jnp.max(s, axis=-1, keepdims=True) for s in scores]
        xs = [jnp.exp(s - top) for s, top in zip(scores, tops)]
        totals = [jnp.sum(x, axis=-1, keepdims=True) for x in xs]
        lane = lax.broadcasted_iota(jnp.int32, (ROWS, HEAD), 1)
        lse = jnp.zeros((ROWS, HEAD), F32)
        for e in range(heads):
            lo, hi = e * HEAD, (e + 1) * HEAD
            v = sq[pl.ds(base, span), 2 * inner + lo:2 * inner + hi]
            so[m, :, lo:hi] = (mm(xs[e].astype(BF), v) * (1.0 / totals[e])).astype(BF)
            lse = jnp.where(lane == e, tops[e] + jnp.log(totals[e]), lse)
        sl[m] = lse

        @pl.when(section != last)
        def _():
            o = so[m]
            for part in range(2):
                cols = slice(part * inner, (part + 1) * inner)
                out[:, cols] = (
                    sh[m, :, cols].astype(F32) + mm(o, w_out(pack, part, inner))
                ).astype(BF)


def backward_kernel(cycle, micro, last, loss_scale, received, sec, cot, bias, gains, pack, sh, sq, sl, *refs):
    (sg, sd, sn, sp, out) = refs[-5:]
    inner = sd.shape[2] // 3
    feat = sh.shape[2]
    heads = inner // HEAD
    late = cycle % 2 == 0
    span = 2 * ROWS if late else ROWS
    section = sec[0]
    d = cycle - 2 * (last - section)
    n = jnp.where(d < 2, d, d - 2)

    @pl.when((d >= 0) & (n < micro) & (d // 2 != 1))
    def _():
        m = n + 1 if late else n - 1
        own = pl.multiple_of(m * ROWS, ROWS)
        base = pl.multiple_of(own + ROWS - span, ROWS)

        @pl.when(section == last)
        def _():
            sg[m] = (cot[pl.ds(own, ROWS)].astype(F32) * loss_scale).astype(BF)

        if received:
            @pl.when(section != last)
            def _():
                sg[m] = refs[0][...]

        g = sg[m]
        do_all = (
            mm(g[:, :inner], w_out(pack, 0, inner), 1, 1)
            + mm(g[:, inner:], w_out(pack, 1, inner), 1, 1)
        ).astype(BF)
        mask = bias[m, :, :span]
        lse = sl[m]
        scale = HEAD ** (-0.5)
        cut = [slice(e * HEAD, (e + 1) * HEAD) for e in range(heads)]
        qs = [sq[pl.ds(own, ROWS), e * HEAD:(e + 1) * HEAD] for e in range(heads)]
        ks = [sq[pl.ds(base, span), inner + e * HEAD:inner + (e + 1) * HEAD] for e in range(heads)]
        vs = [sq[pl.ds(base, span), 2 * inner + e * HEAD:2 * inner + (e + 1) * HEAD] for e in range(heads)]
        dos = [do_all[:, c] for c in cut]
        ps = [jnp.exp(mm(qs[e], ks[e], 1, 1) * scale + mask - lse[:, e:e + 1]) for e in range(heads)]
        dps = [mm(dos[e], vs[e], 1, 1) for e in range(heads)]
        insides = [jnp.sum(dp * p, axis=-1, keepdims=True) for dp, p in zip(dps, ps)]
        dss = [(p * (dp - i) * scale).astype(BF) for p, dp, i in zip(ps, dps, insides)]
        for e in range(heads):
            lo, hi = e * HEAD, (e + 1) * HEAD
            sd[m, :, lo:hi] = mm(dss[e], ks[e]).astype(BF)
            dk = mm(dss[e], qs[e], 0, 0)
            dv = mm(ps[e].astype(BF), dos[e], 0, 0)
            for at, value in ((0, dk), (inner, dv)):
                if late:
                    sp[:, at + lo:at + hi] = value[:ROWS]
                    value = value[ROWS:]
                else:
                    value = value + sp[:, at + lo:at + hi]
                sd[m, :, inner + at + lo:inner + at + hi] = value.astype(BF)
        r, u = unit(sh[m].astype(F32))
        da = None
        for k in range(3):
            term = mm(sd[m, :, k * inner:(k + 1) * inner], w_in(pack, k, inner), 1, 1)
            da = term if da is None else da + term
        sn[m] = jnp.sum((da * u).reshape(ROWS // 8, 8, feat), axis=0)
        e = da * gains[...]
        mean = jnp.mean(e * u, axis=-1, keepdims=True)
        out[...] = (sg[m].astype(F32) + r * (e - u * mean)).astype(BF)


def place(order, rel):
    low, high, y = rel % 2, (rel // 2) % 2, rel // 4
    bit = {2: (low + high) % 2, 6: high, 8: y}
    return 4 * bit[order[0]] + 2 * bit[order[1]] + bit[order[2]]


def gradient_kernel(order, cut, outs, me, sa, sd, so, sg, sn, keep, send):
    micro, rows, feat = sa.shape
    tokens = micro * rows
    inner = so.shape[2]
    width, shard = 2 * keep.shape[0], keep.shape[1]
    lo, hi = cut
    mine = me[1]

    def store(d, pieces):
        low = (d + mine) % 2
        x = (d // 2) % 4
        my_x = (mine // 2) % 4
        first = (x + my_x) % 2
        second = (x // 2 + my_x // 2) % 2
        y = (d // 8 + mine // 8) % 2
        slot = place(order, first + 2 * second + 4 * y)
        for ref, want in ((keep, 0), (send, 1)):
            @pl.when(low == want)
            def _():
                for where, value in pieces:
                    ref[slot, where[0], where[1]] = value

    if outs:
        total = jnp.sum(sn[...], axis=(0, 1)).reshape(1, feat)
        gain = jnp.concatenate(
            [
                jnp.broadcast_to(total[:, c * HEAD:(c + 1) * HEAD], (HEAD, HEAD)).T
                for c in range(feat // HEAD)
            ],
            axis=0,
        ).astype(BF)
    group = 4
    for c in range(width // group):
        a = sa[:, :, c * group * shard:(c + 1) * group * shard].reshape(tokens, group * shard)
        res = mm(a, sd[:, :, lo:hi].reshape(tokens, hi - lo), 0, 0).astype(BF)
        for j in range(group):
            d = c * group + j
            pieces = [((slice(None), slice(0, hi - lo)), res[j * shard:(j + 1) * shard])]
            if outs:
                pieces.append(
                    ((slice(None), slice(hi - lo + inner, None)), gain[d * shard:(d + 1) * shard])
                )
            store(d, pieces)
    if outs:
        half = inner // width
        group = 8
        at = slice(hi - lo, hi - lo + inner)
        g = sg[...].reshape(tokens, feat)
        for c in range(width // group):
            o = so[:, :, c * group * half:(c + 1) * group * half].reshape(tokens, group * half)
            res = mm(o, g, 0, 0).astype(BF)
            for j in range(group):
                rows_of = res[j * half:(j + 1) * half]
                store(c * group + j, [
                    ((slice(0, half), at), rows_of[:, :inner]),
                    ((slice(half, 2 * half), at), rows_of[:, inner:]),
                ])


SMEM = pl.BlockSpec(memory_space=pltpu.SMEM)
VMEM = pl.BlockSpec(memory_space=pltpu.VMEM)


def call(body, ins, states, shapes, out_shape, flops, name):
    count = len(ins)
    got = pl.pallas_call(
        body,
        out_shape=list(shapes) + [out_shape],
        in_specs=[SMEM] + [VMEM] * (count - 1 + len(states)),
        out_specs=[VMEM] * (len(shapes) + 1),
        input_output_aliases={count + i: i for i in range(len(states))},
        compiler_params=pltpu.CompilerParams(vmem_limit_bytes=LIMIT),
        cost_estimate=pl.CostEstimate(flops=flops, bytes_accessed=12 * 1024 * 1024, transcendentals=0),
        name=name,
    )(*ins, *states)
    return got[-1], list(got[:-1])


F_HOPS = ((0,), (0, 1, 2), (0, 1, 2), (1, 2, 3, 4), (1, 2, 3, 4), (3, 4, 5, 6))
B_HOPS = ((0, 2), (1, 2, 4), (0, 2), (0, 1, 3), (1, 2, 4), (2, 3, 5), (3, 4, 6), (4, 5), (5, 6))


def hops(table, step):
    return table[min(step // 2, len(table) - 1)]


def order_of_steps(micro, last):
    turn = 2 * last
    steps = [("f", i) for i in range(turn + 2)]
    steps += [("b", 0), ("b", 1), ("b", 2), ("f", turn + 2), ("b", 3), ("f", turn + 3), ("b", 4), ("b", 5)]
    steps += [("f", i) for i in range(turn + 4, turn + micro)]
    steps += [("b", i) for i in range(6, turn + micro + 2)]
    return steps


def spread_sum(value):
    for masks in ([1], [2, 4, 6], [8], [64], [16, 32, 48]):
        got = [
            lax.ppermute(value, ("section", "dp"), [(i, i ^ mask) for i in range(128)])
            for mask in masks
        ]
        for other in got:
            value = value + other
    return value


def swap(value, mask):
    return lax.ppermute(value, "dp", [(i, i ^ mask) for i in range(16)])


def scatter_sum(keep, send, order):
    total = keep.astype(F32) + swap(send, 1).astype(F32)
    for mask in order:
        half = total.shape[0] // 2
        total = total[:half] + swap(total[half:].astype(BF), mask).astype(F32)
    return total[0]


def local(hidden_in, segment_ids, cotangent, in_proj, out_proj, norm_gains):
    section = lax.axis_index("section")
    sections = lax.axis_size("section")
    width = lax.axis_size("dp")
    last = sections - 1
    seqs, length = segment_ids.shape
    feat = hidden_in.shape[1]
    shard = in_proj.shape[1]
    inner = out_proj.shape[1] * width
    micro = seqs * length // ROWS
    wo = jnp.concatenate([out_proj[0, :, :inner], out_proj[0, :, inner:]], axis=0)
    pack = lax.all_gather(jnp.concatenate([in_proj[0], wo], axis=1), "dp", axis=0)
    loss_scale = 1.0 / math.sqrt(width * hidden_in.shape[0])
    tokens = seqs * length
    ident = segment_ids.reshape(seqs, 2, ROWS)
    rows = lax.broadcasted_iota(jnp.int32, (ROWS, 2 * ROWS), 0)
    cols = lax.broadcasted_iota(jnp.int32, (ROWS, 2 * ROWS), 1)
    same = ident[:, :, :, None] == segment_ids[:, None, None, :]
    causal = jnp.stack([cols <= rows, cols <= rows + ROWS])
    bias = jnp.where(same & causal, 0.0, MASKED).astype(F32).reshape(micro, ROWS, length)
    sec = jnp.stack([section, lax.axis_index("dp")]).astype(jnp.int32)

    def shaped(*shape, dtype=BF):
        return jax.ShapeDtypeStruct(shape, dtype)

    f_shapes = [
        shaped(micro, ROWS, feat),
        shaped(micro, ROWS, feat),
        shaped(tokens, 3 * inner),
        shaped(micro, ROWS, inner),
        shaped(micro, ROWS, HEAD, dtype=F32),
    ]
    b_shapes = [
        shaped(micro, ROWS, feat),
        shaped(micro, ROWS, 3 * inner),
        shaped(micro, 8, feat, dtype=F32),
        shaped(ROWS, 2 * inner, dtype=F32),
    ]
    moved = shaped(ROWS, feat)
    per_row = 2 * feat * 4 * inner
    f_state, b_state = [], []
    f_recv, b_recv = {}, {}
    for kind, step in order_of_steps(micro, last):
        if kind == "f":
            out, f_state = call(
                functools.partial(forward_kernel, step, micro, last, step in f_recv),
                [sec, hidden_in, bias, norm_gains, pack] + ([f_recv[step]] if step in f_recv else []),
                f_state, f_shapes, moved, ROWS * per_row, "fwd_half",
            )
            if step < 2 * last - 2 + micro:
                pairs = [(h, h + 1) for h in hops(F_HOPS, step)]
                f_recv[step + 2] = lax.ppermute(out, "section", pairs)
        else:
            sh, _, sq, _, sl = f_state
            out, b_state = call(
                functools.partial(backward_kernel, step, micro, last, loss_scale, step in b_recv),
                [sec, cotangent, bias, norm_gains, pack, sh, sq, sl]
                + ([b_recv[step]] if step in b_recv else []),
                b_state, b_shapes, moved, 2 * ROWS * per_row, "bwd_half",
            )
            if step < 2 * last + micro:
                pairs = [(last - h, last - h - 1) for h in hops(B_HOPS, step)]
                b_recv[step + 2] = lax.ppermute(out, "section", pairs)
    _, sa, _, so, _ = f_state
    sg, sd, sn, _ = b_state
    third = 4 * inner // 3
    parts = []
    for index, order in enumerate(((2, 6, 8), (6, 8, 2), (8, 2, 6))):
        outs = index == 2
        cut = (index * third, min((index + 1) * third, 3 * inner))
        block = shaped(width // 2, shard, third + (HEAD if outs else 0))
        keep, send = pl.pallas_call(
            functools.partial(gradient_kernel, order, cut, outs),
            out_shape=[block, block],
            in_specs=[SMEM] + [VMEM] * 5,
            out_specs=[VMEM] * 2,
            compiler_params=pltpu.CompilerParams(vmem_limit_bytes=LIMIT),
            cost_estimate=pl.CostEstimate(
                flops=2 * tokens * feat * third, bytes_accessed=12 * 1024 * 1024, transcendentals=0
            ),
            name="gradient",
        )(sec, sa, sd, so, sg, sn)
        parts.append((keep, send, order))
    parts = [scatter_sum(*part) for part in parts]
    rest = parts[2]
    edge = 3 * inner - 2 * third
    half = out_proj.shape[1]
    in_sum = jnp.concatenate([parts[0], parts[1], rest[:, :edge]], axis=1)
    out_sum = jnp.concatenate([rest[:half, edge:third], rest[half:, edge:third]], axis=1)
    gain_sum = rest[:, third]
    squares = sum(jnp.sum(p * p) for p in (parts[0], parts[1], rest[:, :third], gain_sum))
    grand_total = spread_sum(jnp.full((8, HEAD), squares, F32))[0, 0]
    count = float(sections * width * (in_sum.size + out_sum.size + gain_sum.size))
    return (in_sum[None], out_sum[None], gain_sum[None], jnp.sqrt(grand_total / count))


def solution(mesh):
    placed = (
        P("dp", None),
        P("dp", None),
        P("dp", None),
        P("section", "dp", None),
        P("section", "dp", None),
        P("section", None),
    )
    return jax.shard_map(
        local,
        mesh=mesh,
        in_specs=placed,
        out_specs=(P("section", "dp", None), P("section", "dp", None), P("section", "dp"), P()),
        check_vma=False,
    )
```

```python
import functools
import math

import jax
import jax.numpy as jnp
from jax import lax
from jax.experimental import pallas as pl
from jax.experimental.pallas import tpu as pltpu
from jax.sharding import PartitionSpec as P

HEAD = 128
ROWS = 128
EPS = 1e-05
MASKED = -1e30
LIMIT = 8 * 1024 * 1024
BF = jnp.bfloat16
F32 = jnp.float32


def mm(left, right, lc=1, rc=0):
    return lax.dot_general(left, right, (((lc,), (rc,)), ((), ())), preferred_element_type=F32)


def unit(h):
    r = lax.rsqrt(jnp.mean(h * h, axis=-1, keepdims=True) + EPS)
    return r, h * r


def w_in(pack, k, inner):
    return pack[:, :, k * inner:(k + 1) * inner].reshape(-1, inner)


def w_out(pack, part, inner):
    half = pack.shape[1] // 2
    return pack[:, part * half:(part + 1) * half, 3 * inner:].reshape(-1, inner)


def forward_kernel(cycle, micro, last, received, sec, me, hid, bias, gains, pack, *refs):
    (sh, sa, sq, so, sl, out) = refs[-6:]
    inner = so.shape[2]
    heads = inner // HEAD
    odd = cycle % 2
    span = (1 + odd) * ROWS
    section = sec[0]
    m = cycle - 2 * section

    @pl.when((m >= 0) & (m < micro))
    def _():
        own = pl.multiple_of(m * ROWS, ROWS)
        base = pl.multiple_of(own - odd * ROWS, ROWS)

        @pl.when(section == 0)
        def _():
            sh[m] = hid[pl.ds(own, ROWS)]

        if received:
            @pl.when(section != 0)
            def _():
                sh[m] = refs[0][...]

        _, u = unit(sh[m].astype(F32))
        a = (u * gains[...]).astype(BF)
        sa[m] = a
        for k in range(3):
            sq[pl.ds(own, ROWS), k * inner:(k + 1) * inner] = mm(a, w_in(pack, k, inner)).astype(BF)
        mask = bias[m, :, :span]
        scores = []
        for e in range(heads):
            lo, hi = e * HEAD, (e + 1) * HEAD
            q = sq[pl.ds(own, ROWS), lo:hi]
            k = sq[pl.ds(base, span), inner + lo:inner + hi]
            scores.append(mm(q, k, 1, 1) * HEAD ** (-0.5) + mask)
        tops = [jnp.max(s, axis=-1, keepdims=True) for s in scores]
        xs = [jnp.exp(s - top) for s, top in zip(scores, tops)]
        totals = [jnp.sum(x, axis=-1, keepdims=True) for x in xs]
        lane = lax.broadcasted_iota(jnp.int32, (ROWS, HEAD), 1)
        lse = jnp.zeros((ROWS, HEAD), F32)
        for e in range(heads):
            lo, hi = e * HEAD, (e + 1) * HEAD
            v = sq[pl.ds(base, span), 2 * inner + lo:2 * inner + hi]
            so[m, :, lo:hi] = (mm(xs[e].astype(BF), v) * (1.0 / totals[e])).astype(BF)
            lse = jnp.where(lane == e, tops[e] + jnp.log(totals[e]), lse)
        sl[m] = lse

        @pl.when(section != last)
        def _():
            o = so[m]
            for part in range(2):
                cols = slice(part * inner, (part + 1) * inner)
                out[:, cols] = (
                    sh[m, :, cols].astype(F32) + mm(o, w_out(pack, part, inner))
                ).astype(BF)


def backward_kernel(cycle, micro, last, loss_scale, received, sec, me, cot, bias, gains, pack, sh, sq, sl, *refs):
    (sg, sd, sn, sp, out) = refs[-5:]
    inner = sd.shape[2] // 3
    feat = sh.shape[2]
    heads = inner // HEAD
    late = cycle % 2 == 0
    span = 2 * ROWS if late else ROWS
    section = sec[0]
    n = cycle - 2 * (last - section)

    @pl.when((n >= 0) & (n < micro))
    def _():
        m = n + 1 if late else n - 1
        own = pl.multiple_of(m * ROWS, ROWS)
        base = pl.multiple_of(own + ROWS - span, ROWS)

        @pl.when(section == last)
        def _():
            sg[m] = (cot[pl.ds(own, ROWS)].astype(F32) * loss_scale).astype(BF)

        if received:
            @pl.when(section != last)
            def _():
                sg[m] = refs[0][...]

        g = sg[m]
        do_all = (
            mm(g[:, :inner], w_out(pack, 0, inner), 1, 1)
            + mm(g[:, inner:], w_out(pack, 1, inner), 1, 1)
        ).astype(BF)
        mask = bias[m, :, :span]
        lse = sl[m]
        scale = HEAD ** (-0.5)
        cut = [slice(e * HEAD, (e + 1) * HEAD) for e in range(heads)]
        qs = [sq[pl.ds(own, ROWS), e * HEAD:(e + 1) * HEAD] for e in range(heads)]
        ks = [sq[pl.ds(base, span), inner + e * HEAD:inner + (e + 1) * HEAD] for e in range(heads)]
        vs = [sq[pl.ds(base, span), 2 * inner + e * HEAD:2 * inner + (e + 1) * HEAD] for e in range(heads)]
        dos = [do_all[:, c] for c in cut]
        ps = [jnp.exp(mm(qs[e], ks[e], 1, 1) * scale + mask - lse[:, e:e + 1]) for e in range(heads)]
        dps = [mm(dos[e], vs[e], 1, 1) for e in range(heads)]
        insides = [jnp.sum(dp * p, axis=-1, keepdims=True) for dp, p in zip(dps, ps)]
        dss = [(p * (dp - i) * scale).astype(BF) for p, dp, i in zip(ps, dps, insides)]
        for e in range(heads):
            lo, hi = e * HEAD, (e + 1) * HEAD
            sd[m, :, lo:hi] = mm(dss[e], ks[e]).astype(BF)
            dk = mm(dss[e], qs[e], 0, 0)
            dv = mm(ps[e].astype(BF), dos[e], 0, 0)
            for at, value in ((0, dk), (inner, dv)):
                if late:
                    sp[:, at + lo:at + hi] = value[:ROWS]
                    value = value[ROWS:]
                else:
                    value = value + sp[:, at + lo:at + hi]
                sd[m, :, inner + at + lo:inner + at + hi] = value.astype(BF)
        r, u = unit(sh[m].astype(F32))
        da = None
        for k in range(3):
            term = mm(sd[m, :, k * inner:(k + 1) * inner], w_in(pack, k, inner), 1, 1)
            da = term if da is None else da + term
        sn[m] = jnp.sum((da * u).reshape(ROWS // 8, 8, feat), axis=0)
        e = da * gains[...]
        mean = jnp.mean(e * u, axis=-1, keepdims=True)
        out[...] = (sg[m].astype(F32) + r * (e - u * mean)).astype(BF)


def place(order, rel):
    low, high, y = rel % 2, (rel // 2) % 2, rel // 4
    bit = {2: (low + high) % 2, 6: high, 8: y}
    return 4 * bit[order[0]] + 2 * bit[order[1]] + bit[order[2]]


def gradient_kernel(order, cut, outs, me, sa, sd, so, sg, sn, keep, send):
    micro, rows, feat = sa.shape
    tokens = micro * rows
    inner = so.shape[2]
    width, shard = 2 * keep.shape[0], keep.shape[1]
    lo, hi = cut
    mine = me[0]

    def store(d, pieces):
        low = (d + mine) % 2
        x = (d // 2) % 4
        my_x = (mine // 2) % 4
        first = (x + my_x) % 2
        second = (x // 2 + my_x // 2) % 2
        y = (d // 8 + mine // 8) % 2
        slot = place(order, first + 2 * second + 4 * y)
        for ref, want in ((keep, 0), (send, 1)):
            @pl.when(low == want)
            def _():
                for where, value in pieces:
                    ref[slot, where[0], where[1]] = value

    if outs:
        total = jnp.sum(sn[...], axis=(0, 1)).reshape(1, feat)
        gain = jnp.concatenate(
            [
                jnp.broadcast_to(total[:, c * HEAD:(c + 1) * HEAD], (HEAD, HEAD)).T
                for c in range(feat // HEAD)
            ],
            axis=0,
        ).astype(BF)
    group = 4
    for c in range(width // group):
        a = sa[:, :, c * group * shard:(c + 1) * group * shard].reshape(tokens, group * shard)
        res = mm(a, sd[:, :, lo:hi].reshape(tokens, hi - lo), 0, 0).astype(BF)
        for j in range(group):
            d = c * group + j
            pieces = [((slice(None), slice(0, hi - lo)), res[j * shard:(j + 1) * shard])]
            if outs:
                pieces.append(
                    ((slice(None), slice(hi - lo + inner, None)), gain[d * shard:(d + 1) * shard])
                )
            store(d, pieces)
    if outs:
        half = inner // width
        group = 8
        at = slice(hi - lo, hi - lo + inner)
        g = sg[...].reshape(tokens, feat)
        for c in range(width // group):
            o = so[:, :, c * group * half:(c + 1) * group * half].reshape(tokens, group * half)
            res = mm(o, g, 0, 0).astype(BF)
            for j in range(group):
                rows_of = res[j * half:(j + 1) * half]
                store(c * group + j, [
                    ((slice(0, half), at), rows_of[:, :inner]),
                    ((slice(half, 2 * half), at), rows_of[:, inner:]),
                ])


SMEM = pl.BlockSpec(memory_space=pltpu.SMEM)
VMEM = pl.BlockSpec(memory_space=pltpu.VMEM)


def call(body, ins, states, shapes, out_shape, flops, name):
    count = len(ins)
    got = pl.pallas_call(
        body,
        out_shape=list(shapes) + [out_shape],
        in_specs=[SMEM] * 2 + [VMEM] * (count - 2 + len(states)),
        out_specs=[VMEM] * (len(shapes) + 1),
        input_output_aliases={count + i: i for i in range(len(states))},
        compiler_params=pltpu.CompilerParams(vmem_limit_bytes=LIMIT),
        cost_estimate=pl.CostEstimate(flops=flops, bytes_accessed=12 * 1024 * 1024, transcendentals=0),
        name=name,
    )(*ins, *states)
    return got[-1], list(got[:-1])


def hops(step, last):
    runs = [(0, 1), (0, 3), (0, 3), (1, 5), (1, 5), (3, 6)] + [(4, 7)] * 3
    low, high = runs[min(step // 2, len(runs) - 1)]
    return range(low, min(high, last))


def spread_sum(value):
    for masks in ([1], [2, 4, 6], [8], [64], [16, 32, 48]):
        got = [
            lax.ppermute(value, ("section", "dp"), [(i, i ^ mask) for i in range(128)])
            for mask in masks
        ]
        for other in got:
            value = value + other
    return value


def swap(value, mask):
    return lax.ppermute(value, "dp", [(i, i ^ mask) for i in range(16)])


def scatter_sum(keep, send, order):
    total = keep.astype(F32) + swap(send, 1).astype(F32)
    for mask in order:
        half = total.shape[0] // 2
        total = total[:half] + swap(total[half:].astype(BF), mask).astype(F32)
    return total[0]


def local(hidden_in, segment_ids, cotangent, in_proj, out_proj, norm_gains):
    section = lax.axis_index("section")
    sections = lax.axis_size("section")
    width = lax.axis_size("dp")
    last = sections - 1
    seqs, length = segment_ids.shape
    feat = hidden_in.shape[1]
    shard = in_proj.shape[1]
    inner = out_proj.shape[1] * width
    micro = seqs * length // ROWS
    wo = jnp.concatenate([out_proj[0, :, :inner], out_proj[0, :, inner:]], axis=0)
    pack = lax.all_gather(jnp.concatenate([in_proj[0], wo], axis=1), "dp", axis=0)
    loss_scale = 1.0 / math.sqrt(width * hidden_in.shape[0])
    tokens = seqs * length
    ident = segment_ids.reshape(seqs, 2, ROWS)
    rows = lax.broadcasted_iota(jnp.int32, (ROWS, 2 * ROWS), 0)
    cols = lax.broadcasted_iota(jnp.int32, (ROWS, 2 * ROWS), 1)
    same = ident[:, :, :, None] == segment_ids[:, None, None, :]
    causal = jnp.stack([cols <= rows, cols <= rows + ROWS])
    bias = jnp.where(same & causal, 0.0, MASKED).astype(F32).reshape(micro, ROWS, length)
    sec = jnp.full((1,), section, jnp.int32)
    me = jnp.full((1,), lax.axis_index("dp"), jnp.int32)

    def shaped(*shape, dtype=BF):
        return jax.ShapeDtypeStruct(shape, dtype)

    f_shapes = [
        shaped(micro, ROWS, feat),
        shaped(micro, ROWS, feat),
        shaped(tokens, 3 * inner),
        shaped(micro, ROWS, inner),
        shaped(micro, ROWS, HEAD, dtype=F32),
    ]
    b_shapes = [
        shaped(micro, ROWS, feat),
        shaped(micro, ROWS, 3 * inner),
        shaped(micro, 8, feat, dtype=F32),
        shaped(ROWS, 2 * inner, dtype=F32),
    ]
    moved = shaped(ROWS, feat)
    per_row = 2 * feat * 4 * inner
    first = 2 * last + 1
    end = first + 2 * last + micro
    f_state, b_state = [], []
    f_recv, b_recv = {}, {}
    for cycle in range(end):
        on = [s for s in range(sections) if 0 <= cycle - 2 * s < micro]
        if on:
            out, f_state = call(
                functools.partial(forward_kernel, cycle, micro, last, cycle in f_recv),
                [sec, me, hidden_in, bias, norm_gains, pack]
                + ([f_recv[cycle]] if cycle in f_recv else []),
                f_state, f_shapes, moved, ROWS * per_row, "fwd_half",
            )
            if on != [last]:
                pairs = [(s, s + 1) for s in hops(cycle, last)]
                f_recv[cycle + 2] = lax.ppermute(out, "section", pairs)
        on = [s for s in range(sections) if 0 <= cycle - first - 2 * (last - s) < micro]
        if on:
            sh, _, sq, _, sl = f_state
            out, b_state = call(
                functools.partial(
                    backward_kernel, cycle - first, micro, last, loss_scale, cycle in b_recv
                ),
                [sec, me, cotangent, bias, norm_gains, pack, sh, sq, sl]
                + ([b_recv[cycle]] if cycle in b_recv else []),
                b_state, b_shapes, moved, 2 * ROWS * per_row, "bwd_half",
            )
            if on != [0]:
                pairs = [(last - s, last - s - 1) for s in hops(cycle - first, last)]
                b_recv[cycle + 2] = lax.ppermute(out, "section", pairs)
    _, sa, _, so, _ = f_state
    sg, sd, sn, _ = b_state
    third = 4 * inner // 3
    parts = []
    for index, order in enumerate(((2, 6, 8), (6, 8, 2), (8, 2, 6))):
        outs = index == 2
        cut = (index * third, min((index + 1) * third, 3 * inner))
        block = shaped(width // 2, shard, third + (HEAD if outs else 0))
        keep, send = pl.pallas_call(
            functools.partial(gradient_kernel, order, cut, outs),
            out_shape=[block, block],
            in_specs=[SMEM] + [VMEM] * 5,
            out_specs=[VMEM] * 2,
            compiler_params=pltpu.CompilerParams(vmem_limit_bytes=LIMIT),
            cost_estimate=pl.CostEstimate(
                flops=2 * tokens * feat * third, bytes_accessed=12 * 1024 * 1024, transcendentals=0
            ),
            name="gradient",
        )(me, sa, sd, so, sg, sn)
        parts.append((keep, send, order))
    parts = [scatter_sum(*part) for part in parts]
    rest = parts[2]
    edge = 3 * inner - 2 * third
    half = out_proj.shape[1]
    in_sum = jnp.concatenate([parts[0], parts[1], rest[:, :edge]], axis=1)
    out_sum = jnp.concatenate([rest[:half, edge:third], rest[half:, edge:third]], axis=1)
    gain_sum = rest[:, third]
    squares = sum(jnp.sum(p * p) for p in (parts[0], parts[1], rest[:, :third], gain_sum))
    grand_total = spread_sum(jnp.full((8, HEAD), squares, F32))[0, 0]
    count = float(sections * width * (in_sum.size + out_sum.size + gain_sum.size))
    return (in_sum[None], out_sum[None], gain_sum[None], jnp.sqrt(grand_total / count))


def solution(mesh):
    placed = (
        P("dp", None),
        P("dp", None),
        P("dp", None),
        P("section", "dp", None),
        P("section", "dp", None),
        P("section", None),
    )
    return jax.shard_map(
        local,
        mesh=mesh,
        in_specs=placed,
        out_specs=(P("section", "dp", None), P("section", "dp", None), P("section", "dp"), P()),
        check_vma=False,
    )
```

```python
import functools
import math

import jax
import jax.numpy as jnp
from jax import lax
from jax.experimental import pallas as pl
from jax.experimental.pallas import tpu as pltpu
from jax.sharding import PartitionSpec as P

HEAD = 128
ROWS = 128
EPS = 1e-05
MASKED = -1e30
LIMIT = 8 * 1024 * 1024
BF = jnp.bfloat16
F32 = jnp.float32


def mm(left, right, lc=1, rc=0):
    return lax.dot_general(left, right, (((lc,), (rc,)), ((), ())), preferred_element_type=F32)


def unit(h):
    r = lax.rsqrt(jnp.mean(h * h, axis=-1, keepdims=True) + EPS)
    return r, h * r


def w_in(pack, k, inner):
    return pack[:, :, k * inner:(k + 1) * inner].reshape(-1, inner)


def w_out(pack, part, inner):
    half = pack.shape[1] // 2
    return pack[:, part * half:(part + 1) * half, 3 * inner:].reshape(-1, inner)


def forward_kernel(cycle, micro, last, received, sec, me, hid, bias, gains, pack, *refs):
    (sh, sa, sq, so, sl, out) = refs[-6:]
    inner = so.shape[2]
    heads = inner // HEAD
    odd = cycle % 2
    span = (1 + odd) * ROWS
    section = sec[0]
    m = cycle - 2 * section

    def run():
        own = pl.multiple_of(m * ROWS, ROWS)
        base = pl.multiple_of(own - odd * ROWS, ROWS)

        @pl.when(section == 0)
        def _():
            sh[m] = hid[pl.ds(own, ROWS)]

        if received:
            @pl.when(section != 0)
            def _():
                sh[m] = refs[0][...]

        _, u = unit(sh[m].astype(F32))
        a = (u * gains[...]).astype(BF)
        sa[m] = a
        for k in range(3):
            sq[pl.ds(own, ROWS), k * inner:(k + 1) * inner] = mm(a, w_in(pack, k, inner)).astype(BF)
        mask = bias[m, :, :span]
        scores = []
        for e in range(heads):
            lo, hi = e * HEAD, (e + 1) * HEAD
            q = sq[pl.ds(own, ROWS), lo:hi]
            k = sq[pl.ds(base, span), inner + lo:inner + hi]
            scores.append(mm(q, k, 1, 1) * HEAD ** (-0.5) + mask)
        tops = [jnp.max(s, axis=-1, keepdims=True) for s in scores]
        xs = [jnp.exp(s - top) for s, top in zip(scores, tops)]
        totals = [jnp.sum(x, axis=-1, keepdims=True) for x in xs]
        lane = lax.broadcasted_iota(jnp.int32, (ROWS, HEAD), 1)
        lse = jnp.zeros((ROWS, HEAD), F32)
        for e in range(heads):
            lo, hi = e * HEAD, (e + 1) * HEAD
            v = sq[pl.ds(base, span), 2 * inner + lo:2 * inner + hi]
            so[m, :, lo:hi] = (mm(xs[e].astype(BF), v) * (1.0 / totals[e])).astype(BF)
            lse = jnp.where(lane == e, tops[e] + jnp.log(totals[e]), lse)
        sl[m] = lse

        @pl.when(section != last)
        def _():
            o = so[m]
            for part in range(2):
                cols = slice(part * inner, (part + 1) * inner)
                out[:, cols] = (
                    sh[m, :, cols].astype(F32) + mm(o, w_out(pack, part, inner))
                ).astype(BF)

    @pl.when((m >= 0) & (m < micro))
    def _():
        if cycle:
            run()
        else:
            pl.loop(0, 1 + 2 * (me[0] % 2))(lambda _: run())


def backward_kernel(cycle, micro, last, loss_scale, received, sec, me, cot, bias, gains, pack, sh, sq, sl, *refs):
    (sg, sd, sn, sp, out) = refs[-5:]
    inner = sd.shape[2] // 3
    feat = sh.shape[2]
    heads = inner // HEAD
    late = cycle % 2 == 0
    span = 2 * ROWS if late else ROWS
    section = sec[0]
    n = cycle - 2 * (last - section)

    @pl.when((n >= 0) & (n < micro))
    def _():
        m = n + 1 if late else n - 1
        own = pl.multiple_of(m * ROWS, ROWS)
        base = pl.multiple_of(own + ROWS - span, ROWS)

        @pl.when(section == last)
        def _():
            sg[m] = (cot[pl.ds(own, ROWS)].astype(F32) * loss_scale).astype(BF)

        if received:
            @pl.when(section != last)
            def _():
                sg[m] = refs[0][...]

        g = sg[m]
        do_all = (
            mm(g[:, :inner], w_out(pack, 0, inner), 1, 1)
            + mm(g[:, inner:], w_out(pack, 1, inner), 1, 1)
        ).astype(BF)
        mask = bias[m, :, :span]
        lse = sl[m]
        scale = HEAD ** (-0.5)
        cut = [slice(e * HEAD, (e + 1) * HEAD) for e in range(heads)]
        qs = [sq[pl.ds(own, ROWS), e * HEAD:(e + 1) * HEAD] for e in range(heads)]
        ks = [sq[pl.ds(base, span), inner + e * HEAD:inner + (e + 1) * HEAD] for e in range(heads)]
        vs = [sq[pl.ds(base, span), 2 * inner + e * HEAD:2 * inner + (e + 1) * HEAD] for e in range(heads)]
        dos = [do_all[:, c] for c in cut]
        ps = [jnp.exp(mm(qs[e], ks[e], 1, 1) * scale + mask - lse[:, e:e + 1]) for e in range(heads)]
        dps = [mm(dos[e], vs[e], 1, 1) for e in range(heads)]
        insides = [jnp.sum(dp * p, axis=-1, keepdims=True) for dp, p in zip(dps, ps)]
        dss = [(p * (dp - i) * scale).astype(BF) for p, dp, i in zip(ps, dps, insides)]
        for e in range(heads):
            lo, hi = e * HEAD, (e + 1) * HEAD
            sd[m, :, lo:hi] = mm(dss[e], ks[e]).astype(BF)
            dk = mm(dss[e], qs[e], 0, 0)
            dv = mm(ps[e].astype(BF), dos[e], 0, 0)
            for at, value in ((0, dk), (inner, dv)):
                if late:
                    sp[:, at + lo:at + hi] = value[:ROWS]
                    value = value[ROWS:]
                else:
                    value = value + sp[:, at + lo:at + hi]
                sd[m, :, inner + at + lo:inner + at + hi] = value.astype(BF)
        r, u = unit(sh[m].astype(F32))
        da = None
        for k in range(3):
            term = mm(sd[m, :, k * inner:(k + 1) * inner], w_in(pack, k, inner), 1, 1)
            da = term if da is None else da + term
        sn[m] = jnp.sum((da * u).reshape(ROWS // 8, 8, feat), axis=0)
        e = da * gains[...]
        mean = jnp.mean(e * u, axis=-1, keepdims=True)
        out[...] = (sg[m].astype(F32) + r * (e - u * mean)).astype(BF)


def place(order, rel):
    low, high, y = rel % 2, (rel // 2) % 2, rel // 4
    bit = {2: (low + high) % 2, 6: high, 8: y}
    return 4 * bit[order[0]] + 2 * bit[order[1]] + bit[order[2]]


def gradient_kernel(order, cut, outs, me, sa, sd, so, sg, sn, keep, send):
    micro, rows, feat = sa.shape
    tokens = micro * rows
    inner = so.shape[2]
    width, shard = 2 * keep.shape[0], keep.shape[1]
    lo, hi = cut
    mine = me[0]

    def store(d, pieces):
        low = (d + mine) % 2
        x = (d // 2) % 4
        my_x = (mine // 2) % 4
        first = (x + my_x) % 2
        second = (x // 2 + my_x // 2) % 2
        y = (d // 8 + mine // 8) % 2
        slot = place(order, first + 2 * second + 4 * y)
        for ref, want in ((keep, 0), (send, 1)):
            @pl.when(low == want)
            def _():
                for where, value in pieces:
                    ref[slot, where[0], where[1]] = value

    if outs:
        total = jnp.sum(sn[...], axis=(0, 1)).reshape(1, feat)
        gain = jnp.concatenate(
            [
                jnp.broadcast_to(total[:, c * HEAD:(c + 1) * HEAD], (HEAD, HEAD)).T
                for c in range(feat // HEAD)
            ],
            axis=0,
        ).astype(BF)
    group = 4
    for c in range(width // group):
        a = sa[:, :, c * group * shard:(c + 1) * group * shard].reshape(tokens, group * shard)
        res = mm(a, sd[:, :, lo:hi].reshape(tokens, hi - lo), 0, 0).astype(BF)
        for j in range(group):
            d = c * group + j
            pieces = [((slice(None), slice(0, hi - lo)), res[j * shard:(j + 1) * shard])]
            if outs:
                pieces.append(
                    ((slice(None), slice(hi - lo + inner, None)), gain[d * shard:(d + 1) * shard])
                )
            store(d, pieces)
    if outs:
        half = inner // width
        group = 8
        at = slice(hi - lo, hi - lo + inner)
        g = sg[...].reshape(tokens, feat)
        for c in range(width // group):
            o = so[:, :, c * group * half:(c + 1) * group * half].reshape(tokens, group * half)
            res = mm(o, g, 0, 0).astype(BF)
            for j in range(group):
                rows_of = res[j * half:(j + 1) * half]
                store(c * group + j, [
                    ((slice(0, half), at), rows_of[:, :inner]),
                    ((slice(half, 2 * half), at), rows_of[:, inner:]),
                ])


SMEM = pl.BlockSpec(memory_space=pltpu.SMEM)
VMEM = pl.BlockSpec(memory_space=pltpu.VMEM)


def call(body, ins, states, shapes, out_shape, flops, name):
    count = len(ins)
    got = pl.pallas_call(
        body,
        out_shape=list(shapes) + [out_shape],
        in_specs=[SMEM] * 2 + [VMEM] * (count - 2 + len(states)),
        out_specs=[VMEM] * (len(shapes) + 1),
        input_output_aliases={count + i: i for i in range(len(states))},
        compiler_params=pltpu.CompilerParams(vmem_limit_bytes=LIMIT),
        cost_estimate=pl.CostEstimate(flops=flops, bytes_accessed=12 * 1024 * 1024, transcendentals=0),
        name=name,
    )(*ins, *states)
    return got[-1], list(got[:-1])


def after(value, *others):
    def copy_kernel(src, *refs):
        refs[-1][...] = src[...]

    return pl.pallas_call(
        copy_kernel,
        out_shape=jax.ShapeDtypeStruct(value.shape, value.dtype),
        in_specs=[VMEM] + [pl.BlockSpec(memory_space=pl.ANY)] * len(others),
        out_specs=VMEM,
        compiler_params=pltpu.CompilerParams(vmem_limit_bytes=LIMIT),
        name="after",
    )(value, *others)


def hops(step, last):
    runs = [(0, 1), (0, 3), (0, 3), (1, 5), (1, 5), (3, 6)] + [(4, 7)] * 3
    low, high = runs[min(step // 2, len(runs) - 1)]
    return range(low, min(high, last))


def spread_sum(value):
    for masks in ([1], [2, 4, 6], [8], [64], [16, 32, 48]):
        got = [
            lax.ppermute(value, ("section", "dp"), [(i, i ^ mask) for i in range(128)])
            for mask in masks
        ]
        for other in got:
            value = value + other
    return value


def swap(value, mask):
    return lax.ppermute(value, "dp", [(i, i ^ mask) for i in range(16)])


def scatter_sum(keep, send, order):
    total = keep.astype(F32) + swap(send, 1).astype(F32)
    for mask in order:
        half = total.shape[0] // 2
        total = total[:half] + swap(total[half:].astype(BF), mask).astype(F32)
    return total[0]


def local(hidden_in, segment_ids, cotangent, in_proj, out_proj, norm_gains):
    section = lax.axis_index("section")
    sections = lax.axis_size("section")
    width = lax.axis_size("dp")
    last = sections - 1
    seqs, length = segment_ids.shape
    feat = hidden_in.shape[1]
    shard = in_proj.shape[1]
    inner = out_proj.shape[1] * width
    micro = seqs * length // ROWS
    wo = jnp.concatenate([out_proj[0, :, :inner], out_proj[0, :, inner:]], axis=0)
    pack = lax.all_gather(jnp.concatenate([in_proj[0], wo], axis=1), "dp", axis=0)
    loss_scale = 1.0 / math.sqrt(width * hidden_in.shape[0])
    tokens = seqs * length
    ident = segment_ids.reshape(seqs, 2, ROWS)
    rows = lax.broadcasted_iota(jnp.int32, (ROWS, 2 * ROWS), 0)
    cols = lax.broadcasted_iota(jnp.int32, (ROWS, 2 * ROWS), 1)
    same = ident[:, :, :, None] == segment_ids[:, None, None, :]
    causal = jnp.stack([cols <= rows, cols <= rows + ROWS])
    bias = jnp.where(same & causal, 0.0, MASKED).astype(F32).reshape(micro, ROWS, length)
    sec = jnp.full((1,), section, jnp.int32)
    me = jnp.full((1,), lax.axis_index("dp"), jnp.int32)

    def shaped(*shape, dtype=BF):
        return jax.ShapeDtypeStruct(shape, dtype)

    f_shapes = [
        shaped(micro, ROWS, feat),
        shaped(micro, ROWS, feat),
        shaped(tokens, 3 * inner),
        shaped(micro, ROWS, inner),
        shaped(micro, ROWS, HEAD, dtype=F32),
    ]
    b_shapes = [
        shaped(micro, ROWS, feat),
        shaped(micro, ROWS, 3 * inner),
        shaped(micro, 8, feat, dtype=F32),
        shaped(ROWS, 2 * inner, dtype=F32),
    ]
    moved = shaped(ROWS, feat)
    per_row = 2 * feat * 4 * inner
    first = 2 * last + 1
    end = first + 2 * last + micro
    f_state, b_state = [], []
    f_recv, b_recv = {}, {}
    for cycle in range(end):
        on = [s for s in range(sections) if 0 <= cycle - 2 * s < micro]
        if on:
            got = [f_recv[cycle]] if cycle in f_recv else []
            out, f_state = call(
                functools.partial(forward_kernel, cycle, micro, last, len(got)),
                [sec, me, hidden_in, bias, norm_gains, pack] + got,
                f_state, f_shapes, moved, ROWS * per_row, "fwd_half",
            )
            pairs = [(s, s + 1) for s in hops(cycle, last)]
            if cycle == 1:
                held = out
            elif on != [last]:
                if cycle == 2:
                    f_recv[3] = lax.ppermute(after(held, out), "section", [(0, 1)])
                f_recv[cycle + 2] = lax.ppermute(out, "section", pairs)
        if cycle == first:
            sh, _, sq, _, sl = f_state
            _, b_state = call(
                functools.partial(backward_kernel, -2, micro, last, loss_scale, False),
                [sec, me, cotangent, bias, norm_gains, pack, sh, sq, sl],
                [], b_shapes, moved, 2 * ROWS * per_row, "bwd_half",
            )
        on = [s for s in range(sections) if 0 <= cycle - first - 2 * (last - s) < micro]
        if on:
            sh, _, sq, _, sl = f_state
            out, b_state = call(
                functools.partial(
                    backward_kernel, cycle - first, micro, last, loss_scale, cycle in b_recv
                ),
                [sec, me, cotangent, bias, norm_gains, pack, sh, sq, sl]
                + ([b_recv[cycle]] if cycle in b_recv else []),
                b_state, b_shapes, moved, 2 * ROWS * per_row, "bwd_half",
            )
            if on != [0]:
                pairs = [(last - s, last - s - 1) for s in hops(cycle - first, last)]
                b_recv[cycle + 2] = lax.ppermute(out, "section", pairs)
    _, sa, _, so, _ = f_state
    sg, sd, sn, _ = b_state
    third = 4 * inner // 3
    parts = []
    for index, order in enumerate(((2, 6, 8), (6, 8, 2), (8, 2, 6))):
        outs = index == 2
        cut = (index * third, min((index + 1) * third, 3 * inner))
        block = shaped(width // 2, shard, third + (HEAD if outs else 0))
        keep, send = pl.pallas_call(
            functools.partial(gradient_kernel, order, cut, outs),
            out_shape=[block, block],
            in_specs=[SMEM] + [VMEM] * 5,
            out_specs=[VMEM] * 2,
            compiler_params=pltpu.CompilerParams(vmem_limit_bytes=LIMIT),
            cost_estimate=pl.CostEstimate(
                flops=2 * tokens * feat * third, bytes_accessed=12 * 1024 * 1024, transcendentals=0
            ),
            name="gradient",
        )(me, sa, sd, so, sg, sn)
        parts.append((keep, send, order))
    parts = [scatter_sum(*part) for part in parts]
    rest = parts[2]
    edge = 3 * inner - 2 * third
    half = out_proj.shape[1]
    in_sum = jnp.concatenate([parts[0], parts[1], rest[:, :edge]], axis=1)
    out_sum = jnp.concatenate([rest[:half, edge:third], rest[half:, edge:third]], axis=1)
    gain_sum = rest[:, third]
    squares = sum(jnp.sum(p * p) for p in (parts[0], parts[1], rest[:, :third], gain_sum))
    grand_total = spread_sum(jnp.full((8, HEAD), squares, F32))[0, 0]
    count = float(sections * width * (in_sum.size + out_sum.size + gain_sum.size))
    return (in_sum[None], out_sum[None], gain_sum[None], jnp.sqrt(grand_total / count))


def solution(mesh):
    placed = (
        P("dp", None),
        P("dp", None),
        P("dp", None),
        P("section", "dp", None),
        P("section", "dp", None),
        P("section", None),
    )
    return jax.shard_map(
        local,
        mesh=mesh,
        in_specs=placed,
        out_specs=(P("section", "dp", None), P("section", "dp", None), P("section", "dp"), P()),
        check_vma=False,
    )
```

```python
import functools
import math

import jax
import jax.numpy as jnp
from jax import lax
from jax.experimental import pallas as pl
from jax.experimental.pallas import tpu as pltpu
from jax.sharding import PartitionSpec as P

HEAD = 128
ROWS = 128
EPS = 1e-05
MASKED = -1e30
LIMIT = 8 * 1024 * 1024
BF = jnp.bfloat16
F32 = jnp.float32


def mm(left, right, lc=1, rc=0):
    return lax.dot_general(left, right, (((lc,), (rc,)), ((), ())), preferred_element_type=F32)


def unit(h):
    r = lax.rsqrt(jnp.mean(h * h, axis=-1, keepdims=True) + EPS)
    return r, h * r


def w_in(pack, k, inner):
    return pack[:, :, k * inner:(k + 1) * inner].reshape(-1, inner)


def w_out(pack, part, inner):
    half = pack.shape[1] // 2
    return pack[:, part * half:(part + 1) * half, 3 * inner:].reshape(-1, inner)


def forward_kernel(cycle, micro, last, received, sec, me, hid, bias, gains, pack, *refs):
    (sh, sa, sq, so, sl, out) = refs[-6:]
    inner = so.shape[2]
    heads = inner // HEAD
    odd = cycle % 2
    span = (1 + odd) * ROWS
    section = sec[0]
    m = cycle - 2 * section

    @pl.when((m >= 0) & (m < micro))
    def _():
        own = pl.multiple_of(m * ROWS, ROWS)
        base = pl.multiple_of(own - odd * ROWS, ROWS)

        @pl.when(section == 0)
        def _():
            sh[m] = hid[pl.ds(own, ROWS)]

        if received:
            @pl.when(section != 0)
            def _():
                sh[m] = refs[0][...]

        _, u = unit(sh[m].astype(F32))
        a = (u * gains[...]).astype(BF)
        sa[m] = a
        for k in range(3):
            sq[pl.ds(own, ROWS), k * inner:(k + 1) * inner] = mm(a, w_in(pack, k, inner)).astype(BF)
        mask = bias[m, :, :span]
        scores = []
        for e in range(heads):
            lo, hi = e * HEAD, (e + 1) * HEAD
            q = sq[pl.ds(own, ROWS), lo:hi]
            k = sq[pl.ds(base, span), inner + lo:inner + hi]
            scores.append(mm(q, k, 1, 1) * HEAD ** (-0.5) + mask)
        tops = [jnp.max(s, axis=-1, keepdims=True) for s in scores]
        xs = [jnp.exp(s - top) for s, top in zip(scores, tops)]
        totals = [jnp.sum(x, axis=-1, keepdims=True) for x in xs]
        lane = lax.broadcasted_iota(jnp.int32, (ROWS, HEAD), 1)
        lse = jnp.zeros((ROWS, HEAD), F32)
        for e in range(heads):
            lo, hi = e * HEAD, (e + 1) * HEAD
            v = sq[pl.ds(base, span), 2 * inner + lo:2 * inner + hi]
            so[m, :, lo:hi] = (mm(xs[e].astype(BF), v) * (1.0 / totals[e])).astype(BF)
            lse = jnp.where(lane == e, tops[e] + jnp.log(totals[e]), lse)
        sl[m] = lse

        @pl.when(section != last)
        def _():
            o = so[m]
            for part in range(2):
                cols = slice(part * inner, (part + 1) * inner)
                out[:, cols] = (
                    sh[m, :, cols].astype(F32) + mm(o, w_out(pack, part, inner))
                ).astype(BF)


def backward_kernel(cycle, micro, last, loss_scale, received, sec, me, cot, bias, gains, pack, sh, sq, sl, *refs):
    (sg, sd, sn, sp, out) = refs[-5:]
    inner = sd.shape[2] // 3
    feat = sh.shape[2]
    heads = inner // HEAD
    late = cycle % 2 == 0
    span = 2 * ROWS if late else ROWS
    section = sec[0]
    n = cycle - 2 * (last - section)

    @pl.when((n >= 0) & (n < micro))
    def _():
        m = n + 1 if late else n - 1
        own = pl.multiple_of(m * ROWS, ROWS)
        base = pl.multiple_of(own + ROWS - span, ROWS)

        @pl.when(section == last)
        def _():
            sg[m] = (cot[pl.ds(own, ROWS)].astype(F32) * loss_scale).astype(BF)

        if received:
            @pl.when(section != last)
            def _():
                sg[m] = refs[0][...]

        g = sg[m]
        do_all = (
            mm(g[:, :inner], w_out(pack, 0, inner), 1, 1)
            + mm(g[:, inner:], w_out(pack, 1, inner), 1, 1)
        ).astype(BF)
        mask = bias[m, :, :span]
        lse = sl[m]
        scale = HEAD ** (-0.5)
        cut = [slice(e * HEAD, (e + 1) * HEAD) for e in range(heads)]
        qs = [sq[pl.ds(own, ROWS), e * HEAD:(e + 1) * HEAD] for e in range(heads)]
        ks = [sq[pl.ds(base, span), inner + e * HEAD:inner + (e + 1) * HEAD] for e in range(heads)]
        vs = [sq[pl.ds(base, span), 2 * inner + e * HEAD:2 * inner + (e + 1) * HEAD] for e in range(heads)]
        dos = [do_all[:, c] for c in cut]
        ps = [jnp.exp(mm(qs[e], ks[e], 1, 1) * scale + mask - lse[:, e:e + 1]) for e in range(heads)]
        dps = [mm(dos[e], vs[e], 1, 1) for e in range(heads)]
        insides = [jnp.sum(dp * p, axis=-1, keepdims=True) for dp, p in zip(dps, ps)]
        dss = [(p * (dp - i) * scale).astype(BF) for p, dp, i in zip(ps, dps, insides)]
        for e in range(heads):
            lo, hi = e * HEAD, (e + 1) * HEAD
            sd[m, :, lo:hi] = mm(dss[e], ks[e]).astype(BF)
            dk = mm(dss[e], qs[e], 0, 0)
            dv = mm(ps[e].astype(BF), dos[e], 0, 0)
            for at, value in ((0, dk), (inner, dv)):
                if late:
                    sp[:, at + lo:at + hi] = value[:ROWS]
                    value = value[ROWS:]
                else:
                    value = value + sp[:, at + lo:at + hi]
                sd[m, :, inner + at + lo:inner + at + hi] = value.astype(BF)
        r, u = unit(sh[m].astype(F32))
        da = None
        for k in range(3):
            term = mm(sd[m, :, k * inner:(k + 1) * inner], w_in(pack, k, inner), 1, 1)
            da = term if da is None else da + term
        sn[m] = jnp.sum((da * u).reshape(ROWS // 8, 8, feat), axis=0)
        e = da * gains[...]
        mean = jnp.mean(e * u, axis=-1, keepdims=True)
        out[...] = (sg[m].astype(F32) + r * (e - u * mean)).astype(BF)


def pack_kernel(wi, wo, out):
    rows, inner = wo.shape[0], wo.shape[1] // 2
    out[:, :3 * inner] = wi[...]
    out[:rows, 3 * inner:] = wo[:, :inner]
    out[rows:, 3 * inner:] = wo[:, inner:]


def place(order, rel):
    low, high, y = rel % 2, (rel // 2) % 2, rel // 4
    bit = {2: (low + high) % 2, 6: high, 8: y}
    return 4 * bit[order[0]] + 2 * bit[order[1]] + bit[order[2]]


def gradient_kernel(order, cut, outs, me, sa, sd, so, sg, sn, keep, send):
    micro, rows, feat = sa.shape
    tokens = micro * rows
    inner = so.shape[2]
    width, shard = 2 * keep.shape[0], keep.shape[1]
    lo, hi = cut
    mine = me[0]

    def store(d, pieces):
        low = (d + mine) % 2
        x = (d // 2) % 4
        my_x = (mine // 2) % 4
        first = (x + my_x) % 2
        second = (x // 2 + my_x // 2) % 2
        y = (d // 8 + mine // 8) % 2
        slot = place(order, first + 2 * second + 4 * y)
        for ref, want in ((keep, 0), (send, 1)):
            @pl.when(low == want)
            def _():
                for where, value in pieces:
                    ref[slot, where[0], where[1]] = value

    if outs:
        total = jnp.sum(sn[...], axis=(0, 1)).reshape(1, feat)
        gain = jnp.concatenate(
            [
                jnp.broadcast_to(total[:, c * HEAD:(c + 1) * HEAD], (HEAD, HEAD)).T
                for c in range(feat // HEAD)
            ],
            axis=0,
        ).astype(BF)
    group = 4
    for c in range(width // group):
        a = sa[:, :, c * group * shard:(c + 1) * group * shard].reshape(tokens, group * shard)
        res = mm(a, sd[:, :, lo:hi].reshape(tokens, hi - lo), 0, 0).astype(BF)
        for j in range(group):
            d = c * group + j
            pieces = [((slice(None), slice(0, hi - lo)), res[j * shard:(j + 1) * shard])]
            if outs:
                pieces.append(
                    ((slice(None), slice(hi - lo + inner, None)), gain[d * shard:(d + 1) * shard])
                )
            store(d, pieces)
    if outs:
        half = inner // width
        group = 8
        at = slice(hi - lo, hi - lo + inner)
        g = sg[...].reshape(tokens, feat)
        for c in range(width // group):
            o = so[:, :, c * group * half:(c + 1) * group * half].reshape(tokens, group * half)
            res = mm(o, g, 0, 0).astype(BF)
            for j in range(group):
                rows_of = res[j * half:(j + 1) * half]
                store(c * group + j, [
                    ((slice(0, half), at), rows_of[:, :inner]),
                    ((slice(half, 2 * half), at), rows_of[:, inner:]),
                ])


SMEM = pl.BlockSpec(memory_space=pltpu.SMEM)
VMEM = pl.BlockSpec(memory_space=pltpu.VMEM)


def call(body, ins, states, shapes, out_shape, flops, name):
    count = len(ins)
    got = pl.pallas_call(
        body,
        out_shape=list(shapes) + [out_shape],
        in_specs=[SMEM] * 2 + [VMEM] * (count - 2 + len(states)),
        out_specs=[VMEM] * (len(shapes) + 1),
        input_output_aliases={count + i: i for i in range(len(states))},
        compiler_params=pltpu.CompilerParams(vmem_limit_bytes=LIMIT),
        cost_estimate=pl.CostEstimate(flops=flops, bytes_accessed=12 * 1024 * 1024, transcendentals=0),
        name=name,
    )(*ins, *states)
    return got[-1], list(got[:-1])


def hops(step, last):
    runs = [(0, 1), (0, 3), (0, 3), (1, 5), (1, 5), (3, 6)] + [(4, 7)] * 3
    low, high = runs[min(step // 2, len(runs) - 1)]
    return range(low, min(high, last))


def spread_sum(value):
    for masks in ([1], [2, 4, 6], [8], [64], [16, 32, 48]):
        got = [
            lax.ppermute(value, ("section", "dp"), [(i, i ^ mask) for i in range(128)])
            for mask in masks
        ]
        for other in got:
            value = value + other
    return value


def swap(value, mask):
    return lax.ppermute(value, "dp", [(i, i ^ mask) for i in range(16)])


def scatter_sum(keep, send, order):
    total = keep.astype(F32) + swap(send, 1).astype(F32)
    for mask in order:
        half = total.shape[0] // 2
        total = total[:half] + swap(total[half:].astype(BF), mask).astype(F32)
    return total[0]


def local(hidden_in, segment_ids, cotangent, in_proj, out_proj, norm_gains):
    section = lax.axis_index("section")
    sections = lax.axis_size("section")
    width = lax.axis_size("dp")
    last = sections - 1
    seqs, length = segment_ids.shape
    feat = hidden_in.shape[1]
    shard = in_proj.shape[1]
    inner = out_proj.shape[1] * width
    micro = seqs * length // ROWS
    pack = pl.pallas_call(
        pack_kernel,
        out_shape=jax.ShapeDtypeStruct((shard, 4 * inner), BF),
        in_specs=[VMEM] * 2,
        out_specs=VMEM,
        compiler_params=pltpu.CompilerParams(vmem_limit_bytes=LIMIT),
        name="pack",
    )(in_proj[0], out_proj[0])
    pack = lax.all_gather(pack, "dp", axis=0)
    loss_scale = 1.0 / math.sqrt(width * hidden_in.shape[0])
    tokens = seqs * length
    ident = segment_ids.reshape(seqs, 2, ROWS)
    rows = lax.broadcasted_iota(jnp.int32, (ROWS, 2 * ROWS), 0)
    cols = lax.broadcasted_iota(jnp.int32, (ROWS, 2 * ROWS), 1)
    same = ident[:, :, :, None] == segment_ids[:, None, None, :]
    causal = jnp.stack([cols <= rows, cols <= rows + ROWS])
    bias = jnp.where(same & causal, 0.0, MASKED).astype(F32).reshape(micro, ROWS, length)
    sec = jnp.full((1,), section, jnp.int32)
    me = jnp.full((1,), lax.axis_index("dp"), jnp.int32)

    def shaped(*shape, dtype=BF):
        return jax.ShapeDtypeStruct(shape, dtype)

    f_shapes = [
        shaped(micro, ROWS, feat),
        shaped(micro, ROWS, feat),
        shaped(tokens, 3 * inner),
        shaped(micro, ROWS, inner),
        shaped(micro, ROWS, HEAD, dtype=F32),
    ]
    b_shapes = [
        shaped(micro, ROWS, feat),
        shaped(micro, ROWS, 3 * inner),
        shaped(micro, 8, feat, dtype=F32),
        shaped(ROWS, 2 * inner, dtype=F32),
    ]
    moved = shaped(ROWS, feat)
    per_row = 2 * feat * 4 * inner
    first = 2 * last + 1
    end = first + 2 * last + micro
    f_state, b_state = [], []
    f_recv, b_recv = {}, {}
    for cycle in range(end):
        on = [s for s in range(sections) if 0 <= cycle - 2 * s < micro]
        if on or cycle == 2 * last + micro:
            out, f_state = call(
                functools.partial(forward_kernel, cycle, micro, last, cycle in f_recv),
                [sec, me, hidden_in, bias, norm_gains, pack]
                + ([f_recv[cycle]] if cycle in f_recv else []),
                f_state, f_shapes, moved, ROWS * per_row, "fwd_half",
            )
            if on and on != [last]:
                pairs = [(s, s + 1) for s in hops(cycle, last)]
                f_recv[cycle + 2] = lax.ppermute(out, "section", pairs)
        on = [s for s in range(sections) if 0 <= cycle - first - 2 * (last - s) < micro]
        if on:
            sh, _, sq, _, sl = f_state
            out, b_state = call(
                functools.partial(
                    backward_kernel, cycle - first, micro, last, loss_scale, cycle in b_recv
                ),
                [sec, me, cotangent, bias, norm_gains, pack, sh, sq, sl]
                + ([b_recv[cycle]] if cycle in b_recv else []),
                b_state, b_shapes, moved, 2 * ROWS * per_row, "bwd_half",
            )
            if on != [0]:
                pairs = [(last - s, last - s - 1) for s in hops(cycle - first, last)]
                b_recv[cycle + 2] = lax.ppermute(out, "section", pairs)
    _, sa, _, so, _ = f_state
    sg, sd, sn, _ = b_state
    third = 4 * inner // 3
    parts = []
    for index, order in enumerate(((2, 6, 8), (6, 8, 2), (8, 2, 6))):
        outs = index == 2
        cut = (index * third, min((index + 1) * third, 3 * inner))
        block = shaped(width // 2, shard, third + (HEAD if outs else 0))
        keep, send = pl.pallas_call(
            functools.partial(gradient_kernel, order, cut, outs),
            out_shape=[block, block],
            in_specs=[SMEM] + [VMEM] * 5,
            out_specs=[VMEM] * 2,
            compiler_params=pltpu.CompilerParams(vmem_limit_bytes=LIMIT),
            cost_estimate=pl.CostEstimate(
                flops=2 * tokens * feat * third, bytes_accessed=12 * 1024 * 1024, transcendentals=0
            ),
            name="gradient",
        )(me, sa, sd, so, sg, sn)
        parts.append((keep, send, order))
    parts = [scatter_sum(*part) for part in parts]
    rest = parts[2]
    edge = 3 * inner - 2 * third
    half = out_proj.shape[1]
    in_sum = jnp.concatenate([parts[0], parts[1], rest[:, :edge]], axis=1)
    out_sum = jnp.concatenate([rest[:half, edge:third], rest[half:, edge:third]], axis=1)
    gain_sum = rest[:, third]
    squares = sum(jnp.sum(p * p) for p in (parts[0], parts[1], rest[:, :third], gain_sum))
    grand_total = spread_sum(jnp.full((8, HEAD), squares, F32))[0, 0]
    count = float(sections * width * (in_sum.size + out_sum.size + gain_sum.size))
    return (in_sum[None], out_sum[None], gain_sum[None], jnp.sqrt(grand_total / count))


def solution(mesh):
    placed = (
        P("dp", None),
        P("dp", None),
        P("dp", None),
        P("section", "dp", None),
        P("section", "dp", None),
        P("section", None),
    )
    return jax.shard_map(
        local,
        mesh=mesh,
        in_specs=placed,
        out_specs=(P("section", "dp", None), P("section", "dp", None), P("section", "dp"), P()),
        check_vma=False,
    )
```

```python
import functools
import math

import jax
import jax.numpy as jnp
from jax import lax
from jax.experimental import pallas as pl
from jax.experimental.pallas import tpu as pltpu
from jax.sharding import PartitionSpec as P

HEAD = 128
ROWS = 128
EPS = 1e-05
MASKED = -1e30
LIMIT = 8 * 1024 * 1024
BF = jnp.bfloat16
F32 = jnp.float32


def mm(left, right, lc=1, rc=0):
    return lax.dot_general(left, right, (((lc,), (rc,)), ((), ())), preferred_element_type=F32)


def unit(h):
    r = lax.rsqrt(jnp.mean(h * h, axis=-1, keepdims=True) + EPS)
    return r, h * r


def w_in(pack, k, inner):
    return pack[:, :, k * inner:(k + 1) * inner].reshape(-1, inner)


def w_out(pack, part, inner):
    half = pack.shape[1] // 2
    return pack[:, part * half:(part + 1) * half, 3 * inner:].reshape(-1, inner)


def forward_kernel(cycle, micro, last, received, sec, me, hid, bias, gains, pack, *refs):
    (sh, sa, sq, so, sl, out) = refs[-6:]
    inner = so.shape[2]
    heads = inner // HEAD
    odd = cycle % 2
    span = (1 + odd) * ROWS
    section = sec[0]
    m = cycle - 2 * section

    @pl.when((m >= 0) & (m < micro))
    def _():
        own = pl.multiple_of(m * ROWS, ROWS)
        base = pl.multiple_of(own - odd * ROWS, ROWS)

        @pl.when(section == 0)
        def _():
            sh[m] = hid[pl.ds(own, ROWS)]

        if received:
            @pl.when(section != 0)
            def _():
                sh[m] = refs[0][...]

        _, u = unit(sh[m].astype(F32))
        a = (u * gains[...]).astype(BF)
        sa[m] = a
        for k in range(3):
            sq[pl.ds(own, ROWS), k * inner:(k + 1) * inner] = mm(a, w_in(pack, k, inner)).astype(BF)
        mask = bias[m, :, :span]
        scores = []
        for e in range(heads):
            lo, hi = e * HEAD, (e + 1) * HEAD
            q = sq[pl.ds(own, ROWS), lo:hi]
            k = sq[pl.ds(base, span), inner + lo:inner + hi]
            scores.append(mm(q, k, 1, 1) * HEAD ** (-0.5) + mask)
        tops = [jnp.max(s, axis=-1, keepdims=True) for s in scores]
        xs = [jnp.exp(s - top) for s, top in zip(scores, tops)]
        totals = [jnp.sum(x, axis=-1, keepdims=True) for x in xs]
        lane = lax.broadcasted_iota(jnp.int32, (ROWS, HEAD), 1)
        lse = jnp.zeros((ROWS, HEAD), F32)
        for e in range(heads):
            lo, hi = e * HEAD, (e + 1) * HEAD
            v = sq[pl.ds(base, span), 2 * inner + lo:2 * inner + hi]
            so[m, :, lo:hi] = (mm(xs[e].astype(BF), v) * (1.0 / totals[e])).astype(BF)
            lse = jnp.where(lane == e, tops[e] + jnp.log(totals[e]), lse)
        sl[m] = lse

        @pl.when(section != last)
        def _():
            o = so[m]
            for part in range(2):
                cols = slice(part * inner, (part + 1) * inner)
                out[:, cols] = (
                    sh[m, :, cols].astype(F32) + mm(o, w_out(pack, part, inner))
                ).astype(BF)


def backward_kernel(cycle, micro, last, loss_scale, received, sec, me, cot, bias, gains, pack, sh, sq, sl, *refs):
    (sg, sd, sn, sp, out) = refs[-5:]
    inner = sd.shape[2] // 3
    feat = sh.shape[2]
    heads = inner // HEAD
    late = cycle % 2 == 0
    span = 2 * ROWS if late else ROWS
    section = sec[0]
    n = cycle - 2 * (last - section)

    @pl.when((n >= 0) & (n < micro))
    def _():
        m = n + 1 if late else n - 1
        own = pl.multiple_of(m * ROWS, ROWS)
        base = pl.multiple_of(own + ROWS - span, ROWS)

        @pl.when(section == last)
        def _():
            sg[m] = (cot[pl.ds(own, ROWS)].astype(F32) * loss_scale).astype(BF)

        if received:
            @pl.when(section != last)
            def _():
                sg[m] = refs[0][...]

        g = sg[m]
        do_all = (
            mm(g[:, :inner], w_out(pack, 0, inner), 1, 1)
            + mm(g[:, inner:], w_out(pack, 1, inner), 1, 1)
        ).astype(BF)
        mask = bias[m, :, :span]
        lse = sl[m]
        scale = HEAD ** (-0.5)
        cut = [slice(e * HEAD, (e + 1) * HEAD) for e in range(heads)]
        qs = [sq[pl.ds(own, ROWS), e * HEAD:(e + 1) * HEAD] for e in range(heads)]
        ks = [sq[pl.ds(base, span), inner + e * HEAD:inner + (e + 1) * HEAD] for e in range(heads)]
        vs = [sq[pl.ds(base, span), 2 * inner + e * HEAD:2 * inner + (e + 1) * HEAD] for e in range(heads)]
        dos = [do_all[:, c] for c in cut]
        ps = [jnp.exp(mm(qs[e], ks[e], 1, 1) * scale + mask - lse[:, e:e + 1]) for e in range(heads)]
        dps = [mm(dos[e], vs[e], 1, 1) for e in range(heads)]
        insides = [jnp.sum(dp * p, axis=-1, keepdims=True) for dp, p in zip(dps, ps)]
        dss = [(p * (dp - i) * scale).astype(BF) for p, dp, i in zip(ps, dps, insides)]
        for e in range(heads):
            lo, hi = e * HEAD, (e + 1) * HEAD
            sd[m, :, lo:hi] = mm(dss[e], ks[e]).astype(BF)
            dk = mm(dss[e], qs[e], 0, 0)
            dv = mm(ps[e].astype(BF), dos[e], 0, 0)
            for at, value in ((0, dk), (inner, dv)):
                if late:
                    sp[:, at + lo:at + hi] = value[:ROWS]
                    value = value[ROWS:]
                else:
                    value = value + sp[:, at + lo:at + hi]
                sd[m, :, inner + at + lo:inner + at + hi] = value.astype(BF)
        r, u = unit(sh[m].astype(F32))
        da = None
        for k in range(3):
            term = mm(sd[m, :, k * inner:(k + 1) * inner], w_in(pack, k, inner), 1, 1)
            da = term if da is None else da + term
        sn[m] = jnp.sum((da * u).reshape(ROWS // 8, 8, feat), axis=0)
        e = da * gains[...]
        mean = jnp.mean(e * u, axis=-1, keepdims=True)
        out[...] = (sg[m].astype(F32) + r * (e - u * mean)).astype(BF)


def place(order, rel):
    low, high, y = rel % 2, (rel // 2) % 2, rel // 4
    bit = {2: (low + high) % 2, 6: high, 8: y}
    return 4 * bit[order[0]] + 2 * bit[order[1]] + bit[order[2]]


def gradient_kernel(order, cut, me, sa, sd, so, sg, sn, *refs):
    keep, send = refs[-2:]
    micro, rows, feat = sa.shape
    tokens = micro * rows
    inner = so.shape[2]
    width, shard = 2 * keep.shape[0], keep.shape[1]
    half = inner // width
    mine = me[0]

    def store(d, pieces):
        low = (d + mine) % 2
        x = (d // 2) % 4
        my_x = (mine // 2) % 4
        first = (x + my_x) % 2
        second = (x // 2 + my_x // 2) % 2
        y = (d // 8 + mine // 8) % 2
        slot = place(order, first + 2 * second + 4 * y)
        for ref, want in ((keep, 0), (send, 1)):
            @pl.when(low == want)
            def _():
                for rows_of, cols, value in pieces:
                    ref[slot, rows_of, cols] = value

    if cut:
        group = 4
        d_of = sd[:, :, cut[0]:cut[1]].reshape(tokens, cut[1] - cut[0])
        for c in range(width // group):
            a = sa[:, :, c * group * shard:(c + 1) * group * shard].reshape(tokens, group * shard)
            res = mm(a, d_of, 0, 0).astype(BF)
            for j in range(group):
                store(c * group + j, [(slice(None), slice(None), res[j * shard:(j + 1) * shard])])
        return
    total = jnp.sum(sn[...], axis=(0, 1)).reshape(1, feat)
    gain = jnp.concatenate(
        [
            jnp.broadcast_to(total[:, c * HEAD:(c + 1) * HEAD], (HEAD, HEAD)).T
            for c in range(feat // HEAD)
        ],
        axis=0,
    ).astype(BF)
    group = 8
    g = sg[...].reshape(tokens, feat)
    for c in range(width // group):
        o = so[:, :, c * group * half:(c + 1) * group * half].reshape(tokens, group * half)
        res = mm(o, g, 0, 0).astype(BF)
        for j in range(group):
            d = c * group + j
            rows_of = res[j * half:(j + 1) * half]
            store(d, [
                (slice(0, half), slice(0, inner), rows_of[:, :inner]),
                (slice(half, 2 * half), slice(0, inner), rows_of[:, inner:]),
                (slice(None), slice(inner, None), gain[d * shard:(d + 1) * shard]),
            ])


SMEM = pl.BlockSpec(memory_space=pltpu.SMEM)
VMEM = pl.BlockSpec(memory_space=pltpu.VMEM)


def call(body, ins, states, shapes, out_shape, flops, name):
    count = len(ins)
    got = pl.pallas_call(
        body,
        out_shape=list(shapes) + [out_shape],
        in_specs=[SMEM] * 2 + [VMEM] * (count - 2 + len(states)),
        out_specs=[VMEM] * (len(shapes) + 1),
        input_output_aliases={count + i: i for i in range(len(states))},
        compiler_params=pltpu.CompilerParams(vmem_limit_bytes=LIMIT),
        cost_estimate=pl.CostEstimate(flops=flops, bytes_accessed=12 * 1024 * 1024, transcendentals=0),
        name=name,
    )(*ins, *states)
    return got[-1], list(got[:-1])


def hops(step, last):
    runs = [(0, 1), (0, 3), (0, 3), (1, 5), (1, 5), (3, 6)] + [(4, 7)] * 3
    low, high = runs[min(step // 2, len(runs) - 1)]
    return range(low, min(high, last))


def spread_sum(value):
    for masks in ([1], [2, 4, 6], [8], [64], [16, 32, 48]):
        got = [
            lax.ppermute(value, ("section", "dp"), [(i, i ^ mask) for i in range(128)])
            for mask in masks
        ]
        for other in got:
            value = value + other
    return value


def swap(value, mask):
    return lax.ppermute(value, "dp", [(i, i ^ mask) for i in range(16)])


def halved(total, mask):
    half = total.shape[0] // 2
    return total[:half], total[half:].astype(BF), mask


def added(kept, sent, mask):
    return kept.astype(F32) + swap(sent, mask).astype(F32)


def local(hidden_in, segment_ids, cotangent, in_proj, out_proj, norm_gains):
    section = lax.axis_index("section")
    sections = lax.axis_size("section")
    width = lax.axis_size("dp")
    last = sections - 1
    seqs, length = segment_ids.shape
    feat = hidden_in.shape[1]
    shard = in_proj.shape[1]
    inner = out_proj.shape[1] * width
    micro = seqs * length // ROWS
    wo = jnp.concatenate([out_proj[0, :, :inner], out_proj[0, :, inner:]], axis=0)
    pack = lax.all_gather(jnp.concatenate([in_proj[0], wo], axis=1), "dp", axis=0)
    loss_scale = 1.0 / math.sqrt(width * hidden_in.shape[0])
    tokens = seqs * length
    ident = segment_ids.reshape(seqs, 2, ROWS)
    rows = lax.broadcasted_iota(jnp.int32, (ROWS, 2 * ROWS), 0)
    cols = lax.broadcasted_iota(jnp.int32, (ROWS, 2 * ROWS), 1)
    same = ident[:, :, :, None] == segment_ids[:, None, None, :]
    causal = jnp.stack([cols <= rows, cols <= rows + ROWS])
    bias = jnp.where(same & causal, 0.0, MASKED).astype(F32).reshape(micro, ROWS, length)
    sec = jnp.full((1,), section, jnp.int32)
    me = jnp.full((1,), lax.axis_index("dp"), jnp.int32)

    def shaped(*shape, dtype=BF):
        return jax.ShapeDtypeStruct(shape, dtype)

    f_shapes = [
        shaped(micro, ROWS, feat),
        shaped(micro, ROWS, feat),
        shaped(tokens, 3 * inner),
        shaped(micro, ROWS, inner),
        shaped(micro, ROWS, HEAD, dtype=F32),
    ]
    b_shapes = [
        shaped(micro, ROWS, feat),
        shaped(micro, ROWS, 3 * inner),
        shaped(micro, 8, feat, dtype=F32),
        shaped(ROWS, 2 * inner, dtype=F32),
    ]
    moved = shaped(ROWS, feat)
    per_row = 2 * feat * 4 * inner
    first = 2 * last + 1
    end = first + 2 * last + micro
    f_state, b_state = [], []
    f_recv, b_recv = {}, {}
    for cycle in range(end):
        on = [s for s in range(sections) if 0 <= cycle - 2 * s < micro]
        if on or cycle == 2 * last + micro:
            out, f_state = call(
                functools.partial(forward_kernel, cycle, micro, last, cycle in f_recv),
                [sec, me, hidden_in, bias, norm_gains, pack]
                + ([f_recv[cycle]] if cycle in f_recv else []),
                f_state, f_shapes, moved, ROWS * per_row, "fwd_half",
            )
            if on and on != [last]:
                pairs = [(s, s + 1) for s in hops(cycle, last)]
                f_recv[cycle + 2] = lax.ppermute(out, "section", pairs)
        on = [s for s in range(sections) if 0 <= cycle - first - 2 * (last - s) < micro]
        if on:
            sh, _, sq, _, sl = f_state
            out, b_state = call(
                functools.partial(
                    backward_kernel, cycle - first, micro, last, loss_scale, cycle in b_recv
                ),
                [sec, me, cotangent, bias, norm_gains, pack, sh, sq, sl]
                + ([b_recv[cycle]] if cycle in b_recv else []),
                b_state, b_shapes, moved, 2 * ROWS * per_row, "bwd_half",
            )
            if on != [0]:
                pairs = [(last - s, last - s - 1) for s in hops(cycle - first, last)]
                b_recv[cycle + 2] = lax.ppermute(out, "section", pairs)
    _, sa, _, so, _ = f_state
    sg, sd, sn, _ = b_state
    edge = 3 * inner // 2
    work = [(2, 6, 8), (6, 8, 2), (8, 2, 6)]
    cuts = [(0, edge), (edge, 3 * inner), None]
    parts = []
    for order, cut in zip(work, cuts):
        block = shaped(width // 2, shard, cut[1] - cut[0] if cut else inner + HEAD)
        keep, send = pl.pallas_call(
            functools.partial(gradient_kernel, order, cut),
            out_shape=[block, block],
            in_specs=[SMEM] + [VMEM] * 5,
            out_specs=[VMEM] * 2,
            compiler_params=pltpu.CompilerParams(vmem_limit_bytes=LIMIT),
            cost_estimate=pl.CostEstimate(
                flops=2 * tokens * feat * block.shape[2], bytes_accessed=12 * 1024 * 1024, transcendentals=0
            ),
            name="gradient",
        )(me, sa, sd, so, sg, sn)
        parts.append(halved(added(keep, send, 1), order[0]))
    sums = []
    for part, order in zip(parts, work):
        total = added(*part)
        for mask in order[1:]:
            total = added(*halved(total, mask))
        sums.append(total[0])
    rest = sums[2]
    half = out_proj.shape[1]
    in_sum = jnp.concatenate(sums[:2], axis=1)
    out_sum = jnp.concatenate([rest[:half, :inner], rest[half:, :inner]], axis=1)
    gain_sum = rest[:, inner]
    squares = sum(jnp.sum(p * p) for p in (sums[0], sums[1], rest[:, :inner], gain_sum))
    grand_total = spread_sum(jnp.full((8, HEAD), squares, F32))[0, 0]
    count = float(sections * width * (in_sum.size + out_sum.size + gain_sum.size))
    return (in_sum[None], out_sum[None], gain_sum[None], jnp.sqrt(grand_total / count))


def solution(mesh):
    placed = (
        P("dp", None),
        P("dp", None),
        P("dp", None),
        P("section", "dp", None),
        P("section", "dp", None),
        P("section", None),
    )
    return jax.shard_map(
        local,
        mesh=mesh,
        in_specs=placed,
        out_specs=(P("section", "dp", None), P("section", "dp", None), P("section", "dp"), P()),
        check_vma=False,
    )
```

```python
import functools
import math

import jax
import jax.numpy as jnp
from jax import lax
from jax.experimental import pallas as pl
from jax.experimental.pallas import tpu as pltpu
from jax.sharding import PartitionSpec as P

HEAD = 128
ROWS = 128
EPS = 1e-05
MASKED = -1e30
LIMIT = 8 * 1024 * 1024
BF = jnp.bfloat16
F32 = jnp.float32


def mm(left, right, lc=1, rc=0):
    return lax.dot_general(left, right, (((lc,), (rc,)), ((), ())), preferred_element_type=F32)


def unit(h):
    r = lax.rsqrt(jnp.mean(h * h, axis=-1, keepdims=True) + EPS)
    return r, h * r


def w_in(pack, k, inner):
    return pack[:, :, k * inner:(k + 1) * inner].reshape(-1, inner)


def w_out(pack, part, inner):
    half = pack.shape[1] // 2
    return pack[:, part * half:(part + 1) * half, 3 * inner:].reshape(-1, inner)


def forward_kernel(cycle, micro, last, received, sec, me, hid, bias, gains, pack, *refs):
    (sh, sa, sq, so, sl, out) = refs[-6:]
    inner = so.shape[2]
    heads = inner // HEAD
    odd = cycle % 2
    span = (1 + odd) * ROWS
    section = sec[0]
    m = cycle - 2 * section

    @pl.when((m >= 0) & (m < micro))
    def _():
        own = pl.multiple_of(m * ROWS, ROWS)
        base = pl.multiple_of(own - odd * ROWS, ROWS)

        @pl.when(section == 0)
        def _():
            sh[m] = hid[pl.ds(own, ROWS)]

        if received:
            @pl.when(section != 0)
            def _():
                sh[m] = refs[0][...]

        _, u = unit(sh[m].astype(F32))
        a = (u * gains[...]).astype(BF)
        sa[m] = a
        for k in range(3):
            sq[pl.ds(own, ROWS), k * inner:(k + 1) * inner] = mm(a, w_in(pack, k, inner)).astype(BF)
        mask = bias[m, :, :span]
        scores = []
        for e in range(heads):
            lo, hi = e * HEAD, (e + 1) * HEAD
            q = sq[pl.ds(own, ROWS), lo:hi]
            k = sq[pl.ds(base, span), inner + lo:inner + hi]
            scores.append(mm(q, k, 1, 1) * HEAD ** (-0.5) + mask)
        tops = [jnp.max(s, axis=-1, keepdims=True) for s in scores]
        xs = [jnp.exp(s - top) for s, top in zip(scores, tops)]
        totals = [jnp.sum(x, axis=-1, keepdims=True) for x in xs]
        lane = lax.broadcasted_iota(jnp.int32, (ROWS, HEAD), 1)
        lse = jnp.zeros((ROWS, HEAD), F32)
        for e in range(heads):
            lo, hi = e * HEAD, (e + 1) * HEAD
            v = sq[pl.ds(base, span), 2 * inner + lo:2 * inner + hi]
            so[m, :, lo:hi] = (mm(xs[e].astype(BF), v) * (1.0 / totals[e])).astype(BF)
            lse = jnp.where(lane == e, tops[e] + jnp.log(totals[e]), lse)
        sl[m] = lse

        @pl.when(section != last)
        def _():
            o = so[m]
            for part in range(2):
                cols = slice(part * inner, (part + 1) * inner)
                out[:, cols] = (
                    sh[m, :, cols].astype(F32) + mm(o, w_out(pack, part, inner))
                ).astype(BF)


def backward_kernel(cycle, micro, last, loss_scale, received, sec, me, cot, bias, gains, pack, sh, sq, sl, *refs):
    (sg, sd, sn, sp, out) = refs[-5:]
    inner = sd.shape[2] // 3
    feat = sh.shape[2]
    heads = inner // HEAD
    late = cycle % 2 == 0
    span = 2 * ROWS if late else ROWS
    section = sec[0]
    d = cycle - 2 * (last - section)
    n = jnp.where(d < 2, d, d - 2)

    @pl.when((d >= 0) & (n < micro) & (d // 2 != 1))
    def _():
        m = n + 1 if late else n - 1
        own = pl.multiple_of(m * ROWS, ROWS)
        base = pl.multiple_of(own + ROWS - span, ROWS)

        @pl.when(section == last)
        def _():
            sg[m] = (cot[pl.ds(own, ROWS)].astype(F32) * loss_scale).astype(BF)

        if received:
            @pl.when(section != last)
            def _():
                sg[m] = refs[0][...]

        g = sg[m]
        do_all = (
            mm(g[:, :inner], w_out(pack, 0, inner), 1, 1)
            + mm(g[:, inner:], w_out(pack, 1, inner), 1, 1)
        ).astype(BF)
        mask = bias[m, :, :span]
        lse = sl[m]
        scale = HEAD ** (-0.5)
        cut = [slice(e * HEAD, (e + 1) * HEAD) for e in range(heads)]
        qs = [sq[pl.ds(own, ROWS), e * HEAD:(e + 1) * HEAD] for e in range(heads)]
        ks = [sq[pl.ds(base, span), inner + e * HEAD:inner + (e + 1) * HEAD] for e in range(heads)]
        vs = [sq[pl.ds(base, span), 2 * inner + e * HEAD:2 * inner + (e + 1) * HEAD] for e in range(heads)]
        dos = [do_all[:, c] for c in cut]
        ps = [jnp.exp(mm(qs[e], ks[e], 1, 1) * scale + mask - lse[:, e:e + 1]) for e in range(heads)]
        dps = [mm(dos[e], vs[e], 1, 1) for e in range(heads)]
        insides = [jnp.sum(dp * p, axis=-1, keepdims=True) for dp, p in zip(dps, ps)]
        dss = [(p * (dp - i) * scale).astype(BF) for p, dp, i in zip(ps, dps, insides)]
        for e in range(heads):
            lo, hi = e * HEAD, (e + 1) * HEAD
            sd[m, :, lo:hi] = mm(dss[e], ks[e]).astype(BF)
            dk = mm(dss[e], qs[e], 0, 0)
            dv = mm(ps[e].astype(BF), dos[e], 0, 0)
            for at, value in ((0, dk), (inner, dv)):
                if late:
                    sp[:, at + lo:at + hi] = value[:ROWS]
                    value = value[ROWS:]
                else:
                    value = value + sp[:, at + lo:at + hi]
                sd[m, :, inner + at + lo:inner + at + hi] = value.astype(BF)
        r, u = unit(sh[m].astype(F32))
        da = None
        for k in range(3):
            term = mm(sd[m, :, k * inner:(k + 1) * inner], w_in(pack, k, inner), 1, 1)
            da = term if da is None else da + term
        sn[m] = jnp.sum((da * u).reshape(ROWS // 8, 8, feat), axis=0)
        e = da * gains[...]
        mean = jnp.mean(e * u, axis=-1, keepdims=True)
        out[...] = (sg[m].astype(F32) + r * (e - u * mean)).astype(BF)


def place(order, rel):
    low, high, y = rel % 2, (rel // 2) % 2, rel // 4
    bit = {2: (low + high) % 2, 6: high, 8: y}
    return 4 * bit[order[0]] + 2 * bit[order[1]] + bit[order[2]]


def gradient_kernel(order, cut, outs, me, sa, sd, so, sg, sn, keep, send):
    micro, rows, feat = sa.shape
    tokens = micro * rows
    inner = so.shape[2]
    width, shard = 2 * keep.shape[0], keep.shape[1]
    lo, hi = cut
    mine = me[0]

    def store(d, pieces):
        low = (d + mine) % 2
        x = (d // 2) % 4
        my_x = (mine // 2) % 4
        first = (x + my_x) % 2
        second = (x // 2 + my_x // 2) % 2
        y = (d // 8 + mine // 8) % 2
        slot = place(order, first + 2 * second + 4 * y)
        for ref, want in ((keep, 0), (send, 1)):
            @pl.when(low == want)
            def _():
                for where, value in pieces:
                    ref[slot, where[0], where[1]] = value

    if outs:
        total = jnp.sum(sn[...], axis=(0, 1)).reshape(1, feat)
        gain = jnp.concatenate(
            [
                jnp.broadcast_to(total[:, c * HEAD:(c + 1) * HEAD], (HEAD, HEAD)).T
                for c in range(feat // HEAD)
            ],
            axis=0,
        ).astype(BF)
    group = 4
    for c in range(width // group):
        a = sa[:, :, c * group * shard:(c + 1) * group * shard].reshape(tokens, group * shard)
        res = mm(a, sd[:, :, lo:hi].reshape(tokens, hi - lo), 0, 0).astype(BF)
        for j in range(group):
            d = c * group + j
            pieces = [((slice(None), slice(0, hi - lo)), res[j * shard:(j + 1) * shard])]
            if outs:
                pieces.append(
                    ((slice(None), slice(hi - lo + inner, None)), gain[d * shard:(d + 1) * shard])
                )
            store(d, pieces)
    if outs:
        half = inner // width
        group = 8
        at = slice(hi - lo, hi - lo + inner)
        g = sg[...].reshape(tokens, feat)
        for c in range(width // group):
            o = so[:, :, c * group * half:(c + 1) * group * half].reshape(tokens, group * half)
            res = mm(o, g, 0, 0).astype(BF)
            for j in range(group):
                rows_of = res[j * half:(j + 1) * half]
                store(c * group + j, [
                    ((slice(0, half), at), rows_of[:, :inner]),
                    ((slice(half, 2 * half), at), rows_of[:, inner:]),
                ])


SMEM = pl.BlockSpec(memory_space=pltpu.SMEM)
VMEM = pl.BlockSpec(memory_space=pltpu.VMEM)


def call(body, ins, states, shapes, out_shape, flops, name):
    count = len(ins)
    got = pl.pallas_call(
        body,
        out_shape=list(shapes) + [out_shape],
        in_specs=[SMEM] * 2 + [VMEM] * (count - 2 + len(states)),
        out_specs=[VMEM] * (len(shapes) + 1),
        input_output_aliases={count + i: i for i in range(len(states))},
        compiler_params=pltpu.CompilerParams(vmem_limit_bytes=LIMIT),
        cost_estimate=pl.CostEstimate(flops=flops, bytes_accessed=12 * 1024 * 1024, transcendentals=0),
        name=name,
    )(*ins, *states)
    return got[-1], list(got[:-1])


F_HOPS = ((0,), (0, 1, 2), (0, 1, 2), (1, 2, 3, 4), (1, 2, 3, 4), (3, 4, 5, 6))
B_HOPS = ((0, 2), (1, 2, 4), (0, 2), (0, 1, 3), (1, 2, 4), (2, 3, 5), (3, 4, 6), (4, 5), (5, 6))


def hops(table, step):
    return table[min(step // 2, len(table) - 1)]


def order_of_steps(micro, last):
    turn = 2 * last
    steps = [("f", i) for i in range(turn + 2)]
    steps += [("b", 0), ("b", 1), ("b", 2), ("f", turn + 2), ("b", 3), ("f", turn + 3), ("b", 4), ("b", 5)]
    steps += [("f", i) for i in range(turn + 4, turn + micro)]
    steps += [("b", i) for i in range(6, turn + micro + 2)]
    return steps


def spread_sum(value):
    for masks in ([1], [2, 4, 6], [8], [64], [16, 32, 48]):
        got = [
            lax.ppermute(value, ("section", "dp"), [(i, i ^ mask) for i in range(128)])
            for mask in masks
        ]
        for other in got:
            value = value + other
    return value


def swap(value, mask):
    return lax.ppermute(value, "dp", [(i, i ^ mask) for i in range(16)])


def scatter_sum(keep, send, order):
    total = keep.astype(F32) + swap(send, 1).astype(F32)
    for mask in order:
        half = total.shape[0] // 2
        total = total[:half] + swap(total[half:].astype(BF), mask).astype(F32)
    return total[0]


def local(hidden_in, segment_ids, cotangent, in_proj, out_proj, norm_gains):
    section = lax.axis_index("section")
    sections = lax.axis_size("section")
    width = lax.axis_size("dp")
    last = sections - 1
    seqs, length = segment_ids.shape
    feat = hidden_in.shape[1]
    shard = in_proj.shape[1]
    inner = out_proj.shape[1] * width
    micro = seqs * length // ROWS
    wo = jnp.concatenate([out_proj[0, :, :inner], out_proj[0, :, inner:]], axis=0)
    pack = lax.all_gather(jnp.concatenate([in_proj[0], wo], axis=1), "dp", axis=0)
    loss_scale = 1.0 / math.sqrt(width * hidden_in.shape[0])
    tokens = seqs * length
    ident = segment_ids.reshape(seqs, 2, ROWS)
    rows = lax.broadcasted_iota(jnp.int32, (ROWS, 2 * ROWS), 0)
    cols = lax.broadcasted_iota(jnp.int32, (ROWS, 2 * ROWS), 1)
    same = ident[:, :, :, None] == segment_ids[:, None, None, :]
    causal = jnp.stack([cols <= rows, cols <= rows + ROWS])
    bias = jnp.where(same & causal, 0.0, MASKED).astype(F32).reshape(micro, ROWS, length)
    sec = jnp.full((1,), section, jnp.int32)
    me = jnp.full((1,), lax.axis_index("dp"), jnp.int32)

    def shaped(*shape, dtype=BF):
        return jax.ShapeDtypeStruct(shape, dtype)

    f_shapes = [
        shaped(micro, ROWS, feat),
        shaped(micro, ROWS, feat),
        shaped(tokens, 3 * inner),
        shaped(micro, ROWS, inner),
        shaped(micro, ROWS, HEAD, dtype=F32),
    ]
    b_shapes = [
        shaped(micro, ROWS, feat),
        shaped(micro, ROWS, 3 * inner),
        shaped(micro, 8, feat, dtype=F32),
        shaped(ROWS, 2 * inner, dtype=F32),
    ]
    moved = shaped(ROWS, feat)
    per_row = 2 * feat * 4 * inner
    f_state, b_state = [], []
    f_recv, b_recv = {}, {}
    for kind, step in order_of_steps(micro, last):
        if kind == "f":
            out, f_state = call(
                functools.partial(forward_kernel, step, micro, last, step in f_recv),
                [sec, me, hidden_in, bias, norm_gains, pack] + ([f_recv[step]] if step in f_recv else []),
                f_state, f_shapes, moved, ROWS * per_row, "fwd_half",
            )
            if step < 2 * last - 2 + micro:
                pairs = [(h, h + 1) for h in hops(F_HOPS, step)]
                f_recv[step + 2] = lax.ppermute(out, "section", pairs)
        else:
            sh, _, sq, _, sl = f_state
            out, b_state = call(
                functools.partial(backward_kernel, step, micro, last, loss_scale, step in b_recv),
                [sec, me, cotangent, bias, norm_gains, pack, sh, sq, sl]
                + ([b_recv[step]] if step in b_recv else []),
                b_state, b_shapes, moved, 2 * ROWS * per_row, "bwd_half",
            )
            if step < 2 * last + micro:
                pairs = [(last - h, last - h - 1) for h in hops(B_HOPS, step)]
                b_recv[step + 2] = lax.ppermute(out, "section", pairs)
    _, sa, _, so, _ = f_state
    sg, sd, sn, _ = b_state
    third = 4 * inner // 3
    parts = []
    for index, order in enumerate(((2, 6, 8), (6, 8, 2), (8, 2, 6))):
        outs = index == 2
        cut = (index * third, min((index + 1) * third, 3 * inner))
        block = shaped(width // 2, shard, third + (HEAD if outs else 0))
        keep, send = pl.pallas_call(
            functools.partial(gradient_kernel, order, cut, outs),
            out_shape=[block, block],
            in_specs=[SMEM] + [VMEM] * 5,
            out_specs=[VMEM] * 2,
            compiler_params=pltpu.CompilerParams(vmem_limit_bytes=LIMIT),
            cost_estimate=pl.CostEstimate(
                flops=2 * tokens * feat * third, bytes_accessed=12 * 1024 * 1024, transcendentals=0
            ),
            name="gradient",
        )(me, sa, sd, so, sg, sn)
        parts.append((keep, send, order))
    parts = [scatter_sum(*part) for part in parts]
    rest = parts[2]
    edge = 3 * inner - 2 * third
    half = out_proj.shape[1]
    in_sum = jnp.concatenate([parts[0], parts[1], rest[:, :edge]], axis=1)
    out_sum = jnp.concatenate([rest[:half, edge:third], rest[half:, edge:third]], axis=1)
    gain_sum = rest[:, third]
    squares = sum(jnp.sum(p * p) for p in (parts[0], parts[1], rest[:, :third], gain_sum))
    grand_total = spread_sum(jnp.full((8, HEAD), squares, F32))[0, 0]
    count = float(sections * width * (in_sum.size + out_sum.size + gain_sum.size))
    return (in_sum[None], out_sum[None], gain_sum[None], jnp.sqrt(grand_total / count))


def solution(mesh):
    placed = (
        P("dp", None),
        P("dp", None),
        P("dp", None),
        P("section", "dp", None),
        P("section", "dp", None),
        P("section", None),
    )
    return jax.shard_map(
        local,
        mesh=mesh,
        in_specs=placed,
        out_specs=(P("section", "dp", None), P("section", "dp", None), P("section", "dp"), P()),
        check_vma=False,
    )
```

```python
import functools
import math

import jax
import jax.numpy as jnp
from jax import lax
from jax.experimental import pallas as pl
from jax.experimental.pallas import tpu as pltpu
from jax.sharding import PartitionSpec as P

HEAD = 128
ROWS = 128
EPS = 1e-05
MASKED = -1e30
LIMIT = 8 * 1024 * 1024
BF = jnp.bfloat16
F32 = jnp.float32


def mm(left, right, lc=1, rc=0):
    return lax.dot_general(left, right, (((lc,), (rc,)), ((), ())), preferred_element_type=F32)


def unit(h):
    r = lax.rsqrt(jnp.mean(h * h, axis=-1, keepdims=True) + EPS)
    return r, h * r


def w_in(pack, k, inner):
    return pack[:, :, k * inner:(k + 1) * inner].reshape(-1, inner)


def w_out(pack, part, inner):
    half = pack.shape[1] // 2
    return pack[:, part * half:(part + 1) * half, 3 * inner:].reshape(-1, inner)


def forward_kernel(cycle, micro, last, received, sec, me, hid, bias, gains, pack, *refs):
    (sh, sa, sq, so, sl, out) = refs[-6:]
    inner = so.shape[2]
    heads = inner // HEAD
    odd = cycle % 2
    span = (1 + odd) * ROWS
    section = sec[0]
    m = cycle - 2 * section

    @pl.when((m >= 0) & (m < micro))
    def _():
        own = pl.multiple_of(m * ROWS, ROWS)
        base = pl.multiple_of(own - odd * ROWS, ROWS)

        @pl.when(section == 0)
        def _():
            sh[m] = hid[pl.ds(own, ROWS)]

        if received:
            @pl.when(section != 0)
            def _():
                sh[m] = refs[0][...]

        _, u = unit(sh[m].astype(F32))
        a = (u * gains[...]).astype(BF)
        sa[m] = a
        for k in range(3):
            sq[pl.ds(own, ROWS), k * inner:(k + 1) * inner] = mm(a, w_in(pack, k, inner)).astype(BF)
        mask = bias[m, :, :span]
        scores = []
        for e in range(heads):
            lo, hi = e * HEAD, (e + 1) * HEAD
            q = sq[pl.ds(own, ROWS), lo:hi]
            k = sq[pl.ds(base, span), inner + lo:inner + hi]
            scores.append(mm(q, k, 1, 1) * HEAD ** (-0.5) + mask)
        tops = [jnp.max(s, axis=-1, keepdims=True) for s in scores]
        xs = [jnp.exp(s - top) for s, top in zip(scores, tops)]
        totals = [jnp.sum(x, axis=-1, keepdims=True) for x in xs]
        lane = lax.broadcasted_iota(jnp.int32, (ROWS, HEAD), 1)
        lse = jnp.zeros((ROWS, HEAD), F32)
        for e in range(heads):
            lo, hi = e * HEAD, (e + 1) * HEAD
            v = sq[pl.ds(base, span), 2 * inner + lo:2 * inner + hi]
            so[m, :, lo:hi] = (mm(xs[e].astype(BF), v) * (1.0 / totals[e])).astype(BF)
            lse = jnp.where(lane == e, tops[e] + jnp.log(totals[e]), lse)
        sl[m] = lse

        @pl.when(section != last)
        def _():
            o = so[m]
            for part in range(2):
                cols = slice(part * inner, (part + 1) * inner)
                out[:, cols] = (
                    sh[m, :, cols].astype(F32) + mm(o, w_out(pack, part, inner))
                ).astype(BF)


def backward_kernel(cycle, micro, last, loss_scale, received, sec, me, cot, bias, gains, pack, sh, sq, sl, *refs):
    (sg, sd, sn, sp, out) = refs[-5:]
    inner = sd.shape[2] // 3
    feat = sh.shape[2]
    heads = inner // HEAD
    late = cycle % 2 == 0
    span = 2 * ROWS if late else ROWS
    section = sec[0]
    n = cycle - 2 * (last - section)

    @pl.when((n >= 0) & (n < micro))
    def _():
        m = n + 1 if late else n - 1
        own = pl.multiple_of(m * ROWS, ROWS)
        base = pl.multiple_of(own + ROWS - span, ROWS)

        @pl.when(section == last)
        def _():
            sg[m] = (cot[pl.ds(own, ROWS)].astype(F32) * loss_scale).astype(BF)

        if received:
            @pl.when(section != last)
            def _():
                sg[m] = refs[0][...]

        g = sg[m]
        do_all = (
            mm(g[:, :inner], w_out(pack, 0, inner), 1, 1)
            + mm(g[:, inner:], w_out(pack, 1, inner), 1, 1)
        ).astype(BF)
        mask = bias[m, :, :span]
        lse = sl[m]
        scale = HEAD ** (-0.5)
        cut = [slice(e * HEAD, (e + 1) * HEAD) for e in range(heads)]
        qs = [sq[pl.ds(own, ROWS), e * HEAD:(e + 1) * HEAD] for e in range(heads)]
        ks = [sq[pl.ds(base, span), inner + e * HEAD:inner + (e + 1) * HEAD] for e in range(heads)]
        vs = [sq[pl.ds(base, span), 2 * inner + e * HEAD:2 * inner + (e + 1) * HEAD] for e in range(heads)]
        dos = [do_all[:, c] for c in cut]
        ps = [jnp.exp(mm(qs[e], ks[e], 1, 1) * scale + mask - lse[:, e:e + 1]) for e in range(heads)]
        dps = [mm(dos[e], vs[e], 1, 1) for e in range(heads)]
        insides = [jnp.sum(dp * p, axis=-1, keepdims=True) for dp, p in zip(dps, ps)]
        dss = [(p * (dp - i) * scale).astype(BF) for p, dp, i in zip(ps, dps, insides)]
        for e in range(heads):
            lo, hi = e * HEAD, (e + 1) * HEAD
            sd[m, :, lo:hi] = mm(dss[e], ks[e]).astype(BF)
            dk = mm(dss[e], qs[e], 0, 0)
            dv = mm(ps[e].astype(BF), dos[e], 0, 0)
            for at, value in ((0, dk), (inner, dv)):
                if late:
                    sp[:, at + lo:at + hi] = value[:ROWS]
                    value = value[ROWS:]
                else:
                    value = value + sp[:, at + lo:at + hi]
                sd[m, :, inner + at + lo:inner + at + hi] = value.astype(BF)
        r, u = unit(sh[m].astype(F32))
        da = None
        for k in range(3):
            term = mm(sd[m, :, k * inner:(k + 1) * inner], w_in(pack, k, inner), 1, 1)
            da = term if da is None else da + term
        sn[m] = jnp.sum((da * u).reshape(ROWS // 8, 8, feat), axis=0)
        e = da * gains[...]
        mean = jnp.mean(e * u, axis=-1, keepdims=True)
        out[...] = (sg[m].astype(F32) + r * (e - u * mean)).astype(BF)


def place(order, rel):
    low, high, y = rel % 2, (rel // 2) % 2, rel // 4
    bit = {2: (low + high) % 2, 6: high, 8: y}
    return 4 * bit[order[0]] + 2 * bit[order[1]] + bit[order[2]]


def gradient_kernel(order, cut, outs, me, sa, sd, so, sg, sn, keep, send):
    micro, rows, feat = sa.shape
    tokens = micro * rows
    inner = so.shape[2]
    width, shard = 2 * keep.shape[0], keep.shape[1]
    lo, hi = cut
    mine = me[0]

    def store(d, pieces):
        low = (d + mine) % 2
        x = (d // 2) % 4
        my_x = (mine // 2) % 4
        first = (x + my_x) % 2
        second = (x // 2 + my_x // 2) % 2
        y = (d // 8 + mine // 8) % 2
        slot = place(order, first + 2 * second + 4 * y)
        for ref, want in ((keep, 0), (send, 1)):
            @pl.when(low == want)
            def _():
                for where, value in pieces:
                    ref[slot, where[0], where[1]] = value

    if outs:
        total = jnp.sum(sn[...], axis=(0, 1)).reshape(1, feat)
        gain = jnp.concatenate(
            [
                jnp.broadcast_to(total[:, c * HEAD:(c + 1) * HEAD], (HEAD, HEAD)).T
                for c in range(feat // HEAD)
            ],
            axis=0,
        ).astype(BF)
    group = 4
    for c in range(width // group):
        a = sa[:, :, c * group * shard:(c + 1) * group * shard].reshape(tokens, group * shard)
        res = mm(a, sd[:, :, lo:hi].reshape(tokens, hi - lo), 0, 0).astype(BF)
        for j in range(group):
            d = c * group + j
            pieces = [((slice(None), slice(0, hi - lo)), res[j * shard:(j + 1) * shard])]
            if outs:
                pieces.append(
                    ((slice(None), slice(hi - lo + inner, None)), gain[d * shard:(d + 1) * shard])
                )
            store(d, pieces)
    if outs:
        half = inner // width
        group = 8
        at = slice(hi - lo, hi - lo + inner)
        g = sg[...].reshape(tokens, feat)
        for c in range(width // group):
            o = so[:, :, c * group * half:(c + 1) * group * half].reshape(tokens, group * half)
            res = mm(o, g, 0, 0).astype(BF)
            for j in range(group):
                rows_of = res[j * half:(j + 1) * half]
                store(c * group + j, [
                    ((slice(0, half), at), rows_of[:, :inner]),
                    ((slice(half, 2 * half), at), rows_of[:, inner:]),
                ])


SMEM = pl.BlockSpec(memory_space=pltpu.SMEM)
VMEM = pl.BlockSpec(memory_space=pltpu.VMEM)


def call(body, ins, states, shapes, out_shape, flops, name):
    count = len(ins)
    got = pl.pallas_call(
        body,
        out_shape=list(shapes) + [out_shape],
        in_specs=[SMEM] * 2 + [VMEM] * (count - 2 + len(states)),
        out_specs=[VMEM] * (len(shapes) + 1),
        input_output_aliases={count + i: i for i in range(len(states))},
        compiler_params=pltpu.CompilerParams(vmem_limit_bytes=LIMIT),
        cost_estimate=pl.CostEstimate(flops=flops, bytes_accessed=12 * 1024 * 1024, transcendentals=0),
        name=name,
    )(*ins, *states)
    return got[-1], list(got[:-1])


def after(value, other):
    def copy_kernel(src, _, dst):
        dst[...] = src[...]

    return pl.pallas_call(
        copy_kernel,
        out_shape=jax.ShapeDtypeStruct(value.shape, value.dtype),
        in_specs=[VMEM, pl.BlockSpec(memory_space=pl.ANY)],
        out_specs=VMEM,
        compiler_params=pltpu.CompilerParams(vmem_limit_bytes=LIMIT),
        name="after",
    )(value, other)


def hops(step, last):
    runs = [(0, 1), (0, 3), (0, 3), (1, 5), (1, 5), (3, 6)] + [(4, 7)] * 3
    low, high = runs[min(step // 2, len(runs) - 1)]
    return range(low, min(high, last))


def spread_sum(value):
    for masks in ([1], [2, 4, 6], [8], [64], [16, 32, 48]):
        got = [
            lax.ppermute(value, ("section", "dp"), [(i, i ^ mask) for i in range(128)])
            for mask in masks
        ]
        for other in got:
            value = value + other
    return value


def swap(value, mask):
    return lax.ppermute(value, "dp", [(i, i ^ mask) for i in range(16)])


def scatter_sum(keep, send, order):
    total = keep.astype(F32) + swap(send, 1).astype(F32)
    for mask in order:
        half = total.shape[0] // 2
        total = total[:half] + swap(total[half:].astype(BF), mask).astype(F32)
    return total[0]


def local(hidden_in, segment_ids, cotangent, in_proj, out_proj, norm_gains):
    section = lax.axis_index("section")
    sections = lax.axis_size("section")
    width = lax.axis_size("dp")
    last = sections - 1
    seqs, length = segment_ids.shape
    feat = hidden_in.shape[1]
    shard = in_proj.shape[1]
    inner = out_proj.shape[1] * width
    micro = seqs * length // ROWS
    wo = jnp.concatenate([out_proj[0, :, :inner], out_proj[0, :, inner:]], axis=0)
    pack = lax.all_gather(jnp.concatenate([in_proj[0], wo], axis=1), "dp", axis=0)
    loss_scale = 1.0 / math.sqrt(width * hidden_in.shape[0])
    tokens = seqs * length
    ident = segment_ids.reshape(seqs, 2, ROWS)
    rows = lax.broadcasted_iota(jnp.int32, (ROWS, 2 * ROWS), 0)
    cols = lax.broadcasted_iota(jnp.int32, (ROWS, 2 * ROWS), 1)
    same = ident[:, :, :, None] == segment_ids[:, None, None, :]
    causal = jnp.stack([cols <= rows, cols <= rows + ROWS])
    bias = jnp.where(same & causal, 0.0, MASKED).astype(F32).reshape(micro, ROWS, length)
    sec = jnp.full((1,), section, jnp.int32)
    me = jnp.full((1,), lax.axis_index("dp"), jnp.int32)

    def shaped(*shape, dtype=BF):
        return jax.ShapeDtypeStruct(shape, dtype)

    f_shapes = [
        shaped(micro, ROWS, feat),
        shaped(micro, ROWS, feat),
        shaped(tokens, 3 * inner),
        shaped(micro, ROWS, inner),
        shaped(micro, ROWS, HEAD, dtype=F32),
    ]
    b_shapes = [
        shaped(micro, ROWS, feat),
        shaped(micro, ROWS, 3 * inner),
        shaped(micro, 8, feat, dtype=F32),
        shaped(ROWS, 2 * inner, dtype=F32),
    ]
    moved = shaped(ROWS, feat)
    per_row = 2 * feat * 4 * inner
    first = 2 * last + 1
    end = first + 2 * last + micro
    f_state, b_state = [], []
    f_recv, b_recv = {}, {}
    for cycle in range(end):
        on = [s for s in range(sections) if 0 <= cycle - 2 * s < micro]
        if on:
            out, f_state = call(
                functools.partial(forward_kernel, cycle, micro, last, cycle in f_recv),
                [sec, me, hidden_in, bias, norm_gains, pack]
                + ([f_recv[cycle]] if cycle in f_recv else []),
                f_state, f_shapes, moved, ROWS * per_row, "fwd_half",
            )
            pairs = [(s, s + 1) for s in hops(cycle, last)]
            if cycle == 1:
                held = out
            elif on != [last]:
                if cycle == 2:
                    f_recv[3] = lax.ppermute(after(held, out), "section", [(0, 1)])
                f_recv[cycle + 2] = lax.ppermute(out, "section", pairs)
        on = [s for s in range(sections) if 0 <= cycle - first - 2 * (last - s) < micro]
        if on:
            sh, _, sq, _, sl = f_state
            out, b_state = call(
                functools.partial(
                    backward_kernel, cycle - first, micro, last, loss_scale, cycle in b_recv
                ),
                [sec, me, cotangent, bias, norm_gains, pack, sh, sq, sl]
                + ([b_recv[cycle]] if cycle in b_recv else []),
                b_state, b_shapes, moved, 2 * ROWS * per_row, "bwd_half",
            )
            if on != [0]:
                pairs = [(last - s, last - s - 1) for s in hops(cycle - first, last)]
                b_recv[cycle + 2] = lax.ppermute(out, "section", pairs)
    _, sa, _, so, _ = f_state
    sg, sd, sn, _ = b_state
    third = 4 * inner // 3
    parts = []
    for index, order in enumerate(((2, 6, 8), (6, 8, 2), (8, 2, 6))):
        outs = index == 2
        cut = (index * third, min((index + 1) * third, 3 * inner))
        block = shaped(width // 2, shard, third + (HEAD if outs else 0))
        keep, send = pl.pallas_call(
            functools.partial(gradient_kernel, order, cut, outs),
            out_shape=[block, block],
            in_specs=[SMEM] + [VMEM] * 5,
            out_specs=[VMEM] * 2,
            compiler_params=pltpu.CompilerParams(vmem_limit_bytes=LIMIT),
            cost_estimate=pl.CostEstimate(
                flops=2 * tokens * feat * third, bytes_accessed=12 * 1024 * 1024, transcendentals=0
            ),
            name="gradient",
        )(me, sa, sd, so, sg, sn)
        parts.append((keep, send, order))
    parts = [scatter_sum(*part) for part in parts]
    rest = parts[2]
    edge = 3 * inner - 2 * third
    half = out_proj.shape[1]
    in_sum = jnp.concatenate([parts[0], parts[1], rest[:, :edge]], axis=1)
    out_sum = jnp.concatenate([rest[:half, edge:third], rest[half:, edge:third]], axis=1)
    gain_sum = rest[:, third]
    squares = sum(jnp.sum(p * p) for p in (parts[0], parts[1], rest[:, :third], gain_sum))
    grand_total = spread_sum(jnp.full((8, HEAD), squares, F32))[0, 0]
    count = float(sections * width * (in_sum.size + out_sum.size + gain_sum.size))
    return (in_sum[None], out_sum[None], gain_sum[None], jnp.sqrt(grand_total / count))


def solution(mesh):
    placed = (
        P("dp", None),
        P("dp", None),
        P("dp", None),
        P("section", "dp", None),
        P("section", "dp", None),
        P("section", None),
    )
    return jax.shard_map(
        local,
        mesh=mesh,
        in_specs=placed,
        out_specs=(P("section", "dp", None), P("section", "dp", None), P("section", "dp"), P()),
        check_vma=False,
    )
```

```python
import functools
import math

import jax
import jax.numpy as jnp
from jax import lax
from jax.experimental import pallas as pl
from jax.experimental.pallas import tpu as pltpu
from jax.sharding import PartitionSpec as P

HEAD = 128
ROWS = 128
EPS = 1e-05
MASKED = -1e30
LIMIT = 8 * 1024 * 1024
BF = jnp.bfloat16
F32 = jnp.float32


def mm(left, right, lc=1, rc=0):
    return lax.dot_general(left, right, (((lc,), (rc,)), ((), ())), preferred_element_type=F32)


def unit(h):
    r = lax.rsqrt(jnp.mean(h * h, axis=-1, keepdims=True) + EPS)
    return r, h * r


def w_in(pack, k, inner):
    return pack[:, :, k * inner:(k + 1) * inner].reshape(-1, inner)


def w_out(pack, part, inner):
    half = pack.shape[1] // 2
    return pack[:, part * half:(part + 1) * half, 3 * inner:].reshape(-1, inner)


def forward_kernel(cycle, micro, last, received, sec, me, hid, bias, gains, pack, *refs):
    (sh, sa, sq, so, sl, out) = refs[-6:]
    inner = so.shape[2]
    heads = inner // HEAD
    odd = cycle % 2
    span = (1 + odd) * ROWS
    section = sec[0]
    m = cycle - 2 * section

    @pl.when((m >= 0) & (m < micro))
    def _():
        own = pl.multiple_of(m * ROWS, ROWS)
        base = pl.multiple_of(own - odd * ROWS, ROWS)

        @pl.when(section == 0)
        def _():
            sh[m] = hid[pl.ds(own, ROWS)]

        if received:
            @pl.when(section != 0)
            def _():
                sh[m] = refs[0][...]

        _, u = unit(sh[m].astype(F32))
        a = (u * gains[...]).astype(BF)
        sa[m] = a
        for k in range(3):
            sq[pl.ds(own, ROWS), k * inner:(k + 1) * inner] = mm(a, w_in(pack, k, inner)).astype(BF)
        mask = bias[m, :, :span]
        scores = []
        for e in range(heads):
            lo, hi = e * HEAD, (e + 1) * HEAD
            q = sq[pl.ds(own, ROWS), lo:hi]
            k = sq[pl.ds(base, span), inner + lo:inner + hi]
            scores.append(mm(q, k, 1, 1) * HEAD ** (-0.5) + mask)
        tops = [jnp.max(s, axis=-1, keepdims=True) for s in scores]
        xs = [jnp.exp(s - top) for s, top in zip(scores, tops)]
        totals = [jnp.sum(x, axis=-1, keepdims=True) for x in xs]
        lane = lax.broadcasted_iota(jnp.int32, (ROWS, HEAD), 1)
        lse = jnp.zeros((ROWS, HEAD), F32)
        for e in range(heads):
            lo, hi = e * HEAD, (e + 1) * HEAD
            v = sq[pl.ds(base, span), 2 * inner + lo:2 * inner + hi]
            so[m, :, lo:hi] = (mm(xs[e].astype(BF), v) * (1.0 / totals[e])).astype(BF)
            lse = jnp.where(lane == e, tops[e] + jnp.log(totals[e]), lse)
        sl[m] = lse

        @pl.when(section != last)
        def _():
            o = so[m]
            for part in range(2):
                cols = slice(part * inner, (part + 1) * inner)
                out[:, cols] = (
                    sh[m, :, cols].astype(F32) + mm(o, w_out(pack, part, inner))
                ).astype(BF)


def backward_kernel(cycle, micro, last, loss_scale, received, sec, me, cot, bias, gains, pack, sh, sq, sl, *refs):
    (sg, sd, sn, sp, out) = refs[-5:]
    inner = sd.shape[2] // 3
    feat = sh.shape[2]
    heads = inner // HEAD
    late = cycle % 2 == 0
    span = 2 * ROWS if late else ROWS
    section = sec[0]
    n = cycle - 2 * (last - section)

    @pl.when((n >= 0) & (n < micro))
    def _():
        m = n + 1 if late else n - 1
        own = pl.multiple_of(m * ROWS, ROWS)
        base = pl.multiple_of(own + ROWS - span, ROWS)

        @pl.when(section == last)
        def _():
            sg[m] = (cot[pl.ds(own, ROWS)].astype(F32) * loss_scale).astype(BF)

        if received:
            @pl.when(section != last)
            def _():
                sg[m] = refs[0][...]

        g = sg[m]
        do_all = (
            mm(g[:, :inner], w_out(pack, 0, inner), 1, 1)
            + mm(g[:, inner:], w_out(pack, 1, inner), 1, 1)
        ).astype(BF)
        mask = bias[m, :, :span]
        lse = sl[m]
        scale = HEAD ** (-0.5)
        cut = [slice(e * HEAD, (e + 1) * HEAD) for e in range(heads)]
        qs = [sq[pl.ds(own, ROWS), e * HEAD:(e + 1) * HEAD] for e in range(heads)]
        ks = [sq[pl.ds(base, span), inner + e * HEAD:inner + (e + 1) * HEAD] for e in range(heads)]
        vs = [sq[pl.ds(base, span), 2 * inner + e * HEAD:2 * inner + (e + 1) * HEAD] for e in range(heads)]
        dos = [do_all[:, c] for c in cut]
        ps = [jnp.exp(mm(qs[e], ks[e], 1, 1) * scale + mask - lse[:, e:e + 1]) for e in range(heads)]
        dps = [mm(dos[e], vs[e], 1, 1) for e in range(heads)]
        insides = [jnp.sum(dp * p, axis=-1, keepdims=True) for dp, p in zip(dps, ps)]
        dss = [(p * (dp - i) * scale).astype(BF) for p, dp, i in zip(ps, dps, insides)]
        for e in range(heads):
            lo, hi = e * HEAD, (e + 1) * HEAD
            sd[m, :, lo:hi] = mm(dss[e], ks[e]).astype(BF)
            dk = mm(dss[e], qs[e], 0, 0)
            dv = mm(ps[e].astype(BF), dos[e], 0, 0)
            for at, value in ((0, dk), (inner, dv)):
                if late:
                    sp[:, at + lo:at + hi] = value[:ROWS]
                    value = value[ROWS:]
                else:
                    value = value + sp[:, at + lo:at + hi]
                sd[m, :, inner + at + lo:inner + at + hi] = value.astype(BF)
        r, u = unit(sh[m].astype(F32))
        da = None
        for k in range(3):
            term = mm(sd[m, :, k * inner:(k + 1) * inner], w_in(pack, k, inner), 1, 1)
            da = term if da is None else da + term
        sn[m] = jnp.sum((da * u).reshape(ROWS // 8, 8, feat), axis=0)
        e = da * gains[...]
        mean = jnp.mean(e * u, axis=-1, keepdims=True)
        out[...] = (sg[m].astype(F32) + r * (e - u * mean)).astype(BF)


def place(order, rel):
    low, high, y = rel % 2, (rel // 2) % 2, rel // 4
    bit = {2: (low + high) % 2, 6: high, 8: y}
    return 4 * bit[order[0]] + 2 * bit[order[1]] + bit[order[2]]


def gradient_kernel(order, cut, outs, me, sa, sd, so, sg, sn, keep, send):
    micro, rows, feat = sa.shape
    tokens = micro * rows
    inner = so.shape[2]
    width, shard = 2 * keep.shape[0], keep.shape[1]
    lo, hi = cut
    mine = me[0]

    def store(d, pieces):
        low = (d + mine) % 2
        x = (d // 2) % 4
        my_x = (mine // 2) % 4
        first = (x + my_x) % 2
        second = (x // 2 + my_x // 2) % 2
        y = (d // 8 + mine // 8) % 2
        slot = place(order, first + 2 * second + 4 * y)
        for ref, want in ((keep, 0), (send, 1)):
            @pl.when(low == want)
            def _():
                for where, value in pieces:
                    ref[slot, where[0], where[1]] = value

    if outs:
        total = jnp.sum(sn[...], axis=(0, 1)).reshape(1, feat)
        gain = jnp.concatenate(
            [
                jnp.broadcast_to(total[:, c * HEAD:(c + 1) * HEAD], (HEAD, HEAD)).T
                for c in range(feat // HEAD)
            ],
            axis=0,
        ).astype(BF)
    group = 4
    for c in range(width // group):
        a = sa[:, :, c * group * shard:(c + 1) * group * shard].reshape(tokens, group * shard)
        res = mm(a, sd[:, :, lo:hi].reshape(tokens, hi - lo), 0, 0).astype(BF)
        for j in range(group):
            d = c * group + j
            pieces = [((slice(None), slice(0, hi - lo)), res[j * shard:(j + 1) * shard])]
            if outs:
                pieces.append(
                    ((slice(None), slice(hi - lo + inner, None)), gain[d * shard:(d + 1) * shard])
                )
            store(d, pieces)
    if outs:
        half = inner // width
        group = 8
        at = slice(hi - lo, hi - lo + inner)
        g = sg[...].reshape(tokens, feat)
        for c in range(width // group):
            o = so[:, :, c * group * half:(c + 1) * group * half].reshape(tokens, group * half)
            res = mm(o, g, 0, 0).astype(BF)
            for j in range(group):
                rows_of = res[j * half:(j + 1) * half]
                store(c * group + j, [
                    ((slice(0, half), at), rows_of[:, :inner]),
                    ((slice(half, 2 * half), at), rows_of[:, inner:]),
                ])


SMEM = pl.BlockSpec(memory_space=pltpu.SMEM)
VMEM = pl.BlockSpec(memory_space=pltpu.VMEM)


def call(body, ins, states, shapes, out_shape, flops, name):
    count = len(ins)
    got = pl.pallas_call(
        body,
        out_shape=list(shapes) + [out_shape],
        in_specs=[SMEM] * 2 + [VMEM] * (count - 2 + len(states)),
        out_specs=[VMEM] * (len(shapes) + 1),
        input_output_aliases={count + i: i for i in range(len(states))},
        compiler_params=pltpu.CompilerParams(vmem_limit_bytes=LIMIT),
        cost_estimate=pl.CostEstimate(flops=flops, bytes_accessed=12 * 1024 * 1024, transcendentals=0),
        name=name,
    )(*ins, *states)
    return got[-1], list(got[:-1])


def hops(step, last):
    runs = [(0, 1), (0, 3), (0, 3), (1, 5), (1, 5), (3, 6)] + [(4, 7)] * 3
    low, high = runs[min(step // 2, len(runs) - 1)]
    return range(low, min(high, last))


def spread_sum(value):
    for masks in ([1], [2, 4, 6], [8], [64], [16, 32, 48]):
        got = [
            lax.ppermute(value, ("section", "dp"), [(i, i ^ mask) for i in range(128)])
            for mask in masks
        ]
        for other in got:
            value = value + other
    return value


def swap(value, mask):
    return lax.ppermute(value, "dp", [(i, i ^ mask) for i in range(16)])


def scatter_sum(keep, send, order):
    total = keep.astype(F32) + swap(send, 1).astype(F32)
    for mask in order:
        half = total.shape[0] // 2
        total = total[:half] + swap(total[half:].astype(BF), mask).astype(F32)
    return total[0]


def local(hidden_in, segment_ids, cotangent, in_proj, out_proj, norm_gains):
    section = lax.axis_index("section")
    sections = lax.axis_size("section")
    width = lax.axis_size("dp")
    last = sections - 1
    seqs, length = segment_ids.shape
    feat = hidden_in.shape[1]
    shard = in_proj.shape[1]
    inner = out_proj.shape[1] * width
    micro = seqs * length // ROWS
    wo = jnp.concatenate([out_proj[0, :, :inner], out_proj[0, :, inner:]], axis=0)
    pack = lax.all_gather(jnp.concatenate([in_proj[0], wo], axis=1), "dp", axis=0)
    loss_scale = 1.0 / math.sqrt(width * hidden_in.shape[0])
    tokens = seqs * length
    ident = segment_ids.reshape(seqs, 2, ROWS)
    rows = lax.broadcasted_iota(jnp.int32, (ROWS, 2 * ROWS), 0)
    cols = lax.broadcasted_iota(jnp.int32, (ROWS, 2 * ROWS), 1)
    same = ident[:, :, :, None] == segment_ids[:, None, None, :]
    causal = jnp.stack([cols <= rows, cols <= rows + ROWS])
    bias = jnp.where(same & causal, 0.0, MASKED).astype(F32).reshape(micro, ROWS, length)
    sec = jnp.full((1,), section, jnp.int32)
    me = jnp.full((1,), lax.axis_index("dp"), jnp.int32)

    def shaped(*shape, dtype=BF):
        return jax.ShapeDtypeStruct(shape, dtype)

    f_shapes = [
        shaped(micro, ROWS, feat),
        shaped(micro, ROWS, feat),
        shaped(tokens, 3 * inner),
        shaped(micro, ROWS, inner),
        shaped(micro, ROWS, HEAD, dtype=F32),
    ]
    b_shapes = [
        shaped(micro, ROWS, feat),
        shaped(micro, ROWS, 3 * inner),
        shaped(micro, 8, feat, dtype=F32),
        shaped(ROWS, 2 * inner, dtype=F32),
    ]
    moved = shaped(ROWS, feat)
    per_row = 2 * feat * 4 * inner
    first = 2 * last + 1
    end = first + 2 * last + micro
    f_state, b_state = [], []
    f_recv, b_recv = {}, {}
    for cycle in range(end):
        on = [s for s in range(sections) if 0 <= cycle - 2 * s < micro]
        if on or cycle == 2 * last + micro:
            out, f_state = call(
                functools.partial(forward_kernel, cycle, micro, last, cycle in f_recv),
                [sec, me, hidden_in, bias, norm_gains, pack]
                + ([f_recv[cycle]] if cycle in f_recv else []),
                f_state, f_shapes, moved, ROWS * per_row, "fwd_half",
            )
            if on and on != [last]:
                pairs = [(s, s + 1) for s in hops(cycle, last)]
                f_recv[cycle + 2] = lax.ppermute(out, "section", pairs)
        on = [s for s in range(sections) if 0 <= cycle - first - 2 * (last - s) < micro]
        if on:
            sh, _, sq, _, sl = f_state
            out, b_state = call(
                functools.partial(
                    backward_kernel, cycle - first, micro, last, loss_scale, cycle in b_recv
                ),
                [sec, me, cotangent, bias, norm_gains, pack, sh, sq, sl]
                + ([b_recv[cycle]] if cycle in b_recv else []),
                b_state, b_shapes, moved, 2 * ROWS * per_row, "bwd_half",
            )
            if on != [0]:
                pairs = [(last - s, last - s - 1) for s in hops(cycle - first, last)]
                b_recv[cycle + 2] = lax.ppermute(out, "section", pairs)
    _, sa, _, so, _ = f_state
    sg, sd, sn, _ = b_state
    third = 4 * inner // 3
    parts = []
    for index, order in enumerate(((2, 6, 8), (6, 8, 2), (8, 2, 6))):
        outs = index == 2
        cut = (index * third, min((index + 1) * third, 3 * inner))
        block = shaped(width // 2, shard, third + (HEAD if outs else 0))
        keep, send = pl.pallas_call(
            functools.partial(gradient_kernel, order, cut, outs),
            out_shape=[block, block],
            in_specs=[SMEM] + [VMEM] * 5,
            out_specs=[VMEM] * 2,
            compiler_params=pltpu.CompilerParams(vmem_limit_bytes=LIMIT),
            cost_estimate=pl.CostEstimate(
                flops=2 * tokens * feat * third, bytes_accessed=12 * 1024 * 1024, transcendentals=0
            ),
            name="gradient",
        )(me, sa, sd, so, sg, sn)
        parts.append((keep, send, order))
    parts = [scatter_sum(*part) for part in parts]
    rest = parts[2]
    edge = 3 * inner - 2 * third
    half = out_proj.shape[1]
    in_sum = jnp.concatenate([parts[0], parts[1], rest[:, :edge]], axis=1)
    out_sum = jnp.concatenate([rest[:half, edge:third], rest[half:, edge:third]], axis=1)
    gain_sum = rest[:, third]
    squares = sum(jnp.sum(p * p) for p in (parts[0], parts[1], rest[:, :third], gain_sum))
    grand_total = spread_sum(jnp.full((8, HEAD), squares, F32))[0, 0]
    count = float(sections * width * (in_sum.size + out_sum.size + gain_sum.size))
    return (in_sum[None], out_sum[None], gain_sum[None], jnp.sqrt(grand_total / count))


def solution(mesh):
    placed = (
        P("dp", None),
        P("dp", None),
        P("dp", None),
        P("section", "dp", None),
        P("section", "dp", None),
        P("section", None),
    )
    return jax.shard_map(
        local,
        mesh=mesh,
        in_specs=placed,
        out_specs=(P("section", "dp", None), P("section", "dp", None), P("section", "dp"), P()),
        check_vma=False,
    )
```
